32 devices in a mesh: groups: 2 (over x), samples: 16 (over z, y, core).
Axes of the slice: x: 2, y: 2, z: 4, core: 2. Of those that a mesh axis runs over, the one named last changes fastest.
Arguments:
- acts: bfloat16 [12288, 1024], P(('groups', 'samples')), parts along dimension 0
- grads: bfloat16 [12288, 2048], P(('groups', 'samples')), parts along dimension 0
- counts: int32 [32], P(('groups', 'samples')), parts along dimension 0, may hold values from 1 to 384, 4608 in all
- basis_a: bfloat16 [1024, 1024], P('samples')
- basis_g: bfloat16 [2048, 2048], P('samples')
Outputs:
- precond: bfloat16 [2048, 2048], P(('groups', 'samples')), parts along dimension 0
The draws below stay inside these ranges and needn't reach their ends.
There are 2 independent parts, one for each index of `groups`. The reference program is written for one: setup_inputs(seed, part) draws one part's arguments, and reference() takes and returns one part's arrays. A program takes and returns all parts, laid end to end along the dimension named above; an argument that names none is the same for every part. Nothing has to cross between parts.
Inputs may be any that keep to these rules, and one draw needn't show every extreme that they name: `counts`: one device of every draw holds 384 valid rows.
All inputs are finite; a program needn't handle non-finite values.
Results may differ from the reference program's by a relative error of at most 0.0061.
Values may be sent and summed in bfloat16 or wider, within the bound.
No kernel may reach another device: no remote copies, remote signals or barrier semaphores. Data moves between devices by JAX's collectives and lax.ppermute only.
A program may use at most 64 MiB of HBM per device.

```python
import math
import jax
import jax.numpy as jnp
import numpy as np
from jax import lax

D = 1024
F = 2048
ROWS_DEV = 384
SHARDS = 16
SAMPLES = 6144


def common_rows(key, spread):
    latent = jax.random.normal(key, (SAMPLES, D), jnp.float32)
    jitter = jax.random.uniform(jax.random.fold_in(key, 1), (SAMPLES, 1), jnp.float32)
    rising = jnp.exp(math.log(3.0) * jnp.arange(SAMPLES, dtype=jnp.float32) / SAMPLES)[:, None]
    return (latent, jnp.exp(spread * jitter) * rising)


def draw_acts(key, part):
    latent, scales = common_rows(key, math.log(3.0))
    key = jax.random.fold_in(key, 3)
    column = jnp.exp(jax.random.uniform(key, (1, D), jnp.float32, math.log(0.5), math.log(5.0)))
    return (latent * scales * column).astype(jnp.bfloat16)


def draw_grads(key, part):
    latent, scales = common_rows(key, math.log(3.0))
    key = jax.random.fold_in(key, 5)
    noise = jax.random.normal(key, (SAMPLES, F), jnp.float32)
    column = jnp.exp(jax.random.uniform(jax.random.fold_in(key, 1), (1, F), jnp.float32, math.log(0.5), math.log(5.0)))
    shared = jnp.tile(latent, (1, F // D))
    return (scales * column * (0.5 * shared + 0.85 * noise)).astype(jnp.bfloat16)


def near_identity(key, width):
    spread = jax.random.normal(key, (width, width), jnp.float32)
    return (jnp.eye(width, dtype=jnp.float32) + 0.5 / math.sqrt(width) * spread).astype(jnp.bfloat16)


def draw_basis_a(key, part):
    key = jax.random.fold_in(key, 7)
    return near_identity(key, D)


def draw_basis_g(key, part):
    key = jax.random.fold_in(key, 9)
    return near_identity(key, F)


def split_up(amount, total, most, skew):
    loads = [(1 << 20) // math.isqrt(standing ** skew) + 1 for standing in range(2, amount + 1)]
    rest, given = total - most - (amount - 1), [1] * (amount - 1)
    while rest > 0:
        movable = [i for i in range(amount - 1) if given[i] < most]
        whole, budget = sum([loads[i] for i in movable]), rest
        for i in movable:
            addition = min(most - given[i], max(1, budget * loads[i] // whole), rest)
            given[i] = given[i] + addition
            rest = rest - addition
    return np.array([most] + given)


def uneven(rng, amount, total, most, lean):
    if amount == 2:
        one = jax.random.randint(rng, (), max(1, total - most), min(most, total - 1) + 1)
        return jnp.stack([one, total - one])
    sizes = jnp.asarray(split_up(amount, total, most, lean), jnp.int32)
    pairs = (amount - 1) // 2
    donor, receiver = sizes[1:1 + 2 * pairs:2], sizes[2:2 + 2 * pairs:2]
    margin = jnp.minimum(donor - 1, most - receiver)
    moved = jax.random.randint(jax.random.fold_in(rng, 1), (pairs,), 0, 1 << 20) % (margin + 1)
    sizes = sizes.at[1:1 + 2 * pairs:2].set(donor - moved).at[2:2 + 2 * pairs:2].set(receiver + moved)
    return sizes[jax.random.permutation(jax.random.fold_in(rng, 2), amount)]


def setup_inputs(seed: int = 0, part: int = 0) -> dict:
    keys = jax.random.split(jax.random.key(seed), 6)
    part_keys = jax.random.split(jax.random.fold_in(keys[5], part), 6)
    return {
        "acts": draw_acts(jax.random.fold_in(jax.random.fold_in(keys[5], part), 71), part),
        "grads": draw_grads(jax.random.fold_in(jax.random.fold_in(keys[5], part), 71), part),
        "counts": uneven(part_keys[2], SHARDS, SHARDS * ROWS_DEV * 3 // 4, ROWS_DEV, 1).astype(jnp.int32),
        "basis_a": draw_basis_a(jax.random.fold_in(keys[5], 71), part),
        "basis_g": draw_basis_g(jax.random.fold_in(keys[5], 71), part),
    }


damping = 0.01


def reference(acts, grads, counts, basis_a, basis_g):
    position = jnp.arange(SAMPLES, dtype=jnp.int32)
    limit = jnp.repeat(counts, ROWS_DEV)
    mask = (position % ROWS_DEV < limit).astype(jnp.bfloat16)[:, None]
    total = jnp.sum(counts).astype(jnp.float32)
    rot_a = jnp.dot(acts, basis_a, preferred_element_type=jnp.float32).astype(jnp.bfloat16) * mask
    rot_g = jnp.dot(grads, basis_g, preferred_element_type=jnp.float32).astype(jnp.bfloat16) * mask
    lam_a = jnp.sum(jnp.square(rot_a.astype(jnp.float32)), axis=0) / total
    lam_g = jnp.sum(jnp.square(rot_g.astype(jnp.float32)), axis=0) / total
    rotated = lax.dot_general(rot_a, rot_g, (((0,), (0,)), ((), ())), preferred_element_type=jnp.float32) / total
    scaled = (rotated / (lam_a[:, None] * lam_g[None, :] + damping)).astype(jnp.bfloat16)
    mid = jnp.dot(basis_a, scaled, preferred_element_type=jnp.float32).astype(jnp.bfloat16)
    return lax.dot_general(mid, basis_g, (((1,), (1,)), ((), ())), preferred_element_type=jnp.float32).astype(jnp.bfloat16)
```

```python
import jax
import jax.numpy as jnp
from jax import lax
from jax.sharding import Mesh, PartitionSpec as P

damping = 0.01
bf16 = jnp.bfloat16
f32 = jnp.float32
SWAP = [(0, 1), (1, 0)]


def cut(x, first, size, axis=0):
    return lax.dynamic_slice_in_dim(x, first, size, axis)


def ordered(second, mine, other):
    return jnp.where(second == 0, jnp.concatenate([mine, other]), jnp.concatenate([other, mine]))


def two_parts(v):
    high = lax.reduce_precision(v, 8, 7)
    return high.astype(bf16), (v - high).astype(bf16)


def across(x, step, levels):
    return lax.ppermute(x, "level", [(i, i ^ step) for i in range(levels)])


def body(acts, grads, counts, basis_a, basis_g):
    group, level, chip, core = (lax.axis_index(n) for n in ("group", "level", "chip", "core"))
    levels = lax.axis_size("level")
    rows, width_a = acts.shape
    width_g = grads.shape[1]
    rows_a, rows_g = basis_a.shape[0], basis_g.shape[0]
    part_a, part_g = width_a // 4, width_g // 8

    def columns(c, chips):
        pieces = [cut(basis_g, ((y * 2 + c) * 2 + group) * part_g, part_g, 1) for y in chips]
        return jnp.concatenate(pieces + [cut(basis_a, (c * 2 + group) * part_a, part_a, 1)])

    mine = columns(core, (chip, 1 - chip))
    theirs = lax.ppermute(columns(1 - core, (chip, 1 - chip)), "core", SWAP)
    here_g = ordered(core, mine[:rows_g], theirs[:rows_g])
    there_g = ordered(core, mine[rows_g : 2 * rows_g], theirs[rows_g : 2 * rows_g])
    here_a = ordered(core, mine[2 * rows_g :], theirs[2 * rows_g :])
    passed = lax.ppermute(jnp.concatenate([there_g, here_a]), "chip", SWAP)
    level_g = 4 * rows_g
    level_a = 4 * rows_a
    unit = jnp.concatenate(
        [
            ordered(chip, here_g, passed[: 2 * rows_g]),
            ordered(chip, here_a, passed[2 * rows_g :]),
        ]
    )
    full_g = jnp.zeros((width_g, 2 * part_g), bf16)
    full_a = jnp.zeros((width_a, 2 * part_a), bf16)
    own_a = []
    for step in range(levels):
        slot = unit if step == 0 else across(unit, step, levels)
        other = lax.ppermute(slot, "group", SWAP)
        at = level ^ step
        for place, block in enumerate((slot, other)):
            full_g = lax.dynamic_update_slice(full_g, block[:level_g], (at * level_g, place * part_g))
            full_a = lax.dynamic_update_slice(full_a, block[level_g:], (at * level_a, place * part_a))
        if step == 0:
            own_a = [slot[level_g:], other[level_g:]]
    level_rows = jnp.concatenate(own_a, axis=1)
    level_rows = jnp.concatenate([level_rows, lax.ppermute(level_rows, "core", SWAP)], axis=1)

    valid = counts[0]
    keep = jnp.arange(rows, dtype=jnp.int32)[:, None] < valid
    marks = jnp.stack([valid // 16 * 16, valid % 16]).astype(bf16)
    marks = jnp.broadcast_to(jnp.pad(marks, (0, 14))[:, None], (16, width_a))
    acts = jnp.concatenate([jnp.where(keep, acts, 0), marks])
    grads = jnp.where(keep, grads, 0)
    half = rows // 2
    pieces_a = [acts, lax.ppermute(acts, "core", SWAP)]
    pieces_g = [grads, lax.ppermute(grads, "core", SWAP)]
    for piece, found in ((acts, pieces_a), (grads[:half], pieces_g), (grads[half:], pieces_g)):
        got = lax.ppermute(piece, "chip", SWAP)
        found += [got, lax.ppermute(got, "core", SWAP)]
    valid_here = sum(p[rows, 0].astype(f32) + p[rows + 1, 0].astype(f32) for p in pieces_a)

    def rotate(piece, basis):
        return jnp.dot(piece, basis, preferred_element_type=f32).astype(bf16)

    turned = [rotate(p[:rows], full_a) for p in pieces_a]
    turned_core = lax.ppermute(jnp.concatenate([turned[1], turned[0], turned[3], turned[2]]), "core", SWAP)
    rot_a = jnp.concatenate([jnp.concatenate(turned), turned_core], axis=1)
    r = [rotate(p, full_g) for p in pieces_g]
    rot_g = jnp.concatenate([r[0], r[1], r[2], r[4], r[3], r[5]])
    square_a = jnp.sum(jnp.square(rot_a.astype(f32)), axis=0)
    square_g = jnp.sum(jnp.square(rot_g.astype(f32)), axis=0)
    rotated = lax.dot_general(rot_a, rot_g, (((0,), (0,)), ((), ())), preferred_element_type=f32)

    chunk = width_a // levels
    cols = rot_g.shape[1]
    high_g, low_g = two_parts(square_g)
    high_a, low_a = two_parts(square_a)
    high_n, low_n = two_parts(valid_here)

    def message(to):
        def line(v):
            return jnp.pad(cut(v, to * chunk, chunk), (0, cols - chunk))

        extra = jnp.stack(
            [high_g, low_g, line(high_a), line(low_a), jnp.broadcast_to(high_n, cols), jnp.broadcast_to(low_n, cols)]
        )
        return jnp.concatenate([cut(rotated, to * chunk, chunk).astype(bf16), jnp.pad(extra, ((0, 10), (0, 0)))])

    got = [across(message(level ^ step), step, levels).astype(f32) for step in range(1, levels)]
    summed = cut(rotated, level * chunk, chunk)
    own_square_a = cut(square_a, level * chunk, chunk)
    total = valid_here
    for g in got:
        summed = summed + g[:chunk]
        square_g = square_g + (g[chunk] + g[chunk + 1])
        own_square_a = own_square_a + (g[chunk + 2, :chunk] + g[chunk + 3, :chunk])
        total = total + (g[chunk + 4, 0] + g[chunk + 5, 0])
    lam_a = own_square_a / total
    lam_g = square_g / total
    scaled = (summed / total / (lam_a[:, None] * lam_g[None, :] + damping)).astype(bf16)

    scaled_all = jnp.zeros((width_a, cols), bf16)
    for step in range(levels):
        slot = scaled if step == 0 else across(scaled, step, levels)
        scaled_all = lax.dynamic_update_slice(scaled_all, slot, ((level ^ step) * chunk, 0))

    def result(c):
        picked = jnp.concatenate(
            [cut(level_rows, ((1 - chip) * 2 + c) * rows_a, rows_a), cut(level_rows, (chip * 2 + c) * rows_a, rows_a)]
        )
        mid = jnp.dot(picked, scaled_all, preferred_element_type=f32).astype(bf16)
        return lax.dot_general(mid, full_g, (((1,), (1,)), ((), ())), preferred_element_type=f32)

    sent = lax.ppermute(result(1 - core).astype(bf16), "core", SWAP)
    both = result(core) + sent.astype(f32)
    last = lax.ppermute(both[:rows_a].astype(bf16), "chip", SWAP)
    return (both[rows_a:] + last.astype(f32)).astype(bf16)


def solution(mesh):
    groups, samples = mesh.shape["groups"], mesh.shape["samples"]
    grid = Mesh(mesh.devices.reshape(groups, samples // 4, 2, 2), ("group", "level", "chip", "core"))
    every = ("group", "level", "chip", "core")
    in_specs = (
        P(every, None),
        P(every, None),
        P(every),
        P(every[1:], None),
        P(every[1:], None),
    )
    return jax.shard_map(body, mesh=grid, in_specs=in_specs, out_specs=P(every, None), check_vma=False)
```

```python
import functools

import jax
import jax.numpy as jnp
from jax import lax
from jax.experimental import pallas as pl
from jax.experimental.pallas import tpu as pltpu
from jax.sharding import Mesh, PartitionSpec as P

damping = 0.01
bf16 = jnp.bfloat16
f32 = jnp.float32
SWAP = [(0, 1), (1, 0)]
ANY = pl.BlockSpec(memory_space=pl.ANY)
VMEM = pl.BlockSpec(memory_space=pltpu.VMEM)
SMEM = pl.BlockSpec(memory_space=pltpu.SMEM)
LIMIT = 40 * 2**20


def params():
    return pltpu.CompilerParams(vmem_limit_bytes=LIMIT)


def cost(flops, moved):
    return pl.CostEstimate(flops=flops, bytes_accessed=moved, transcendentals=0)


def shape(dims, dtype):
    return jax.ShapeDtypeStruct(dims, dtype)


def cut(x, first, size, axis=0):
    return lax.dynamic_slice_in_dim(x, first, size, axis)


def across(x, step, levels):
    return lax.ppermute(x, "level", [(i, i ^ step) for i in range(levels)])


def spread(slots, level, levels, source, height, target, sems):
    copies = []
    for i, slot in enumerate(slots):
        step, place = i // 2, i % 2
        width = slot.shape[1]
        row = pl.multiple_of((level ^ step) * height, height)
        copy = pltpu.make_async_copy(
            slot.at[pl.ds(source, height)],
            target.at[pl.ds(row, height), pl.ds(place * width, width)],
            sems.at[i],
        )
        copy.start()
        copies.append(copy)
    return copies


def turn_acts_kernel(levels, level_g, level_a, rows, where, *refs):
    slots, pieces = refs[: 2 * levels], refs[2 * levels : 2 * levels + 4]
    out, basis, held, sems, piece_sems = refs[2 * levels + 4 :]
    copies = spread(slots, where[0], levels, level_g, level_a, basis, sems)
    moves = []
    for i, piece in enumerate(pieces):
        move = pltpu.make_async_copy(piece.at[pl.ds(0, rows)], held.at[i], piece_sems.at[i])
        move.start()
        moves.append(move)
    for copy in copies:
        copy.wait()
    for i, move in enumerate(moves):
        move.wait()
        out[pl.ds(i * rows, rows)] = jnp.dot(held[i], basis[...], preferred_element_type=f32).astype(bf16)


def turn_acts(where, slots, pieces, rows, level_g, level_a):
    levels = len(slots) // 2
    width = levels * level_a
    cols = 2 * slots[0].shape[1]
    return pl.pallas_call(
        functools.partial(turn_acts_kernel, levels, level_g, level_a, rows),
        out_shape=shape((4 * rows, cols), bf16),
        in_specs=[SMEM] + [ANY] * (2 * levels + 4),
        out_specs=VMEM,
        scratch_shapes=[
            pltpu.VMEM((width, cols), bf16),
            pltpu.VMEM((4, rows, width), bf16),
            pltpu.SemaphoreType.DMA((2 * levels,)),
            pltpu.SemaphoreType.DMA((4,)),
        ],
        compiler_params=params(),
        cost_estimate=cost(8 * rows * width * cols, 8 * rows * width + 2 * width * cols),
    )(where, *slots, *pieces)


def turn_grads_kernel(levels, level_g, where, *refs):
    slots, pieces = refs[: 2 * levels], refs[2 * levels : 2 * levels + 8]
    out, basis, held, sems, piece_sems = refs[2 * levels + 8 :]
    half = pieces[0].shape[0]
    copies = spread(slots, where[0], levels, 0, level_g, basis, sems)
    moves = []
    for i, piece in enumerate(pieces):
        move = pltpu.make_async_copy(piece, held.at[pl.ds(i * half, half)], piece_sems.at[i])
        move.start()
        moves.append(move)
    for copy in copies:
        copy.wait()
    for i in range(0, 8, 2):
        moves[i].wait()
        moves[i + 1].wait()
        block = pl.ds(i * half, 2 * half)
        out[block] = jnp.dot(held[block], basis[...], preferred_element_type=f32).astype(bf16)


def turn_grads(where, slots, pieces, level_g):
    levels = len(slots) // 2
    half, width = pieces[0].shape
    cols = 2 * slots[0].shape[1]
    return pl.pallas_call(
        functools.partial(turn_grads_kernel, levels, level_g),
        out_shape=(shape((8 * half, cols), bf16), shape((width, cols), bf16)),
        in_specs=[SMEM] + [ANY] * (2 * levels + 8),
        out_specs=(VMEM, VMEM),
        scratch_shapes=[
            pltpu.VMEM((8 * half, width), bf16),
            pltpu.SemaphoreType.DMA((2 * levels,)),
            pltpu.SemaphoreType.DMA((8,)),
        ],
        compiler_params=params(),
        cost_estimate=cost(16 * half * width * cols, 16 * half * width + 4 * width * cols),
    )(where, *slots, *pieces)


def high_low(v):
    high = v.astype(bf16)
    return high, (v - high.astype(f32)).astype(bf16)


def cross_kernel(levels, rows, where, valid, mine, theirs, right, *refs):
    own, own_extra, messages = refs[0], refs[1], refs[2 : 1 + levels]
    whole, extra, swapped = refs[1 + levels :]
    level = where[0]
    width = whole.shape[0]
    chunk = width // levels
    cols = right.shape[1]
    for i, j in enumerate((1, 0, 3, 2)):
        swapped[pl.ds(i * rows, rows)] = theirs[pl.ds(j * rows, rows)]
    extra[...] = jnp.zeros_like(extra)
    turned = right[...]
    extra[0:1] = jnp.sum(jnp.square(turned.astype(f32)), axis=0, keepdims=True)
    for i, source in enumerate((mine, swapped)):
        extra[1 + i : 2 + i] = jnp.sum(jnp.square(source[...].astype(f32)), axis=0, keepdims=True)
        for j in range(2):
            part = cols // 2
            whole[pl.ds(i * cols + j * part, part)] = lax.dot_general(
                source[:, j * part : (j + 1) * part], turned, (((0,), (0,)), ((), ())), preferred_element_type=f32
            )
    extra[3:4] = jnp.full((1, cols), valid[0], f32)
    high, low = high_low(extra[...])
    own_extra[...] = extra[...]
    own[...] = whole[pl.ds(pl.multiple_of(level * chunk, chunk), chunk)]
    for step in range(1, levels):
        to = pl.multiple_of((level ^ step) * chunk, chunk)
        message = messages[step - 1]
        message[pl.ds(0, chunk)] = whole[pl.ds(to, chunk)].astype(bf16)
        message[pl.ds(chunk, 16)] = jnp.concatenate([high, low])


def cross(where, valid, mine, theirs, right, levels):
    samples, cols = right.shape
    width = 2 * mine.shape[1]
    chunk = width // levels
    return pl.pallas_call(
        functools.partial(cross_kernel, levels, samples // 4),
        out_shape=[shape((chunk, cols), f32), shape((8, cols), f32)] + [shape((chunk + 16, cols), bf16)] * (levels - 1),
        in_specs=[SMEM, SMEM, VMEM, VMEM, VMEM],
        out_specs=[VMEM] * (1 + levels),
        scratch_shapes=[
            pltpu.VMEM((width, cols), f32),
            pltpu.VMEM((8, cols), f32),
            pltpu.VMEM((samples, cols), bf16),
        ],
        compiler_params=params(),
        cost_estimate=cost(2 * samples * width * cols, 6 * samples * cols + 2 * width * cols),
    )(where, valid, mine, theirs, right)


def scale_kernel(levels, where, own, own_extra, *refs):
    messages, (out, turned) = refs[: levels - 1], refs[levels - 1 :]
    chunk, cols = own.shape
    total = own[...]
    extra = own_extra[...]
    for message in messages:
        total = total + message[pl.ds(0, chunk)].astype(f32)
        more = message[pl.ds(chunk, 16)].astype(f32)
        extra = extra + (more[0:8] + more[8:16])
    count = extra[3:4]
    lam_g = extra[0:1] / count
    turned[...] = jnp.transpose(extra / count)
    first = where[0] * chunk
    inside = pl.multiple_of(lax.rem(first, cols), chunk)
    picked = turned[pl.ds(inside, chunk)]
    lam_a = jnp.where(first < cols, picked[:, 1:2], picked[:, 2:3])
    out[...] = (total / count / (lam_a * lam_g + damping)).astype(bf16)


def scale(where, own, own_extra, messages):
    levels = len(messages) + 1
    chunk, cols = own.shape
    return pl.pallas_call(
        functools.partial(scale_kernel, levels),
        out_shape=shape((chunk, cols), bf16),
        in_specs=[SMEM] + [VMEM] * (1 + levels),
        out_specs=VMEM,
        scratch_shapes=[pltpu.VMEM((cols, 8), f32)],
        compiler_params=params(),
        cost_estimate=cost(8 * chunk * cols, 2 * levels * chunk * cols),
    )(where, own, own_extra, *messages)


def result_kernel(levels, where, *refs):
    slots = refs[:levels]
    picked, basis, sent, kept, scaled, sems = refs[levels:]
    chunk = slots[0].shape[0]
    copies = []
    for step, slot in enumerate(slots):
        row = pl.multiple_of((where[0] ^ step) * chunk, chunk)
        copy = pltpu.make_async_copy(slot, scaled.at[pl.ds(row, chunk)], sems.at[step])
        copy.start()
        copies.append(copy)
    for copy in copies:
        copy.wait()
    mid = jnp.dot(picked[...], scaled[...], preferred_element_type=f32).astype(bf16)
    half = mid.shape[0] // 2
    width = basis.shape[0]
    part = width // 4
    for j in range(4):
        columns = pl.ds(j * part, part)
        block = lax.dot_general(mid, basis[columns], (((1,), (1,)), ((), ())), preferred_element_type=f32)
        sent[:, columns] = block[:half].astype(bf16)
        kept[:, columns] = block[half:]


def result(where, slots, picked, basis):
    levels = len(slots)
    height, width = picked.shape
    wide, cols = basis.shape
    return pl.pallas_call(
        functools.partial(result_kernel, levels),
        out_shape=(shape((height // 2, wide), bf16), shape((height // 2, wide), f32)),
        in_specs=[SMEM] + [ANY] * levels + [VMEM, VMEM],
        out_specs=(VMEM, VMEM),
        scratch_shapes=[pltpu.VMEM((width, cols), bf16), pltpu.SemaphoreType.DMA((levels,))],
        compiler_params=params(),
        cost_estimate=cost(2 * height * cols * (width + wide), 2 * wide * cols + 2 * width * cols),
    )(where, *slots, picked, basis)


def gather_levels(unit, level, levels):
    if levels != 4:
        return [unit] + [across(unit, step, levels) for step in range(1, levels)]
    middle = (level == 1) | (level == 2)
    inner, outward = [(1, 2), (2, 1)], [(1, 0), (2, 3)]
    first = across(unit, 1, levels)
    third = lax.ppermute(unit, "level", inner)
    second_in = lax.ppermute(first, "level", inner)
    second_out = lax.ppermute(third, "level", outward)
    second = jnp.where(middle, second_in, second_out)
    third_out = lax.ppermute(second_in, "level", outward)
    third = jnp.where(middle, third, third_out)
    return [unit, first, second, third]


def body(acts, grads, counts, basis_a, basis_g):
    group, level, chip, core = (lax.axis_index(n) for n in ("group", "level", "chip", "core"))
    levels = lax.axis_size("level")
    rows, width_a = acts.shape
    width_g = grads.shape[1]
    rows_a, rows_g = basis_a.shape[0], basis_g.shape[0]
    part_a, part_g = width_a // 4, width_g // 8
    where = jnp.reshape(level, (1,)).astype(jnp.int32)

    def columns(y, c):
        return jnp.concatenate(
            [
                cut(basis_g, ((y * 2 + c) * 2 + group) * part_g, part_g, 1),
                cut(basis_a, (c * 2 + group) * part_a, part_a, 1),
            ]
        )

    def diagonal(x):
        return lax.ppermute(x, ("chip", "core"), [(i, 3 - i) for i in range(4)])

    blocks = jnp.stack(
        [
            columns(chip, core),
            lax.ppermute(columns(chip, 1 - core), "core", SWAP),
            lax.ppermute(columns(1 - chip, core), "chip", SWAP),
            diagonal(columns(1 - chip, 1 - core)),
        ]
    )
    blocks = [lax.dynamic_index_in_dim(blocks, j ^ (chip * 2 + core), 0, False) for j in range(4)]
    unit = jnp.concatenate([b[:rows_g] for b in blocks] + [b[rows_g:] for b in blocks])
    level_g, level_a = 4 * rows_g, 4 * rows_a

    slots = []
    for slot in gather_levels(unit, level, levels):
        slots += [slot, lax.ppermute(slot, "group", SWAP)]
    own_a = jnp.concatenate([slots[0][level_g:], slots[1][level_g:]], axis=1)
    own_a = jnp.concatenate([own_a, lax.ppermute(own_a, "core", SWAP)], axis=1)
    me = chip * 2 + core
    picked = jnp.concatenate([cut(own_a, (me ^ j) * rows_a, rows_a) for j in (3, 1, 2, 0)])

    valid = counts[0]
    keep = jnp.arange(rows, dtype=jnp.int32)[:, None] < valid
    marks = jnp.stack([valid // 16 * 16, valid % 16]).astype(bf16)
    marks = jnp.broadcast_to(jnp.pad(marks, (0, 14))[:, None], (16, width_a))
    acts = jnp.concatenate([jnp.where(keep, acts, 0), marks])
    half = rows // 2
    grads = [jnp.where(keep[:half], grads[:half], 0), jnp.where(keep[half:], grads[half:], 0)]
    ready, _ = lax.optimization_barrier(((acts, grads[0], grads[1]), unit))

    pieces_a = [acts, lax.ppermute(acts, "core", SWAP)]
    got = lax.ppermute(ready[0], "chip", SWAP)
    pieces_a += [got, lax.ppermute(got, "core", SWAP)]
    pieces_g = list(grads) + [lax.ppermute(g, "core", SWAP) for g in grads]
    far = [lax.ppermute(g, "chip", SWAP) for g in ready[1:]]
    pieces_g += far + [lax.ppermute(g, "core", SWAP) for g in far]
    valid_here = sum(p[rows, 0].astype(f32) + p[rows + 1, 0].astype(f32) for p in pieces_a)

    turned_a = turn_acts(where, slots, pieces_a, rows, level_g, level_a)
    their_a = lax.ppermute(turned_a, "core", SWAP)
    turned_g, full_g = turn_grads(where, slots, pieces_g, level_g)
    own, own_extra, *messages = cross(where, jnp.reshape(valid_here, (1,)), turned_a, their_a, turned_g, levels)

    got = [across(m, step + 1, levels) for step, m in enumerate(messages)]
    scaled = scale(where, own, own_extra, got)
    scaled_all = [scaled] + [across(scaled, step, levels) for step in range(1, levels)]

    sent, kept = result(where, scaled_all, picked, full_g)
    sent = lax.ppermute(sent, "core", SWAP).astype(f32)
    last = lax.ppermute((kept[:rows_a] + sent[:rows_a]).astype(bf16), "chip", SWAP)
    return (kept[rows_a:] + sent[rows_a:] + last.astype(f32)).astype(bf16)


def solution(mesh):
    groups, samples = mesh.shape["groups"], mesh.shape["samples"]
    grid = Mesh(mesh.devices.reshape(groups, samples // 4, 2, 2), ("group", "level", "chip", "core"))
    every = ("group", "level", "chip", "core")
    in_specs = (
        P(every, None),
        P(every, None),
        P(every),
        P(every[1:], None),
        P(every[1:], None),
    )
    return jax.shard_map(body, mesh=grid, in_specs=in_specs, out_specs=P(every, None), check_vma=False)
```

```python
import functools

import jax
import jax.numpy as jnp
from jax import lax
from jax.experimental import pallas as pl
from jax.experimental.pallas import tpu as pltpu
from jax.sharding import Mesh, PartitionSpec as P

damping = 0.01
bf16 = jnp.bfloat16
f32 = jnp.float32
SWAP = [(0, 1), (1, 0)]
ANY = pl.BlockSpec(memory_space=pl.ANY)
VMEM = pl.BlockSpec(memory_space=pltpu.VMEM)
SMEM = pl.BlockSpec(memory_space=pltpu.SMEM)
LARGE = 60 * 2**20
MIDDLE = 26 * 2**20
SMALL = 20 * 2**20


def params(limit):
    return pltpu.CompilerParams(vmem_limit_bytes=limit)


def cost(flops, moved):
    return pl.CostEstimate(flops=flops, bytes_accessed=moved, transcendentals=0)


def shape(dims, dtype):
    return jax.ShapeDtypeStruct(dims, dtype)


def cut(x, first, size, axis=0):
    return lax.dynamic_slice_in_dim(x, first, size, axis)


def across(x, step, levels):
    return lax.ppermute(x, "level", [(i, i ^ step) for i in range(levels)])


def turn_kernel(levels, level_g, level_a, rows, where, *refs):
    slots, pieces = refs[:levels], refs[levels : levels + 4]
    out_a, out_g, basis_g, sums, basis_a, held_a, held_g, sems, piece_sems = refs[levels + 4 :]
    half, width = rows // 2, held_a.shape[2]
    part = basis_a.shape[1]
    copies = []
    for step, slot in enumerate(slots):
        at = where[0] ^ step
        for i, (first, height, target) in enumerate(((level_g, level_a, basis_a), (0, level_g, basis_g))):
            row = pl.multiple_of(at * height, height)
            copies.append(
                pltpu.make_async_copy(
                    slot.at[pl.ds(first, height)], target.at[pl.ds(row, height)], sems.at[2 * step + i]
                )
            )
    moves = []
    for i, piece in enumerate(pieces):
        moves.append(pltpu.make_async_copy(piece.at[pl.ds(0, rows + 16)], held_a.at[i], piece_sems.at[3 * i]))
        for j in range(2):
            moves.append(
                pltpu.make_async_copy(
                    piece.at[pl.ds(rows + 16 + j * half, half)],
                    held_g.at[pl.ds(i * half, half), pl.ds(j * width, width)],
                    piece_sems.at[3 * i + 1 + j],
                )
            )
    for copy in copies + moves:
        copy.start()
    for copy in copies:
        copy.wait()
    total_a = jnp.zeros((1, part), f32)
    total_g = jnp.zeros((1, part), f32)
    for i in range(4):
        moves[3 * i].wait()
        block = jnp.dot(held_a[i, :rows], basis_a[...], preferred_element_type=f32).astype(bf16).astype(f32)
        total_a = total_a + jnp.sum(jnp.square(block), axis=0, keepdims=True)
        out_a[:part, i * rows : (i + 1) * rows] = jnp.transpose(block).astype(bf16)
    for i in range(0, 4, 2):
        for j in (1, 2, 4, 5):
            moves[3 * i + j].wait()
        block = pl.ds(i * half, 2 * half)
        turned = jnp.dot(held_g[block], basis_g[...], preferred_element_type=f32).astype(bf16)
        out_g[block] = turned
        total_g = total_g + jnp.sum(jnp.square(turned.astype(f32)), axis=0, keepdims=True)
    high, low = high_low(jnp.broadcast_to(total_a, (8, part)))
    out_a[part:, :part] = jnp.concatenate([high, low])
    out_a[part:, part:] = jnp.zeros((16, 4 * rows - part), bf16)
    marks = sum(held_a[i, rows : rows + 16, :part].astype(f32) for i in range(4))
    sums[0:1] = total_g
    sums[1:2] = marks[0:1] + marks[1:2]
    sums[2:8] = jnp.zeros((6, part), f32)


def turn(where, slots, pieces, rows, level_g, level_a):
    levels = len(slots)
    width_a, width_g = levels * level_a, levels * level_g
    part = slots[0].shape[1]
    half = rows // 2
    return pl.pallas_call(
        functools.partial(turn_kernel, levels, level_g, level_a, rows),
        out_shape=(
            shape((part + 16, 4 * rows), bf16),
            shape((4 * half, part), bf16),
            shape((width_g, part), bf16),
            shape((8, part), f32),
        ),
        in_specs=[SMEM] + [ANY] * (levels + 4),
        out_specs=(VMEM,) * 4,
        scratch_shapes=[
            pltpu.VMEM((width_a, part), bf16),
            pltpu.VMEM((4, rows + 16, width_a), bf16),
            pltpu.VMEM((4 * half, width_g), bf16),
            pltpu.SemaphoreType.DMA((2 * levels,)),
            pltpu.SemaphoreType.DMA((12,)),
        ],
        compiler_params=params(MIDDLE),
        cost_estimate=cost(8 * rows * part * (width_a + width_g // 2), 8 * rows * (width_a + width_g // 2)),
    )(where, *slots, *pieces)


def high_low(v):
    high = v.astype(bf16)
    return high, (v - high.astype(f32)).astype(bf16)


def cross_kernel(levels, rows, where, *refs):
    turned_a, early, bases, pieces, sums = refs[:4], refs[4:6], refs[6:8], refs[8:12], refs[12:14]
    own, own_extra, messages = refs[14], refs[15], refs[16 : 15 + levels]
    left, right, basis, held, whole, extra, sems = refs[15 + levels :]
    half = rows // 2
    part = bases[0].shape[1]
    cols = 2 * part
    width = whole.shape[0]
    chunk = width // levels
    level = where[0]
    count = 0

    def copy(source, target):
        nonlocal count
        made = pltpu.make_async_copy(source, target, sems.at[count])
        made.start()
        count += 1
        return made

    first = [copy(b, basis.at[:, pl.ds(i * part, part)]) for i, b in enumerate(bases)]
    moves = [copy(p, held.at[pl.ds(i * half, half)]) for i, p in enumerate(pieces)]
    rest = [copy(turned_a[i], left.at[i]) for i in range(2)]
    for i in range(2):
        for j, k in enumerate((1, 0, 3, 2)):
            rest.append(
                copy(turned_a[2 + i].at[:, pl.ds(k * rows, rows)], left.at[2 + i, :, pl.ds(j * rows, rows)])
            )
    for i in range(2):
        for j in range(4):
            rest.append(
                copy(early[i].at[pl.ds(j * half, half)], right.at[pl.ds(j * rows, half), pl.ds(i * part, part)])
            )
    for made in first:
        made.wait()
    total = jnp.concatenate([sums[0][0:1], sums[1][0:1]], axis=1)
    for i in range(0, 4, 2):
        moves[i].wait()
        moves[i + 1].wait()
        block = jnp.dot(held[pl.ds(i * half, rows)], basis[...], preferred_element_type=f32).astype(bf16)
        right[pl.ds(i * rows + half, half)] = block[:half]
        right[pl.ds(i * rows + rows + half, half)] = block[half:]
        total = total + jnp.sum(jnp.square(block.astype(f32)), axis=0, keepdims=True)
    for made in rest:
        made.wait()
    extra[...] = jnp.zeros_like(extra)
    extra[0:1] = total
    for i in range(4):
        moved = rows * (i // 2)
        tail = left[i, part:, moved : moved + part].astype(f32)
        at = pl.ds((i % 2) * part, part)
        extra[1 + i // 2 : 2 + i // 2, at] = tail[0:1] + tail[8:9]
        whole[pl.ds(i * part, part)] = jnp.dot(left[i, :part], right[...], preferred_element_type=f32)
        if i < 2:
            extra[3:4, at] = sums[i][1:2]
    high, low = high_low(extra[...])
    own_extra[...] = extra[...]
    own[...] = whole[pl.ds(pl.multiple_of(level * chunk, chunk), chunk)]
    for step in range(1, levels):
        to = pl.multiple_of((level ^ step) * chunk, chunk)
        message = messages[step - 1]
        message[pl.ds(0, chunk)] = whole[pl.ds(to, chunk)].astype(bf16)
        message[pl.ds(chunk, 16)] = jnp.concatenate([high, low])


def cross(where, turned_a, early, bases, pieces, sums, rows, levels):
    width_g, part = bases[0].shape
    width = 4 * part
    cols = 2 * part
    chunk = width // levels
    return pl.pallas_call(
        functools.partial(cross_kernel, levels, rows),
        out_shape=[shape((chunk, cols), f32), shape((8, cols), f32)] + [shape((chunk + 16, cols), bf16)] * (levels - 1),
        in_specs=[SMEM] + [ANY] * 12 + [VMEM] * 2,
        out_specs=[VMEM] * (1 + levels),
        scratch_shapes=[
            pltpu.VMEM((4, part + 16, 4 * rows), bf16),
            pltpu.VMEM((4 * rows, cols), bf16),
            pltpu.VMEM((width_g, cols), bf16),
            pltpu.VMEM((2 * rows, width_g), bf16),
            pltpu.VMEM((width, cols), f32),
            pltpu.VMEM((8, cols), f32),
            pltpu.SemaphoreType.DMA((24,)),
        ],
        compiler_params=params(LARGE),
        cost_estimate=cost(4 * rows * cols * (width_g + 2 * width), 16 * rows * width),
    )(where, *turned_a, *early, *bases, *pieces, *sums)


def scale_kernel(levels, where, own, own_extra, *refs):
    messages, (out, turned) = refs[: levels - 1], refs[levels - 1 :]
    chunk, cols = own.shape
    total = own[...]
    extra = own_extra[...]
    for message in messages:
        total = total + message[pl.ds(0, chunk)].astype(f32)
        more = message[pl.ds(chunk, 16)].astype(f32)
        extra = extra + (more[0:8] + more[8:16])
    count = extra[3:4]
    lam_g = extra[0:1] / count
    turned[...] = jnp.transpose(extra / count)
    first = where[0] * chunk
    inside = pl.multiple_of(lax.rem(first, cols), chunk)
    picked = turned[pl.ds(inside, chunk)]
    lam_a = jnp.where(first < cols, picked[:, 1:2], picked[:, 2:3])
    out[...] = (total / count / (lam_a * lam_g + damping)).astype(bf16)


def scale(where, own, own_extra, messages):
    levels = len(messages) + 1
    chunk, cols = own.shape
    return pl.pallas_call(
        functools.partial(scale_kernel, levels),
        out_shape=shape((chunk, cols), bf16),
        in_specs=[SMEM] + [VMEM] * (1 + levels),
        out_specs=VMEM,
        scratch_shapes=[pltpu.VMEM((cols, 8), f32)],
        compiler_params=params(SMALL),
        cost_estimate=cost(8 * chunk * cols, 2 * levels * chunk * cols),
    )(where, own, own_extra, *messages)


def result_kernel(levels, where, *refs):
    slots = refs[:levels]
    picked, one, two, sent, kept, scaled, sems = refs[levels:]
    chunk = slots[0].shape[0]
    copies = []
    for step, slot in enumerate(slots):
        row = pl.multiple_of((where[0] ^ step) * chunk, chunk)
        copy = pltpu.make_async_copy(slot, scaled.at[pl.ds(row, chunk)], sems.at[step])
        copy.start()
        copies.append(copy)
    for copy in copies:
        copy.wait()
    mid = jnp.dot(picked[...], scaled[...], preferred_element_type=f32).astype(bf16)
    half = mid.shape[0] // 2
    wide, side = one.shape
    part = wide // 4
    for j in range(4):
        columns = pl.ds(j * part, part)
        block = sum(
            lax.dot_general(m, b[columns], (((1,), (1,)), ((), ())), preferred_element_type=f32)
            for m, b in ((mid[:, :side], one), (mid[:, side:], two))
        )
        sent[:, columns] = block[:half].astype(bf16)
        kept[:, columns] = block[half:]


def result(where, slots, picked, bases):
    levels = len(slots)
    height, width = picked.shape
    wide, cols = bases[0].shape[0], 2 * bases[0].shape[1]
    return pl.pallas_call(
        functools.partial(result_kernel, levels),
        out_shape=(shape((height // 2, wide), bf16), shape((height // 2, wide), f32)),
        in_specs=[SMEM] + [ANY] * levels + [VMEM] * 3,
        out_specs=(VMEM, VMEM),
        scratch_shapes=[pltpu.VMEM((width, cols), bf16), pltpu.SemaphoreType.DMA((levels,))],
        compiler_params=params(SMALL),
        cost_estimate=cost(2 * height * cols * (width + wide), 2 * wide * cols + 2 * width * cols),
    )(where, *slots, picked, *bases)


def gather_levels(unit, level, levels):
    def over(slot):
        return lax.ppermute(slot, "group", SWAP)

    if levels != 4:
        slots = [unit] + [across(unit, step, levels) for step in range(1, levels)]
        return slots, [over(slot) for slot in slots]
    middle = (level == 1) | (level == 2)
    inner, outward = [(1, 2), (2, 1)], [(1, 0), (2, 3)]
    together = lax.optimization_barrier
    first, third, other0 = together((across(unit, 1, levels), lax.ppermute(unit, "level", inner), over(unit)))
    inside, outside, other1 = together(
        (lax.ppermute(first, "level", inner), lax.ppermute(third, "level", outward), over(first))
    )
    second = jnp.where(middle, inside, outside)
    outside, other2 = together((lax.ppermute(inside, "level", outward), over(second)))
    third = jnp.where(middle, third, outside)
    return [unit, first, second, third], [other0, other1, other2, over(third)]


def body(acts, grads, counts, basis_a, basis_g):
    group, level, chip, core = (lax.axis_index(n) for n in ("group", "level", "chip", "core"))
    levels = lax.axis_size("level")
    rows, width_a = acts.shape
    width_g = grads.shape[1]
    rows_a, rows_g = basis_a.shape[0], basis_g.shape[0]
    part_a, part_g = width_a // 4, width_g // 8
    where = jnp.reshape(level, (1,)).astype(jnp.int32)

    def columns(y, c):
        return jnp.concatenate(
            [
                cut(basis_g, ((y * 2 + c) * 2 + group) * part_g, part_g, 1),
                cut(basis_a, (c * 2 + group) * part_a, part_a, 1),
            ]
        )

    def diagonal(x):
        return lax.ppermute(x, ("chip", "core"), [(i, 3 - i) for i in range(4)])

    blocks = jnp.stack(
        [
            columns(chip, core),
            lax.ppermute(columns(chip, 1 - core), "core", SWAP),
            lax.ppermute(columns(1 - chip, core), "chip", SWAP),
            diagonal(columns(1 - chip, 1 - core)),
        ]
    )
    blocks = [lax.dynamic_index_in_dim(blocks, j ^ (chip * 2 + core), 0, False) for j in range(4)]
    unit = jnp.concatenate([b[:rows_g] for b in blocks] + [b[rows_g:] for b in blocks])
    level_g, level_a = 4 * rows_g, 4 * rows_a

    slots, others = gather_levels(unit, level, levels)
    own_a = jnp.concatenate([slots[0][level_g:], others[0][level_g:]], axis=1)
    own_a = jnp.concatenate([own_a, lax.ppermute(own_a, "core", SWAP)], axis=1)
    me = chip * 2 + core
    picked = jnp.concatenate([cut(own_a, (me ^ j) * rows_a, rows_a) for j in (3, 1, 2, 0)])

    valid = counts[0]
    keep = jnp.arange(rows, dtype=jnp.int32)[:, None] < valid
    marks = jnp.stack([valid // 16 * 16, valid % 16]).astype(bf16)
    marks = jnp.broadcast_to(jnp.pad(marks, (0, 14))[:, None], (16, width_a))
    half = rows // 2
    early = jnp.where(keep[:half], grads[:half], 0)
    early = jnp.concatenate([jnp.where(keep, acts, 0), marks, early[:, :width_a], early[:, width_a:]])
    late = jnp.where(keep[half:], grads[half:], 0)
    (early_out, late_out), _ = lax.optimization_barrier(((early, late), unit))

    def four(mine, out, after=None):
        far = lax.ppermute(out, "chip", SWAP)
        if after is not None:
            far, _ = lax.optimization_barrier((far, after))
        return [mine, lax.ppermute(mine, "core", SWAP), far, lax.ppermute(far, "core", SWAP)]

    early, late = four(early, early_out, slots[-1]), four(late, late_out)
    turned_a, turned_g, bases, sums = zip(
        turn(where, slots, early, rows, level_g, level_a), turn(where, others, early, rows, level_g, level_a)
    )
    turned_a += tuple(lax.ppermute(t, "core", SWAP) for t in turned_a)
    own, own_extra, *messages = cross(where, turned_a, turned_g, bases, late, sums, rows, levels)

    got = [across(m, step + 1, levels) for step, m in enumerate(messages)]
    scaled = scale(where, own, own_extra, got)
    scaled_all = [scaled] + [across(scaled, step, levels) for step in range(1, levels)]

    sent, kept = result(where, scaled_all, picked, bases)
    sent = lax.ppermute(sent, "core", SWAP).astype(f32)
    last = lax.ppermute((kept[:rows_a] + sent[:rows_a]).astype(bf16), "chip", SWAP)
    return (kept[rows_a:] + sent[rows_a:] + last.astype(f32)).astype(bf16)


def solution(mesh):
    groups, samples = mesh.shape["groups"], mesh.shape["samples"]
    grid = Mesh(mesh.devices.reshape(groups, samples // 4, 2, 2), ("group", "level", "chip", "core"))
    every = ("group", "level", "chip", "core")
    in_specs = (
        P(every, None),
        P(every, None),
        P(every),
        P(every[1:], None),
        P(every[1:], None),
    )
    return jax.shard_map(body, mesh=grid, in_specs=in_specs, out_specs=P(every, None), check_vma=False)
```

```python
import functools

import jax
import jax.numpy as jnp
from jax import lax
from jax.experimental import pallas as pl
from jax.experimental.pallas import tpu as pltpu
from jax.sharding import Mesh, PartitionSpec as P

damping = 0.01
bf16 = jnp.bfloat16
f32 = jnp.float32
SWAP = [(0, 1), (1, 0)]
ANY = pl.BlockSpec(memory_space=pl.ANY)
VMEM = pl.BlockSpec(memory_space=pltpu.VMEM)
SMEM = pl.BlockSpec(memory_space=pltpu.SMEM)
LARGE = 18 * 2**20
MIDDLE = 16 * 2**20
SMALL = 12 * 2**20


def params(limit):
    return pltpu.CompilerParams(vmem_limit_bytes=limit)


def cost(flops, moved):
    return pl.CostEstimate(flops=flops, bytes_accessed=moved, transcendentals=0)


def shape(dims, dtype):
    return jax.ShapeDtypeStruct(dims, dtype)


def cut(x, first, size, axis=0):
    return lax.dynamic_slice_in_dim(x, first, size, axis)


def across(x, step, levels):
    return lax.ppermute(x, "level", [(i, i ^ step) for i in range(levels)])


def split(rows):
    return rows * 2 // 3, rows - rows * 2 // 3


def turn_kernel(levels, level_g, level_a, rows, where, *refs):
    slots, pieces = refs[:levels], refs[levels : levels + 4]
    basis_a, out_g, basis_g, sums, sems = refs[levels + 4 :]
    half, width = split(rows)[0], basis_a.shape[0]
    part = basis_a.shape[1]
    copies = []
    for i, (first, height, target) in enumerate(((level_g, level_a, basis_a), (0, level_g, basis_g))):
        for step, slot in enumerate(slots):
            row = pl.multiple_of((where[0] ^ step) * height, height)
            copy = pltpu.make_async_copy(
                slot.at[pl.ds(first, height)], target.at[pl.ds(row, height)], sems.at[i * levels + step]
            )
            copy.start()
            copies.append(copy)
    for copy in copies[:levels]:
        copy.wait()
    total_a = jnp.zeros((1, part), f32)
    total_g = jnp.zeros((1, part), f32)
    for piece in pieces:
        block = jnp.dot(piece[:rows], basis_a[...], preferred_element_type=f32).astype(bf16)
        total_a = total_a + jnp.sum(jnp.square(block.astype(f32)), axis=0, keepdims=True)
    for copy in copies[levels:]:
        copy.wait()
    for i, piece in enumerate(pieces):
        turned = sum(
            jnp.dot(
                piece[pl.ds(rows + 16 + j * half, half)],
                basis_g[pl.ds(j * width, width)],
                preferred_element_type=f32,
            )
            for j in range(2)
        ).astype(bf16)
        out_g[pl.ds(i * half, half)] = turned
        total_g = total_g + jnp.sum(jnp.square(turned.astype(f32)), axis=0, keepdims=True)
    marks = sum(piece[rows : rows + 16, :part].astype(f32) for piece in pieces)
    sums[0:1] = total_g
    sums[1:2] = marks[0:1] + marks[1:2]
    sums[2:3] = total_a
    sums[3:8] = jnp.zeros((5, part), f32)


def turn(where, slots, pieces, rows, level_g, level_a):
    levels = len(slots)
    width_a, width_g = levels * level_a, levels * level_g
    part = slots[0].shape[1]
    half = split(rows)[0]
    return pl.pallas_call(
        functools.partial(turn_kernel, levels, level_g, level_a, rows),
        out_shape=(
            shape((width_a, part), bf16),
            shape((4 * half, part), bf16),
            shape((width_g, part), bf16),
            shape((8, part), f32),
        ),
        in_specs=[SMEM] + [ANY] * levels + [VMEM] * 4,
        out_specs=(VMEM,) * 4,
        scratch_shapes=[pltpu.SemaphoreType.DMA((2 * levels,))],
        compiler_params=params(MIDDLE),
        cost_estimate=cost(8 * rows * part * (width_a + width_g // 2), 8 * rows * (width_a + width_g // 2)),
    )(where, *slots, *pieces)


def high_low(v):
    high = v.astype(bf16)
    return high, (v - high.astype(f32)).astype(bf16)


def cross_kernel(levels, rows, where, *refs):
    acts, early, bases, pieces, sums = refs[:4], refs[4:6], refs[6:8], refs[8:12], refs[12:16]
    own, own_extra, messages = refs[16], refs[17], refs[18 : 17 + levels]
    left, right, basis, held, whole, extra, sems = refs[17 + levels :]
    half, late = split(rows)
    part = bases[0].shape[1]
    cols = 2 * part
    chunk = cols // levels
    level = where[0]
    count = 0

    def copy(source, target):
        nonlocal count
        made = pltpu.make_async_copy(source, target, sems.at[count])
        made.start()
        count += 1
        return made

    first = [copy(b, basis.at[:, pl.ds(i * part, part)]) for i, b in enumerate(bases)]
    moves = [copy(p, held.at[pl.ds(i * late, late)]) for i, p in enumerate(pieces)]
    rest = [copy(a.at[pl.ds(0, rows)], left.at[pl.ds(i * rows, rows)]) for i, a in enumerate(acts)]
    for i in range(2):
        for j in range(4):
            rest.append(
                copy(early[i].at[pl.ds(j * half, half)], right.at[pl.ds(j * rows, half), pl.ds(i * part, part)])
            )
    for made in first:
        made.wait()
    total = jnp.concatenate([sums[0][0:1], sums[1][0:1]], axis=1)
    for i in range(0, 4, 2):
        moves[i].wait()
        moves[i + 1].wait()
        block = jnp.dot(held[pl.ds(i * late, 2 * late)], basis[...], preferred_element_type=f32).astype(bf16)
        right[pl.ds(i * rows + half, late)] = block[:late]
        right[pl.ds(i * rows + rows + half, late)] = block[late:]
        total = total + jnp.sum(jnp.square(block.astype(f32)), axis=0, keepdims=True)
    for made in rest:
        made.wait()
    extra[...] = jnp.zeros_like(extra)
    extra[0:1, :cols] = total
    for i in range(4):
        extra[1:2, pl.ds(i * part, part)] = sums[i][2:3]
        extra[2:3, pl.ds(i * part, part)] = sums[i][1:2]
    for i in range(2):
        block = pl.ds(i * part, part)
        whole[block] = lax.dot_general(
            right[:, block], left[...], (((0,), (0,)), ((), ())), preferred_element_type=f32
        )
    high, low = high_low(extra[...])
    own_extra[...] = extra[...]
    own[...] = whole[pl.ds(pl.multiple_of(level * chunk, chunk), chunk)]
    for step in range(1, levels):
        to = pl.multiple_of((level ^ step) * chunk, chunk)
        message = messages[step - 1]
        message[pl.ds(0, chunk)] = whole[pl.ds(to, chunk)].astype(bf16)
        message[pl.ds(chunk, 16)] = jnp.concatenate([high, low])


def cross(where, acts, early, bases, pieces, sums, rows, levels):
    width_g, part = bases[0].shape
    width = acts[0].shape[1]
    cols = 2 * part
    chunk = cols // levels
    return pl.pallas_call(
        functools.partial(cross_kernel, levels, rows),
        out_shape=[shape((chunk, width), f32), shape((8, width), f32)]
        + [shape((chunk + 16, width), bf16)] * (levels - 1),
        in_specs=[SMEM] + [ANY] * 12 + [VMEM] * 4,
        out_specs=[VMEM] * (1 + levels),
        scratch_shapes=[
            pltpu.VMEM((4 * rows, width), bf16),
            pltpu.VMEM((4 * rows, cols), bf16),
            pltpu.VMEM((width_g, cols), bf16),
            pltpu.VMEM((4 * split(rows)[1], width_g), bf16),
            pltpu.VMEM((cols, width), f32),
            pltpu.VMEM((8, width), f32),
            pltpu.SemaphoreType.DMA((18,)),
        ],
        compiler_params=params(LARGE),
        cost_estimate=cost(4 * rows * cols * (width_g + 2 * width), 16 * rows * width),
    )(where, *acts, *early, *bases, *pieces, *sums)


def middle_kernel(levels, where, own, own_extra, *refs):
    messages, bases, outs = refs[: levels - 1], refs[levels - 1 : levels + 3], refs[levels + 3 : 2 * levels + 3]
    basis, turned = refs[2 * levels + 3 :]
    chunk, width = own.shape
    cols = chunk * levels
    part = bases[0].shape[1]
    for i, b in enumerate(bases):
        basis[:, pl.ds(i * part, part)] = b[...]
    total = own[...]
    extra = own_extra[...]
    for message in messages:
        total = total + message[pl.ds(0, chunk)].astype(f32)
        more = message[pl.ds(chunk, 16)].astype(f32)
        extra = extra + (more[0:8] + more[8:16])
    count = extra[2:3]
    extra = extra / count
    lam_a = extra[1:2]
    turned[...] = jnp.transpose(extra[:, :cols])
    lam_g = turned[pl.ds(pl.multiple_of(where[0] * chunk, chunk), chunk)][:, 0:1]
    both = jnp.dot(jnp.concatenate(high_low(total)), basis[...], preferred_element_type=f32)
    rotated = (both[:chunk] + both[chunk:]) / count
    scaled = (rotated / (lam_g * lam_a + damping)).astype(bf16)
    height = width // levels
    for step, out in enumerate(outs):
        rows = pl.ds(pl.multiple_of((where[0] ^ step) * height, height), height)
        out[...] = lax.dot_general(
            scaled, basis[rows], (((1,), (1,)), ((), ())), preferred_element_type=f32
        ).astype(bf16)


def middle(where, own, own_extra, messages, bases):
    levels = len(messages) + 1
    chunk, width = own.shape
    return pl.pallas_call(
        functools.partial(middle_kernel, levels),
        out_shape=[shape((chunk, width // levels), bf16)] * levels,
        in_specs=[SMEM] + [VMEM] * (levels + 5),
        out_specs=[VMEM] * levels,
        scratch_shapes=[pltpu.VMEM((width, width), bf16), pltpu.VMEM((chunk * levels, 8), f32)],
        compiler_params=params(SMALL),
        cost_estimate=cost(6 * chunk * width * width, 2 * width * width),
    )(where, own, own_extra, *messages, *bases)


def result_kernel(levels, where, *refs):
    slots = refs[:levels]
    one, two, sent, kept, mid, whole, sems = refs[levels:]
    chunk, height = slots[0].shape
    wide, part = one.shape
    copies = []
    for step, slot in enumerate(slots):
        row = pl.multiple_of((where[0] ^ step) * chunk, chunk)
        copy = pltpu.make_async_copy(slot, mid.at[pl.ds(row, chunk)], sems.at[step])
        copy.start()
        copies.append(copy)
    for copy in copies:
        copy.wait()
    quarter = wide // 4
    for j in range(4):
        columns = pl.ds(j * quarter, quarter)
        whole[:, columns] = sum(
            lax.dot_general(
                mid[pl.ds(i * part, part)], b[columns], (((0,), (1,)), ((), ())), preferred_element_type=f32
            )
            for i, b in enumerate((one, two))
        )
    rows = height // 4
    for i, (other, target) in enumerate(((3, sent), (1, sent), (2, kept), (0, kept))):
        block = whole[pl.ds(pl.multiple_of((where[1] ^ other) * rows, rows), rows)]
        target[pl.ds((i % 2) * rows, rows)] = block.astype(target.dtype)


def result(where, slots, bases):
    levels = len(slots)
    chunk, height = slots[0].shape
    wide, part = bases[0].shape
    return pl.pallas_call(
        functools.partial(result_kernel, levels),
        out_shape=(shape((height // 2, wide), f32), shape((height // 2, wide), f32)),
        in_specs=[SMEM] + [ANY] * levels + [VMEM] * 2,
        out_specs=(VMEM, VMEM),
        scratch_shapes=[
            pltpu.VMEM((2 * part, height), bf16),
            pltpu.VMEM((height, wide), f32),
            pltpu.SemaphoreType.DMA((levels,)),
        ],
        compiler_params=params(SMALL),
        cost_estimate=cost(4 * height * part * wide, 4 * wide * part),
    )(where, *slots, *bases)


def gather_levels(unit, level, levels):
    def over(slot):
        return lax.ppermute(slot, "group", SWAP)

    if levels != 4:
        slots = [unit] + [across(unit, step, levels) for step in range(1, levels)]
        return slots, [over(slot) for slot in slots]
    middle = (level == 1) | (level == 2)
    inner, outward = [(1, 2), (2, 1)], [(1, 0), (2, 3)]
    together = lax.optimization_barrier
    first, third, other0 = together((across(unit, 1, levels), lax.ppermute(unit, "level", inner), over(unit)))
    inside, outside, other1 = together(
        (lax.ppermute(first, "level", inner), lax.ppermute(third, "level", outward), over(first))
    )
    second = jnp.where(middle, inside, outside)
    outside, other2 = together((lax.ppermute(inside, "level", outward), over(second)))
    third = jnp.where(middle, third, outside)
    return [unit, first, second, third], [other0, other1, other2, over(third)]


def body(acts, grads, counts, basis_a, basis_g):
    group, level, chip, core = (lax.axis_index(n) for n in ("group", "level", "chip", "core"))
    levels = lax.axis_size("level")
    rows, width_a = acts.shape
    width_g = grads.shape[1]
    rows_a, rows_g = basis_a.shape[0], basis_g.shape[0]
    part_a, part_g = width_a // 4, width_g // 8
    where = jnp.stack([level, chip * 2 + core]).astype(jnp.int32)

    def columns(y, c):
        return jnp.concatenate(
            [
                cut(basis_g, ((y * 2 + c) * 2 + group) * part_g, part_g, 1),
                cut(basis_a, (c * 2 + group) * part_a, part_a, 1),
            ]
        )

    def diagonal(x):
        return lax.ppermute(x, ("chip", "core"), [(i, 3 - i) for i in range(4)])

    beside = lax.ppermute(columns(chip, 1 - core), "core", SWAP)
    blocks = jnp.stack(
        [
            columns(chip, core),
            beside,
            lax.ppermute(columns(1 - chip, core), "chip", SWAP),
            diagonal(columns(1 - chip, 1 - core)),
        ]
    )
    blocks = [lax.dynamic_index_in_dim(blocks, j ^ (chip * 2 + core), 0, False) for j in range(4)]
    unit = jnp.concatenate([b[:rows_g] for b in blocks] + [b[rows_g:] for b in blocks])
    level_g, level_a = 4 * rows_g, 4 * rows_a

    slots, others = gather_levels(unit, level, levels)
    valid = counts[0]
    keep = jnp.arange(rows, dtype=jnp.int32)[:, None] < valid
    marks = jnp.stack([valid // 16 * 16, valid % 16]).astype(bf16)
    marks = jnp.broadcast_to(jnp.pad(marks, (0, 14))[:, None], (16, width_a))
    half = split(rows)[0]
    early = jnp.where(keep[:half], grads[:half], 0)
    early = jnp.concatenate([jnp.where(keep, acts, 0), marks, early[:, :width_a], early[:, width_a:]])
    late = jnp.where(keep[half:], grads[half:], 0)
    (early_out, late_out), _ = lax.optimization_barrier(((early, late), beside))

    def four(mine, out, after):
        far = lax.ppermute(out, "chip", SWAP)
        if after is not None:
            far, after = lax.optimization_barrier((far, after))
        return [mine, lax.ppermute(mine, "core", SWAP), far, lax.ppermute(far, "core", SWAP)], after

    early, slots[-1] = four(early, early_out, slots[-1])
    late, _ = four(late, late_out, None)
    bases_a, turned_g, bases_g, sums = zip(
        turn(where, slots, early, rows, level_g, level_a), turn(where, others, early, rows, level_g, level_a)
    )
    sums += tuple(lax.ppermute(t, "core", SWAP) for t in sums)
    bases_a += tuple(lax.ppermute(t, "core", SWAP) for t in bases_a)
    own, own_extra, *messages = cross(where, early, turned_g, bases_g, late, sums, rows, levels)

    got = [across(m, step + 1, levels) for step, m in enumerate(messages)]
    mids = middle(where, own, own_extra, got, bases_a)
    mids = [m if step == 0 else across(m, step, levels) for step, m in enumerate(mids)]

    sent, kept = result(where, mids, bases_g)
    sent = lax.ppermute(sent.astype(bf16), "core", SWAP).astype(f32)
    last = lax.ppermute((kept[:rows_a] + sent[:rows_a]).astype(bf16), "chip", SWAP)
    return (kept[rows_a:] + sent[rows_a:] + last.astype(f32)).astype(bf16)


def solution(mesh):
    groups, samples = mesh.shape["groups"], mesh.shape["samples"]
    grid = Mesh(mesh.devices.reshape(groups, samples // 4, 2, 2), ("group", "level", "chip", "core"))
    every = ("group", "level", "chip", "core")
    in_specs = (
        P(every, None),
        P(every, None),
        P(every),
        P(every[1:], None),
        P(every[1:], None),
    )
    return jax.shard_map(body, mesh=grid, in_specs=in_specs, out_specs=P(every, None), check_vma=False)
```

```python
import functools

import jax
import jax.numpy as jnp
from jax import lax
from jax.experimental import pallas as pl
from jax.experimental.pallas import tpu as pltpu
from jax.sharding import Mesh, PartitionSpec as P

damping = 0.01
bf16 = jnp.bfloat16
f32 = jnp.float32
SWAP = [(0, 1), (1, 0)]
ANY = pl.BlockSpec(memory_space=pl.ANY)
VMEM = pl.BlockSpec(memory_space=pltpu.VMEM)
SMEM = pl.BlockSpec(memory_space=pltpu.SMEM)
LARGE = 18 * 2**20
MIDDLE = 16 * 2**20
SMALL = 12 * 2**20


def params(limit):
    return pltpu.CompilerParams(vmem_limit_bytes=limit)


def cost(flops, moved):
    return pl.CostEstimate(flops=flops, bytes_accessed=moved, transcendentals=0)


def shape(dims, dtype):
    return jax.ShapeDtypeStruct(dims, dtype)


def cut(x, first, size, axis=0):
    return lax.dynamic_slice_in_dim(x, first, size, axis)


def across(x, step, levels):
    return lax.ppermute(x, "level", [(i, i ^ step) for i in range(levels)])


def split(rows):
    return rows * 2 // 3, rows - rows * 2 // 3


def turn_kernel(levels, level_g, level_a, rows, where, *refs):
    slots, pieces = refs[:levels], refs[levels : levels + 4]
    basis_a, out_g, basis_g, sums, sems = refs[levels + 4 :]
    half, width = split(rows)[0], basis_a.shape[0]
    part = basis_a.shape[1]
    copies = []
    for i, (first, height, target) in enumerate(((level_g, level_a, basis_a), (0, level_g, basis_g))):
        for step, slot in enumerate(slots):
            row = pl.multiple_of((where[0] ^ step) * height, height)
            copy = pltpu.make_async_copy(
                slot.at[pl.ds(first, height)], target.at[pl.ds(row, height)], sems.at[i * levels + step]
            )
            copy.start()
            copies.append(copy)
    for copy in copies[:levels]:
        copy.wait()
    total_a = jnp.zeros((1, part), f32)
    total_g = jnp.zeros((1, part), f32)
    for piece in pieces:
        block = jnp.dot(piece[:rows], basis_a[...], preferred_element_type=f32).astype(bf16)
        total_a = total_a + jnp.sum(jnp.square(block.astype(f32)), axis=0, keepdims=True)
    for copy in copies[levels:]:
        copy.wait()
    for i, piece in enumerate(pieces):
        turned = sum(
            jnp.dot(
                piece[pl.ds(rows + 16 + j * half, half)],
                basis_g[pl.ds(j * width, width)],
                preferred_element_type=f32,
            )
            for j in range(2)
        ).astype(bf16)
        out_g[pl.ds(i * half, half)] = turned
        total_g = total_g + jnp.sum(jnp.square(turned.astype(f32)), axis=0, keepdims=True)
    marks = sum(piece[rows : rows + 16, :part].astype(f32) for piece in pieces)
    sums[0:1] = total_g
    sums[1:2] = marks[0:1] + marks[1:2]
    sums[2:3] = total_a
    sums[3:8] = jnp.zeros((5, part), f32)


def turn(where, slots, pieces, rows, level_g, level_a):
    levels = len(slots)
    width_a, width_g = levels * level_a, levels * level_g
    part = slots[0].shape[1]
    half = split(rows)[0]
    return pl.pallas_call(
        functools.partial(turn_kernel, levels, level_g, level_a, rows),
        out_shape=(
            shape((width_a, part), bf16),
            shape((4 * half, part), bf16),
            shape((width_g, part), bf16),
            shape((8, part), f32),
        ),
        in_specs=[SMEM] + [ANY] * levels + [VMEM] * 4,
        out_specs=(VMEM,) * 4,
        scratch_shapes=[pltpu.SemaphoreType.DMA((2 * levels,))],
        compiler_params=params(MIDDLE),
        cost_estimate=cost(8 * rows * part * (width_a + width_g // 2), 8 * rows * (width_a + width_g // 2)),
    )(where, *slots, *pieces)


def high_low(v):
    high = v.astype(bf16)
    return high, (v - high.astype(f32)).astype(bf16)


def cross_kernel(levels, rows, where, *refs):
    acts, early, bases, pieces, sums = refs[:4], refs[4:6], refs[6:8], refs[8:12], refs[12:16]
    own, own_extra, messages = refs[16], refs[17], refs[18 : 17 + levels]
    left, right, basis, held, whole, extra, sems = refs[17 + levels :]
    half, late = split(rows)
    part = bases[0].shape[1]
    cols = 2 * part
    chunk = cols // levels
    level = where[0]
    count = 0

    def copy(source, target):
        nonlocal count
        made = pltpu.make_async_copy(source, target, sems.at[count])
        made.start()
        count += 1
        return made

    first = [copy(b, basis.at[:, pl.ds(i * part, part)]) for i, b in enumerate(bases)]
    moves = [copy(p, held.at[pl.ds(i * late, late)]) for i, p in enumerate(pieces)]
    rest = [copy(a.at[pl.ds(0, rows)], left.at[pl.ds(i * rows, rows)]) for i, a in enumerate(acts)]
    for i in range(2):
        for j in range(4):
            rest.append(
                copy(early[i].at[pl.ds(j * half, half)], right.at[pl.ds(j * rows, half), pl.ds(i * part, part)])
            )
    for made in first:
        made.wait()
    total = jnp.concatenate([sums[0][0:1], sums[1][0:1]], axis=1)
    for i in range(0, 4, 2):
        moves[i].wait()
        moves[i + 1].wait()
        block = jnp.dot(held[pl.ds(i * late, 2 * late)], basis[...], preferred_element_type=f32).astype(bf16)
        right[pl.ds(i * rows + half, late)] = block[:late]
        right[pl.ds(i * rows + rows + half, late)] = block[late:]
        total = total + jnp.sum(jnp.square(block.astype(f32)), axis=0, keepdims=True)
    for made in rest:
        made.wait()
    extra[...] = jnp.zeros_like(extra)
    extra[0:1, :cols] = total
    for i in range(4):
        extra[1:2, pl.ds(i * part, part)] = sums[i][2:3]
        extra[2:3, pl.ds(i * part, part)] = sums[i][1:2]
    for i in range(2):
        block = pl.ds(i * part, part)
        whole[block] = lax.dot_general(
            right[:, block], left[...], (((0,), (0,)), ((), ())), preferred_element_type=f32
        )
    high, low = high_low(extra[...])
    own_extra[...] = extra[...]
    own[...] = whole[pl.ds(pl.multiple_of(level * chunk, chunk), chunk)]
    for step in range(1, levels):
        to = pl.multiple_of((level ^ step) * chunk, chunk)
        messages[step - 1][...] = jnp.concatenate([whole[pl.ds(to, chunk)].astype(bf16), high[:4], low[:4]])


def cross(where, acts, early, bases, pieces, sums, rows, levels):
    width_g, part = bases[0].shape
    width = acts[0].shape[1]
    cols = 2 * part
    chunk = cols // levels
    return pl.pallas_call(
        functools.partial(cross_kernel, levels, rows),
        out_shape=[shape((chunk, width), f32), shape((8, width), f32)]
        + [shape((chunk + 8, width), bf16)] * (levels - 1),
        in_specs=[SMEM] + [ANY] * 12 + [VMEM] * 4,
        out_specs=[VMEM] * (1 + levels),
        scratch_shapes=[
            pltpu.VMEM((4 * rows, width), bf16),
            pltpu.VMEM((4 * rows, cols), bf16),
            pltpu.VMEM((width_g, cols), bf16),
            pltpu.VMEM((4 * split(rows)[1], width_g), bf16),
            pltpu.VMEM((cols, width), f32),
            pltpu.VMEM((8, width), f32),
            pltpu.SemaphoreType.DMA((18,)),
        ],
        compiler_params=params(LARGE),
        cost_estimate=cost(4 * rows * cols * (width_g + 2 * width), 16 * rows * width),
    )(where, *acts, *early, *bases, *pieces, *sums)


def middle_kernel(levels, where, own, own_extra, *refs):
    messages, bases, outs = refs[: levels - 1], refs[levels - 1 : levels + 3], refs[levels + 3 : 2 * levels + 3]
    basis, turned = refs[2 * levels + 3 :]
    chunk, width = own.shape
    cols = chunk * levels
    part = bases[0].shape[1]
    for i, b in enumerate(bases):
        basis[:, pl.ds(i * part, part)] = b[...]
    total = own[...]
    extra = own_extra[...]
    for message in messages:
        part_sum = message[...].astype(f32)
        total = total + part_sum[:chunk]
        more = part_sum[chunk:]
        extra = extra + jnp.concatenate([more[0:4] + more[4:8], jnp.zeros_like(more[:4])])
    count = extra[2:3]
    extra = extra / count
    lam_a = extra[1:2]
    turned[...] = jnp.transpose(extra[:, :cols])
    lam_g = turned[pl.ds(pl.multiple_of(where[0] * chunk, chunk), chunk)][:, 0:1]
    both = jnp.dot(jnp.concatenate(high_low(total)), basis[...], preferred_element_type=f32)
    rotated = (both[:chunk] + both[chunk:]) / count
    scaled = (rotated / (lam_g * lam_a + damping)).astype(bf16)
    height = width // levels
    for step, out in enumerate(outs):
        rows = pl.ds(pl.multiple_of((where[0] ^ step) * height, height), height)
        out[...] = lax.dot_general(
            scaled, basis[rows], (((1,), (1,)), ((), ())), preferred_element_type=f32
        ).astype(bf16)


def middle(where, own, own_extra, messages, bases):
    levels = len(messages) + 1
    chunk, width = own.shape
    return pl.pallas_call(
        functools.partial(middle_kernel, levels),
        out_shape=[shape((chunk, width // levels), bf16)] * levels,
        in_specs=[SMEM] + [VMEM] * (levels + 5),
        out_specs=[VMEM] * levels,
        scratch_shapes=[pltpu.VMEM((width, width), bf16), pltpu.VMEM((chunk * levels, 8), f32)],
        compiler_params=params(SMALL),
        cost_estimate=cost(6 * chunk * width * width, 2 * width * width),
    )(where, own, own_extra, *messages, *bases)


def result_kernel(levels, where, *refs):
    slots = refs[:levels]
    one, two, sent, kept, mid, whole, sems = refs[levels:]
    chunk, height = slots[0].shape
    wide, part = one.shape
    copies = []
    for step, slot in enumerate(slots):
        row = pl.multiple_of((where[0] ^ step) * chunk, chunk)
        copy = pltpu.make_async_copy(slot, mid.at[pl.ds(row, chunk)], sems.at[step])
        copy.start()
        copies.append(copy)
    for copy in copies:
        copy.wait()
    quarter = wide // 4
    for j in range(4):
        columns = pl.ds(j * quarter, quarter)
        whole[:, columns] = sum(
            lax.dot_general(
                mid[pl.ds(i * part, part)], b[columns], (((0,), (1,)), ((), ())), preferred_element_type=f32
            )
            for i, b in enumerate((one, two))
        )
    rows = height // 4
    for i, (other, target) in enumerate(((3, sent), (1, sent), (2, kept), (0, kept))):
        block = whole[pl.ds(pl.multiple_of((where[1] ^ other) * rows, rows), rows)]
        target[pl.ds((i % 2) * rows, rows)] = block.astype(target.dtype)


def result(where, slots, bases):
    levels = len(slots)
    chunk, height = slots[0].shape
    wide, part = bases[0].shape
    return pl.pallas_call(
        functools.partial(result_kernel, levels),
        out_shape=(shape((height // 2, wide), f32), shape((height // 2, wide), f32)),
        in_specs=[SMEM] + [ANY] * levels + [VMEM] * 2,
        out_specs=(VMEM, VMEM),
        scratch_shapes=[
            pltpu.VMEM((2 * part, height), bf16),
            pltpu.VMEM((height, wide), f32),
            pltpu.SemaphoreType.DMA((levels,)),
        ],
        compiler_params=params(SMALL),
        cost_estimate=cost(4 * height * part * wide, 4 * wide * part),
    )(where, *slots, *bases)


def gather_levels(unit, level, levels):
    def over(slot):
        return lax.ppermute(slot, "group", SWAP)

    if levels != 4:
        slots = [unit] + [across(unit, step, levels) for step in range(1, levels)]
        return slots, [over(slot) for slot in slots]
    middle = (level == 1) | (level == 2)
    inner, outward = [(1, 2), (2, 1)], [(1, 0), (2, 3)]
    together = lax.optimization_barrier
    first, third, other0 = together((across(unit, 1, levels), lax.ppermute(unit, "level", inner), over(unit)))
    inside, outside, other1 = together(
        (lax.ppermute(first, "level", inner), lax.ppermute(third, "level", outward), over(first))
    )
    second = jnp.where(middle, inside, outside)
    outside, other2 = together((lax.ppermute(inside, "level", outward), over(second)))
    third = jnp.where(middle, third, outside)
    return [unit, first, second, third], [other0, other1, other2, over(third)]


def body(acts, grads, counts, basis_a, basis_g):
    group, level, chip, core = (lax.axis_index(n) for n in ("group", "level", "chip", "core"))
    levels = lax.axis_size("level")
    rows, width_a = acts.shape
    width_g = grads.shape[1]
    rows_a, rows_g = basis_a.shape[0], basis_g.shape[0]
    part_a, part_g = width_a // 4, width_g // 8
    where = jnp.stack([level, chip * 2 + core]).astype(jnp.int32)

    def columns(y, c):
        return jnp.concatenate(
            [
                cut(basis_g, ((y * 2 + c) * 2 + group) * part_g, part_g, 1),
                cut(basis_a, (c * 2 + group) * part_a, part_a, 1),
            ]
        )

    def diagonal(x):
        return lax.ppermute(x, ("chip", "core"), [(i, 3 - i) for i in range(4)])

    beyond = [lax.ppermute(columns(1 - chip, core), "chip", SWAP), diagonal(columns(1 - chip, 1 - core))]
    blocks = jnp.stack([columns(chip, core), lax.ppermute(columns(chip, 1 - core), "core", SWAP)] + beyond)
    blocks = [lax.dynamic_index_in_dim(blocks, j ^ (chip * 2 + core), 0, False) for j in range(4)]
    unit = jnp.concatenate([b[:rows_g] for b in blocks] + [b[rows_g:] for b in blocks])
    level_g, level_a = 4 * rows_g, 4 * rows_a

    slots, others = gather_levels(unit, level, levels)
    valid = counts[0]
    keep = jnp.arange(rows, dtype=jnp.int32)[:, None] < valid
    marks = jnp.stack([valid // 16 * 16, valid % 16]).astype(bf16)
    marks = jnp.broadcast_to(jnp.pad(marks, (0, 14))[:, None], (16, width_a))
    half = split(rows)[0]
    early = jnp.where(keep[:half], grads[:half], 0)
    early = jnp.concatenate([jnp.where(keep, acts, 0), marks, early[:, :width_a], early[:, width_a:]])
    late = jnp.where(keep[half:], grads[half:], 0)
    (early_out, late_out), _ = lax.optimization_barrier(((early, late), beyond))

    def four(mine, out, after):
        far, after = lax.optimization_barrier((lax.ppermute(out, "chip", SWAP), after))
        return [mine, lax.ppermute(mine, "core", SWAP), far, lax.ppermute(far, "core", SWAP)], after

    early, slots[-1] = four(early, early_out, slots[-1])
    first = turn(where, slots, early, rows, level_g, level_a)
    others[-1], first = lax.optimization_barrier((others[-1], first))
    second = turn(where, others, early, rows, level_g, level_a)
    late, second = four(late, late_out, second)
    bases_a, turned_g, bases_g, sums = zip(first, second)
    sums += tuple(lax.ppermute(t, "core", SWAP) for t in sums)
    bases_a += tuple(lax.ppermute(t, "core", SWAP) for t in bases_a)
    own, own_extra, *messages = cross(where, early, turned_g, bases_g, late, sums, rows, levels)

    got = [across(m, step + 1, levels) for step, m in enumerate(messages)]
    mids = middle(where, own, own_extra, got, bases_a)
    mids = [m if step == 0 else across(m, step, levels) for step, m in enumerate(mids)]

    sent, kept = result(where, mids, bases_g)
    sent = lax.ppermute(sent.astype(bf16), "core", SWAP).astype(f32)
    last = lax.ppermute((kept[:rows_a] + sent[:rows_a]).astype(bf16), "chip", SWAP)
    return (kept[rows_a:] + sent[rows_a:] + last.astype(f32)).astype(bf16)


def solution(mesh):
    groups, samples = mesh.shape["groups"], mesh.shape["samples"]
    grid = Mesh(mesh.devices.reshape(groups, samples // 4, 2, 2), ("group", "level", "chip", "core"))
    every = ("group", "level", "chip", "core")
    in_specs = (
        P(every, None),
        P(every, None),
        P(every),
        P(every[1:], None),
        P(every[1:], None),
    )
    return jax.shard_map(body, mesh=grid, in_specs=in_specs, out_specs=P(every, None), check_vma=False)
```

```python
import functools

import jax
import jax.numpy as jnp
from jax import lax
from jax.experimental import pallas as pl
from jax.experimental.pallas import tpu as pltpu
from jax.sharding import Mesh, PartitionSpec as P

damping = 0.01
bf16 = jnp.bfloat16
f32 = jnp.float32
SWAP = [(0, 1), (1, 0)]
ANY = pl.BlockSpec(memory_space=pl.ANY)
VMEM = pl.BlockSpec(memory_space=pltpu.VMEM)
SMEM = pl.BlockSpec(memory_space=pltpu.SMEM)
LARGE = 18 * 2**20
MIDDLE = 16 * 2**20
SMALL = 12 * 2**20


def params(limit):
    return pltpu.CompilerParams(vmem_limit_bytes=limit)


def cost(flops, moved):
    return pl.CostEstimate(flops=flops, bytes_accessed=moved, transcendentals=0)


def shape(dims, dtype):
    return jax.ShapeDtypeStruct(dims, dtype)


def cut(x, first, size, axis=0):
    return lax.dynamic_slice_in_dim(x, first, size, axis)


def across(x, step, levels):
    return lax.ppermute(x, "level", [(i, i ^ step) for i in range(levels)])


def split(rows):
    return rows * 2 // 3, rows - rows * 2 // 3


def turn_kernel(levels, level_g, level_a, rows, where, *refs):
    slots, pieces = refs[:levels], refs[levels : levels + 4]
    basis_a, out_g, basis_g, sums, sems = refs[levels + 4 :]
    half, width = split(rows)[0], basis_a.shape[0]
    part = basis_a.shape[1]
    copies = []
    for i, (first, height, target) in enumerate(((level_g, level_a, basis_a), (0, level_g, basis_g))):
        for step, slot in enumerate(slots):
            row = pl.multiple_of((where[0] ^ step) * height, height)
            copy = pltpu.make_async_copy(
                slot.at[pl.ds(first, height)], target.at[pl.ds(row, height)], sems.at[i * levels + step]
            )
            copy.start()
            copies.append(copy)
    for copy in copies[:levels]:
        copy.wait()
    total_a = jnp.zeros((1, part), f32)
    total_g = jnp.zeros((1, part), f32)
    for piece in pieces:
        block = jnp.dot(piece[:rows], basis_a[...], preferred_element_type=f32).astype(bf16)
        total_a = total_a + jnp.sum(jnp.square(block.astype(f32)), axis=0, keepdims=True)
    for copy in copies[levels:]:
        copy.wait()
    for i, piece in enumerate(pieces):
        turned = sum(
            jnp.dot(
                piece[pl.ds(rows + 16 + j * half, half)],
                basis_g[pl.ds(j * width, width)],
                preferred_element_type=f32,
            )
            for j in range(2)
        ).astype(bf16)
        out_g[pl.ds(i * half, half)] = turned
        total_g = total_g + jnp.sum(jnp.square(turned.astype(f32)), axis=0, keepdims=True)
    marks = sum(piece[rows : rows + 16, :part].astype(f32) for piece in pieces)
    sums[0:1] = total_g
    sums[1:2] = marks[0:1] + marks[1:2]
    sums[2:3] = total_a
    sums[3:8] = jnp.zeros((5, part), f32)


def turn(where, slots, pieces, rows, level_g, level_a):
    levels = len(slots)
    width_a, width_g = levels * level_a, levels * level_g
    part = slots[0].shape[1]
    half = split(rows)[0]
    return pl.pallas_call(
        functools.partial(turn_kernel, levels, level_g, level_a, rows),
        out_shape=(
            shape((width_a, part), bf16),
            shape((4 * half, part), bf16),
            shape((width_g, part), bf16),
            shape((8, part), f32),
        ),
        in_specs=[SMEM] + [ANY] * levels + [VMEM] * 4,
        out_specs=(VMEM,) * 4,
        scratch_shapes=[pltpu.SemaphoreType.DMA((2 * levels,))],
        compiler_params=params(MIDDLE),
        cost_estimate=cost(8 * rows * part * (width_a + width_g // 2), 8 * rows * (width_a + width_g // 2)),
    )(where, *slots, *pieces)


def high_low(v):
    high = v.astype(bf16)
    return high, (v - high.astype(f32)).astype(bf16)


def cross_kernel(levels, rows, where, *refs):
    acts, early, bases, pieces, sums = refs[:4], refs[4:6], refs[6:8], refs[8:12], refs[12:16]
    own, own_extra, messages = refs[16], refs[17], refs[18 : 17 + levels]
    left, right, basis, held, whole, extra, sems = refs[17 + levels :]
    half, late = split(rows)
    part = bases[0].shape[1]
    cols = 2 * part
    chunk = cols // levels
    level = where[0]
    count = 0

    def copy(source, target):
        nonlocal count
        made = pltpu.make_async_copy(source, target, sems.at[count])
        made.start()
        count += 1
        return made

    first = [copy(b, basis.at[:, pl.ds(i * part, part)]) for i, b in enumerate(bases)]
    moves = [copy(p, held.at[pl.ds(i * late, late)]) for i, p in enumerate(pieces)]
    rest = [copy(a.at[pl.ds(0, rows)], left.at[pl.ds(i * rows, rows)]) for i, a in enumerate(acts)]
    for i in range(2):
        for j in range(4):
            rest.append(
                copy(early[i].at[pl.ds(j * half, half)], right.at[pl.ds(j * rows, half), pl.ds(i * part, part)])
            )
    for made in first:
        made.wait()
    total = jnp.concatenate([sums[0][0:1], sums[1][0:1]], axis=1)
    for i in range(0, 4, 2):
        moves[i].wait()
        moves[i + 1].wait()
        block = jnp.dot(held[pl.ds(i * late, 2 * late)], basis[...], preferred_element_type=f32).astype(bf16)
        right[pl.ds(i * rows + half, late)] = block[:late]
        right[pl.ds(i * rows + rows + half, late)] = block[late:]
        total = total + jnp.sum(jnp.square(block.astype(f32)), axis=0, keepdims=True)
    for made in rest:
        made.wait()
    extra[...] = jnp.zeros_like(extra)
    extra[0:1, :cols] = total
    for i in range(4):
        extra[1:2, pl.ds(i * part, part)] = sums[i][2:3]
        extra[2:3, pl.ds(i * part, part)] = sums[i][1:2]
    for i in range(2):
        block = pl.ds(i * part, part)
        whole[block] = lax.dot_general(
            right[:, block], left[...], (((0,), (0,)), ((), ())), preferred_element_type=f32
        )
    high, low = high_low(extra[...])
    own_extra[...] = extra[...]
    own[...] = whole[pl.ds(pl.multiple_of(level * chunk, chunk), chunk)]
    for step in range(1, levels):
        to = pl.multiple_of((level ^ step) * chunk, chunk)
        messages[step - 1][...] = jnp.concatenate([whole[pl.ds(to, chunk)].astype(bf16), high[:4], low[:4]])


def cross(where, acts, early, bases, pieces, sums, rows, levels):
    width_g, part = bases[0].shape
    width = acts[0].shape[1]
    cols = 2 * part
    chunk = cols // levels
    return pl.pallas_call(
        functools.partial(cross_kernel, levels, rows),
        out_shape=[shape((chunk, width), f32), shape((8, width), f32)]
        + [shape((chunk + 8, width), bf16)] * (levels - 1),
        in_specs=[SMEM] + [ANY] * 12 + [VMEM] * 4,
        out_specs=[VMEM] * (1 + levels),
        scratch_shapes=[
            pltpu.VMEM((4 * rows, width), bf16),
            pltpu.VMEM((4 * rows, cols), bf16),
            pltpu.VMEM((width_g, cols), bf16),
            pltpu.VMEM((4 * split(rows)[1], width_g), bf16),
            pltpu.VMEM((cols, width), f32),
            pltpu.VMEM((8, width), f32),
            pltpu.SemaphoreType.DMA((18,)),
        ],
        compiler_params=params(LARGE),
        cost_estimate=cost(4 * rows * cols * (width_g + 2 * width), 16 * rows * width),
    )(where, *acts, *early, *bases, *pieces, *sums)


def far_kernel(levels, rows, where, *refs):
    acts, early, bases, pieces, sums = refs[:4], refs[4:6], refs[6:8], refs[8:12], refs[12:16]
    message, kept, extra, right, left, basis, held, sems = refs[16:]
    half, late = split(rows)
    part = bases[0].shape[1]
    cols = 2 * part
    chunk = cols // levels
    level = where[0]
    count = 0

    def copy(source, target):
        nonlocal count
        made = pltpu.make_async_copy(source, target, sems.at[count])
        made.start()
        count += 1
        return made

    first = [copy(b, basis.at[:, pl.ds(i * part, part)]) for i, b in enumerate(bases)]
    moves = [copy(p, held.at[pl.ds(i * late, late)]) for i, p in enumerate(pieces)]
    rest = [copy(a.at[pl.ds(0, rows)], left.at[pl.ds(i * rows, rows)]) for i, a in enumerate(acts)]
    for i in range(2):
        for j in range(4):
            rest.append(
                copy(early[i].at[pl.ds(j * half, half)], right.at[pl.ds(j * rows, half), pl.ds(i * part, part)])
            )
    for made in first:
        made.wait()
    total = jnp.concatenate([sums[0][0:1], sums[1][0:1]], axis=1)
    for i in range(0, 4, 2):
        moves[i].wait()
        moves[i + 1].wait()
        block = jnp.dot(held[pl.ds(i * late, 2 * late)], basis[...], preferred_element_type=f32).astype(bf16)
        right[pl.ds(i * rows + half, late)] = block[:late]
        right[pl.ds(i * rows + rows + half, late)] = block[late:]
        total = total + jnp.sum(jnp.square(block.astype(f32)), axis=0, keepdims=True)
    for made in rest:
        made.wait()
    extra[...] = jnp.zeros_like(extra)
    extra[0:1, :cols] = total
    for i in range(4):
        extra[1:2, pl.ds(i * part, part)] = sums[i][2:3]
        extra[2:3, pl.ds(i * part, part)] = sums[i][1:2]
    high, low = high_low(extra[...])
    side, place = level // 2, level % 2
    for other, target in ((place, None), (1 - place, kept)):
        columns = pl.ds(pl.multiple_of(((1 - side) * 2 + other) * chunk, chunk), chunk)
        block = lax.dot_general(
            right[:, columns], left[...], (((0,), (0,)), ((), ())), preferred_element_type=f32
        )
        if target is None:
            message[...] = jnp.concatenate([block.astype(bf16), high[:4], low[:4]])
        else:
            target[...] = block


def far(where, acts, early, bases, pieces, sums, rows, levels):
    width_g, part = bases[0].shape
    width = acts[0].shape[1]
    cols = 2 * part
    chunk = cols // levels
    return pl.pallas_call(
        functools.partial(far_kernel, levels, rows),
        out_shape=(
            shape((chunk + 8, width), bf16),
            shape((chunk, width), f32),
            shape((8, width), f32),
            shape((4 * rows, cols), bf16),
        ),
        in_specs=[SMEM] + [ANY] * 12 + [VMEM] * 4,
        out_specs=(VMEM,) * 4,
        scratch_shapes=[
            pltpu.VMEM((4 * rows, width), bf16),
            pltpu.VMEM((width_g, cols), bf16),
            pltpu.VMEM((4 * split(rows)[1], width_g), bf16),
            pltpu.SemaphoreType.DMA((18,)),
        ],
        compiler_params=params(LARGE),
        cost_estimate=cost(4 * rows * cols * (width_g + width), 16 * rows * width),
    )(where, *acts, *early, *bases, *pieces, *sums)


def near_kernel(levels, rows, where, right, extra, *refs):
    acts, own, message = refs[:4], refs[4], refs[5]
    chunk = right.shape[1] // levels
    high, low = high_low(extra[...])
    for step, target in enumerate((own, message)):
        columns = pl.ds(pl.multiple_of((where[0] ^ step) * chunk, chunk), chunk)
        block = sum(
            lax.dot_general(
                right[pl.ds(i * rows, rows), columns], a[:rows], (((0,), (0,)), ((), ())), preferred_element_type=f32
            )
            for i, a in enumerate(acts)
        )
        if step == 0:
            target[...] = block
        else:
            target[...] = jnp.concatenate([block.astype(bf16), high[:4], low[:4]])


def near(where, right, extra, acts, rows, levels):
    width = acts[0].shape[1]
    chunk = right.shape[1] // levels
    return pl.pallas_call(
        functools.partial(near_kernel, levels, rows),
        out_shape=(shape((chunk, width), f32), shape((chunk + 8, width), bf16)),
        in_specs=[SMEM] + [VMEM] * 6,
        out_specs=(VMEM, VMEM),
        compiler_params=params(LARGE),
        cost_estimate=cost(16 * rows * chunk * width, 16 * rows * width),
    )(where, right, extra, *acts)


def add_kernel(kept, extra, got, out):
    chunk = kept.shape[0]
    more = got[...].astype(f32)
    high, low = high_low(extra[0:4] + (more[chunk : chunk + 4] + more[chunk + 4 :]))
    out[...] = jnp.concatenate([(kept[...] + more[:chunk]).astype(bf16), high, low])


def add(kept, extra, got):
    return pl.pallas_call(
        add_kernel,
        out_shape=shape(got.shape, bf16),
        in_specs=[VMEM] * 3,
        out_specs=VMEM,
        compiler_params=params(SMALL),
        cost_estimate=cost(kept.size, 8 * kept.size),
    )(kept, extra, got)


def middle_kernel(levels, where, own, own_extra, *refs):
    count = len(refs) - levels - 6
    messages, bases, outs = refs[:count], refs[count : count + 4], refs[count + 4 : -2]
    basis, turned = refs[-2:]
    chunk, width = own.shape
    cols = chunk * levels
    part = bases[0].shape[1]
    for i, b in enumerate(bases):
        basis[:, pl.ds(i * part, part)] = b[...]
    total = own[...]
    extra = own_extra[...]
    for message in messages:
        part_sum = message[...].astype(f32)
        total = total + part_sum[:chunk]
        more = part_sum[chunk:]
        extra = extra + jnp.concatenate([more[0:4] + more[4:8], jnp.zeros_like(more[:4])])
    count = extra[2:3]
    extra = extra / count
    lam_a = extra[1:2]
    turned[...] = jnp.transpose(extra[:, :cols])
    lam_g = turned[pl.ds(pl.multiple_of(where[0] * chunk, chunk), chunk)][:, 0:1]
    both = jnp.dot(jnp.concatenate(high_low(total)), basis[...], preferred_element_type=f32)
    rotated = (both[:chunk] + both[chunk:]) / count
    scaled = (rotated / (lam_g * lam_a + damping)).astype(bf16)
    height = width // levels
    for step, out in enumerate(outs):
        rows = pl.ds(pl.multiple_of((where[0] ^ step) * height, height), height)
        out[...] = lax.dot_general(
            scaled, basis[rows], (((1,), (1,)), ((), ())), preferred_element_type=f32
        ).astype(bf16)


def middle(where, own, own_extra, messages, bases, levels):
    chunk, width = own.shape
    return pl.pallas_call(
        functools.partial(middle_kernel, levels),
        out_shape=[shape((chunk, width // levels), bf16)] * levels,
        in_specs=[SMEM] + [VMEM] * (len(messages) + 6),
        out_specs=[VMEM] * levels,
        scratch_shapes=[pltpu.VMEM((width, width), bf16), pltpu.VMEM((chunk * levels, 8), f32)],
        compiler_params=params(SMALL),
        cost_estimate=cost(6 * chunk * width * width, 2 * width * width),
    )(where, own, own_extra, *messages, *bases)


def result_kernel(levels, where, *refs):
    slots = refs[:levels]
    one, two, sent, kept, mid, whole, sems = refs[levels:]
    chunk, height = slots[0].shape
    wide, part = one.shape
    copies = []
    for step, slot in enumerate(slots):
        row = pl.multiple_of((where[0] ^ step) * chunk, chunk)
        copy = pltpu.make_async_copy(slot, mid.at[pl.ds(row, chunk)], sems.at[step])
        copy.start()
        copies.append(copy)
    for copy in copies:
        copy.wait()
    quarter = wide // 4
    for j in range(4):
        columns = pl.ds(j * quarter, quarter)
        whole[:, columns] = sum(
            lax.dot_general(
                mid[pl.ds(i * part, part)], b[columns], (((0,), (1,)), ((), ())), preferred_element_type=f32
            )
            for i, b in enumerate((one, two))
        )
    rows = height // 4
    for i, (other, target) in enumerate(((3, sent), (1, sent), (2, kept), (0, kept))):
        block = whole[pl.ds(pl.multiple_of((where[1] ^ other) * rows, rows), rows)]
        target[pl.ds((i % 2) * rows, rows)] = block.astype(target.dtype)


def result(where, slots, bases):
    levels = len(slots)
    chunk, height = slots[0].shape
    wide, part = bases[0].shape
    return pl.pallas_call(
        functools.partial(result_kernel, levels),
        out_shape=(shape((height // 2, wide), f32), shape((height // 2, wide), f32)),
        in_specs=[SMEM] + [ANY] * levels + [VMEM] * 2,
        out_specs=(VMEM, VMEM),
        scratch_shapes=[
            pltpu.VMEM((2 * part, height), bf16),
            pltpu.VMEM((height, wide), f32),
            pltpu.SemaphoreType.DMA((levels,)),
        ],
        compiler_params=params(SMALL),
        cost_estimate=cost(4 * height * part * wide, 4 * wide * part),
    )(where, *slots, *bases)


def gather_levels(unit, level, levels):
    def over(slot):
        return lax.ppermute(slot, "group", SWAP)

    if levels != 4:
        slots = [unit] + [across(unit, step, levels) for step in range(1, levels)]
        return slots, [over(slot) for slot in slots]
    middle = (level == 1) | (level == 2)
    inner, outward = [(1, 2), (2, 1)], [(1, 0), (2, 3)]
    together = lax.optimization_barrier
    first, third, other0 = together((across(unit, 1, levels), lax.ppermute(unit, "level", inner), over(unit)))
    inside, outside, other1 = together(
        (lax.ppermute(first, "level", inner), lax.ppermute(third, "level", outward), over(first))
    )
    second = jnp.where(middle, inside, outside)
    outside, other2 = together((lax.ppermute(inside, "level", outward), over(second)))
    third = jnp.where(middle, third, outside)
    return [unit, first, second, third], [other0, other1, other2, over(third)]


def body(acts, grads, counts, basis_a, basis_g):
    group, level, chip, core = (lax.axis_index(n) for n in ("group", "level", "chip", "core"))
    levels = lax.axis_size("level")
    rows, width_a = acts.shape
    width_g = grads.shape[1]
    rows_a, rows_g = basis_a.shape[0], basis_g.shape[0]
    part_a, part_g = width_a // 4, width_g // 8
    where = jnp.stack([level, chip * 2 + core]).astype(jnp.int32)

    def columns(y, c):
        return jnp.concatenate(
            [
                cut(basis_g, ((y * 2 + c) * 2 + group) * part_g, part_g, 1),
                cut(basis_a, (c * 2 + group) * part_a, part_a, 1),
            ]
        )

    def diagonal(x):
        return lax.ppermute(x, ("chip", "core"), [(i, 3 - i) for i in range(4)])

    beyond = [lax.ppermute(columns(1 - chip, core), "chip", SWAP), diagonal(columns(1 - chip, 1 - core))]
    blocks = jnp.stack([columns(chip, core), lax.ppermute(columns(chip, 1 - core), "core", SWAP)] + beyond)
    blocks = [lax.dynamic_index_in_dim(blocks, j ^ (chip * 2 + core), 0, False) for j in range(4)]
    unit = jnp.concatenate([b[:rows_g] for b in blocks] + [b[rows_g:] for b in blocks])
    level_g, level_a = 4 * rows_g, 4 * rows_a

    slots, others = gather_levels(unit, level, levels)
    valid = counts[0]
    keep = jnp.arange(rows, dtype=jnp.int32)[:, None] < valid
    marks = jnp.stack([valid // 16 * 16, valid % 16]).astype(bf16)
    marks = jnp.broadcast_to(jnp.pad(marks, (0, 14))[:, None], (16, width_a))
    half = split(rows)[0]
    early = jnp.where(keep[:half], grads[:half], 0)
    early = jnp.concatenate([jnp.where(keep, acts, 0), marks, early[:, :width_a], early[:, width_a:]])
    late = jnp.where(keep[half:], grads[half:], 0)
    (early_out, late_out), _ = lax.optimization_barrier(((early, late), beyond))

    def four(mine, out, after):
        far, after = lax.optimization_barrier((lax.ppermute(out, "chip", SWAP), after))
        return [mine, lax.ppermute(mine, "core", SWAP), far, lax.ppermute(far, "core", SWAP)], after

    early, slots[-1] = four(early, early_out, slots[-1])
    first = turn(where, slots, early, rows, level_g, level_a)
    others[-1], first = lax.optimization_barrier((others[-1], first))
    second = turn(where, others, early, rows, level_g, level_a)
    late, second = four(late, late_out, second)
    bases_a, turned_g, bases_g, sums = zip(first, second)
    sums += tuple(lax.ppermute(t, "core", SWAP) for t in sums)
    bases_a += tuple(lax.ppermute(t, "core", SWAP) for t in bases_a)
    if levels == 4:
        message, kept, own_extra, right = far(where, early, turned_g, bases_g, late, sums, rows, levels)
        message = across(message, 1, levels)
        own, beside = near(where, right, own_extra, early, rows, levels)
        got = [across(add(kept, own_extra, message), 3, levels), across(beside, 1, levels)]
    else:
        own, own_extra, *messages = cross(where, early, turned_g, bases_g, late, sums, rows, levels)
        got = [across(m, step + 1, levels) for step, m in enumerate(messages)]
    mids = middle(where, own, own_extra, got, bases_a, levels)
    mids = [m if step == 0 else across(m, step, levels) for step, m in enumerate(mids)]

    sent, kept = result(where, mids, bases_g)
    sent = lax.ppermute(sent.astype(bf16), "core", SWAP).astype(f32)
    last = lax.ppermute((kept[:rows_a] + sent[:rows_a]).astype(bf16), "chip", SWAP)
    return (kept[rows_a:] + sent[rows_a:] + last.astype(f32)).astype(bf16)


def solution(mesh):
    groups, samples = mesh.shape["groups"], mesh.shape["samples"]
    grid = Mesh(mesh.devices.reshape(groups, samples // 4, 2, 2), ("group", "level", "chip", "core"))
    every = ("group", "level", "chip", "core")
    in_specs = (
        P(every, None),
        P(every, None),
        P(every),
        P(every[1:], None),
        P(every[1:], None),
    )
    return jax.shard_map(body, mesh=grid, in_specs=in_specs, out_specs=P(every, None), check_vma=False)
```

```python
import functools

import jax
import jax.numpy as jnp
from jax import lax
from jax.experimental import pallas as pl
from jax.experimental.pallas import tpu as pltpu
from jax.sharding import Mesh, PartitionSpec as P

damping = 0.01
bf16 = jnp.bfloat16
f32 = jnp.float32
SWAP = [(0, 1), (1, 0)]
ANY = pl.BlockSpec(memory_space=pl.ANY)
VMEM = pl.BlockSpec(memory_space=pltpu.VMEM)
SMEM = pl.BlockSpec(memory_space=pltpu.SMEM)
LARGE = 18 * 2**20
MIDDLE = 16 * 2**20
SMALL = 12 * 2**20


def params(limit):
    return pltpu.CompilerParams(vmem_limit_bytes=limit)


def cost(flops, moved):
    return pl.CostEstimate(flops=flops, bytes_accessed=moved, transcendentals=0)


def shape(dims, dtype):
    return jax.ShapeDtypeStruct(dims, dtype)


def cut(x, first, size, axis=0):
    return lax.dynamic_slice_in_dim(x, first, size, axis)


def across(x, step, levels):
    return lax.ppermute(x, "level", [(i, i ^ step) for i in range(levels)])


def split(rows):
    return rows * 2 // 3, rows - rows * 2 // 3


def turn_kernel(levels, level_g, level_a, rows, where, *refs):
    slots, pieces = refs[:levels], refs[levels : levels + 4]
    basis_a, out_g, basis_g, sums, sems = refs[levels + 4 :]
    half, width = split(rows)[0], basis_a.shape[0]
    part = basis_a.shape[1]
    copies = []
    for i, (first, height, target) in enumerate(((level_g, level_a, basis_a), (0, level_g, basis_g))):
        for step, slot in enumerate(slots):
            row = pl.multiple_of((where[0] ^ step) * height, height)
            copy = pltpu.make_async_copy(
                slot.at[pl.ds(first, height)], target.at[pl.ds(row, height)], sems.at[i * levels + step]
            )
            copy.start()
            copies.append(copy)
    for copy in copies[:levels]:
        copy.wait()
    total_a = jnp.zeros((1, part), f32)
    total_g = jnp.zeros((1, part), f32)
    for piece in pieces:
        block = jnp.dot(piece[:rows], basis_a[...], preferred_element_type=f32).astype(bf16)
        total_a = total_a + jnp.sum(jnp.square(block.astype(f32)), axis=0, keepdims=True)
    for copy in copies[levels:]:
        copy.wait()
    for i, piece in enumerate(pieces):
        turned = sum(
            jnp.dot(
                piece[pl.ds(rows + 16 + j * half, half)],
                basis_g[pl.ds(j * width, width)],
                preferred_element_type=f32,
            )
            for j in range(2)
        ).astype(bf16)
        out_g[pl.ds(i * half, half)] = turned
        total_g = total_g + jnp.sum(jnp.square(turned.astype(f32)), axis=0, keepdims=True)
    marks = sum(piece[rows : rows + 16, :part].astype(f32) for piece in pieces)
    sums[0:1] = total_g
    sums[1:2] = marks[0:1] + marks[1:2]
    sums[2:3] = total_a
    sums[3:8] = jnp.zeros((5, part), f32)


def turn(where, slots, pieces, rows, level_g, level_a):
    levels = len(slots)
    width_a, width_g = levels * level_a, levels * level_g
    part = slots[0].shape[1]
    half = split(rows)[0]
    return pl.pallas_call(
        functools.partial(turn_kernel, levels, level_g, level_a, rows),
        out_shape=(
            shape((width_a, part), bf16),
            shape((4 * half, part), bf16),
            shape((width_g, part), bf16),
            shape((8, part), f32),
        ),
        in_specs=[SMEM] + [ANY] * levels + [VMEM] * 4,
        out_specs=(VMEM,) * 4,
        scratch_shapes=[pltpu.SemaphoreType.DMA((2 * levels,))],
        compiler_params=params(MIDDLE),
        cost_estimate=cost(8 * rows * part * (width_a + width_g // 2), 8 * rows * (width_a + width_g // 2)),
    )(where, *slots, *pieces)


def high_low(v):
    high = v.astype(bf16)
    return high, (v - high.astype(f32)).astype(bf16)


def cross_kernel(levels, rows, where, *refs):
    acts, early, bases, pieces, sums = refs[:4], refs[4:6], refs[6:8], refs[8:12], refs[12:16]
    own, own_extra, messages = refs[16], refs[17], refs[18 : 17 + levels]
    left, right, basis, held, whole, extra, sems = refs[17 + levels :]
    half, late = split(rows)
    part = bases[0].shape[1]
    cols = 2 * part
    chunk = cols // levels
    level = where[0]
    count = 0

    def copy(source, target):
        nonlocal count
        made = pltpu.make_async_copy(source, target, sems.at[count])
        made.start()
        count += 1
        return made

    first = [copy(b, basis.at[:, pl.ds(i * part, part)]) for i, b in enumerate(bases)]
    moves = [copy(p, held.at[pl.ds(i * late, late)]) for i, p in enumerate(pieces)]
    rest = [copy(a.at[pl.ds(0, rows)], left.at[pl.ds(i * rows, rows)]) for i, a in enumerate(acts)]
    for i in range(2):
        for j in range(4):
            rest.append(
                copy(early[i].at[pl.ds(j * half, half)], right.at[pl.ds(j * rows, half), pl.ds(i * part, part)])
            )
    for made in first:
        made.wait()
    total = jnp.concatenate([sums[0][0:1], sums[1][0:1]], axis=1)
    for i in range(0, 4, 2):
        moves[i].wait()
        moves[i + 1].wait()
        block = jnp.dot(held[pl.ds(i * late, 2 * late)], basis[...], preferred_element_type=f32).astype(bf16)
        right[pl.ds(i * rows + half, late)] = block[:late]
        right[pl.ds(i * rows + rows + half, late)] = block[late:]
        total = total + jnp.sum(jnp.square(block.astype(f32)), axis=0, keepdims=True)
    for made in rest:
        made.wait()
    extra[...] = jnp.zeros_like(extra)
    extra[0:1, :cols] = total
    for i in range(4):
        extra[1:2, pl.ds(i * part, part)] = sums[i][2:3]
        extra[2:3, pl.ds(i * part, part)] = sums[i][1:2]
    for i in range(2):
        block = pl.ds(i * part, part)
        whole[block] = lax.dot_general(
            right[:, block], left[...], (((0,), (0,)), ((), ())), preferred_element_type=f32
        )
    high, low = high_low(extra[...])
    own_extra[...] = extra[...]
    own[...] = whole[pl.ds(pl.multiple_of(level * chunk, chunk), chunk)]
    for step in range(1, levels):
        to = pl.multiple_of((level ^ step) * chunk, chunk)
        messages[step - 1][...] = jnp.concatenate([whole[pl.ds(to, chunk)].astype(bf16), high[:4], low[:4]])


def cross(where, acts, early, bases, pieces, sums, rows, levels):
    width_g, part = bases[0].shape
    width = acts[0].shape[1]
    cols = 2 * part
    chunk = cols // levels
    return pl.pallas_call(
        functools.partial(cross_kernel, levels, rows),
        out_shape=[shape((chunk, width), f32), shape((8, width), f32)]
        + [shape((chunk + 8, width), bf16)] * (levels - 1),
        in_specs=[SMEM] + [ANY] * 12 + [VMEM] * 4,
        out_specs=[VMEM] * (1 + levels),
        scratch_shapes=[
            pltpu.VMEM((4 * rows, width), bf16),
            pltpu.VMEM((4 * rows, cols), bf16),
            pltpu.VMEM((width_g, cols), bf16),
            pltpu.VMEM((4 * split(rows)[1], width_g), bf16),
            pltpu.VMEM((cols, width), f32),
            pltpu.VMEM((8, width), f32),
            pltpu.SemaphoreType.DMA((18,)),
        ],
        compiler_params=params(LARGE),
        cost_estimate=cost(4 * rows * cols * (width_g + 2 * width), 16 * rows * width),
    )(where, *acts, *early, *bases, *pieces, *sums)


def far_kernel(levels, rows, where, *refs):
    acts, early, bases, pieces, sums = refs[:4], refs[4:6], refs[6:8], refs[8:12], refs[12:16]
    message, kept, extra, right, left, basis, held, sems = refs[16:]
    half, late = split(rows)
    part = bases[0].shape[1]
    cols = 2 * part
    chunk = cols // levels
    level = where[0]
    count = 0

    def copy(source, target):
        nonlocal count
        made = pltpu.make_async_copy(source, target, sems.at[count])
        made.start()
        count += 1
        return made

    first = [copy(b, basis.at[:, pl.ds(i * part, part)]) for i, b in enumerate(bases)]
    moves = [copy(p, held.at[pl.ds(i * late, late)]) for i, p in enumerate(pieces)]
    rest = [copy(a.at[pl.ds(0, rows)], left.at[pl.ds(i * rows, rows)]) for i, a in enumerate(acts)]
    for i in range(2):
        for j in range(4):
            rest.append(
                copy(early[i].at[pl.ds(j * half, half)], right.at[pl.ds(j * rows, half), pl.ds(i * part, part)])
            )
    for made in first:
        made.wait()
    total = jnp.concatenate([sums[0][0:1], sums[1][0:1]], axis=1)
    for i in range(0, 4, 2):
        moves[i].wait()
        moves[i + 1].wait()
        block = jnp.dot(held[pl.ds(i * late, 2 * late)], basis[...], preferred_element_type=f32).astype(bf16)
        right[pl.ds(i * rows + half, late)] = block[:late]
        right[pl.ds(i * rows + rows + half, late)] = block[late:]
        total = total + jnp.sum(jnp.square(block.astype(f32)), axis=0, keepdims=True)
    for made in rest:
        made.wait()
    extra[...] = jnp.zeros_like(extra)
    extra[0:1, :cols] = total
    for i in range(4):
        extra[1:2, pl.ds(i * part, part)] = sums[i][2:3]
        extra[2:3, pl.ds(i * part, part)] = sums[i][1:2]
    high, low = high_low(extra[...])
    side, place = level // 2, level % 2
    for other, target in ((place, None), (1 - place, kept)):
        columns = pl.ds(pl.multiple_of(((1 - side) * 2 + other) * chunk, chunk), chunk)
        block = lax.dot_general(
            right[:, columns], left[...], (((0,), (0,)), ((), ())), preferred_element_type=f32
        )
        if target is None:
            message[...] = jnp.concatenate([block.astype(bf16), high[:4], low[:4]])
        else:
            target[...] = block


def far(where, acts, early, bases, pieces, sums, rows, levels):
    width_g, part = bases[0].shape
    width = acts[0].shape[1]
    cols = 2 * part
    chunk = cols // levels
    return pl.pallas_call(
        functools.partial(far_kernel, levels, rows),
        out_shape=(
            shape((chunk + 8, width), bf16),
            shape((chunk, width), f32),
            shape((8, width), f32),
            shape((4 * rows, cols), bf16),
        ),
        in_specs=[SMEM] + [ANY] * 12 + [VMEM] * 4,
        out_specs=(VMEM,) * 4,
        scratch_shapes=[
            pltpu.VMEM((4 * rows, width), bf16),
            pltpu.VMEM((width_g, cols), bf16),
            pltpu.VMEM((4 * split(rows)[1], width_g), bf16),
            pltpu.SemaphoreType.DMA((18,)),
        ],
        compiler_params=params(LARGE),
        cost_estimate=cost(4 * rows * cols * (width_g + width), 16 * rows * width),
    )(where, *acts, *early, *bases, *pieces, *sums)


def near_kernel(levels, rows, where, right, extra, *refs):
    acts, own, message = refs[:4], refs[4], refs[5]
    chunk = right.shape[1] // levels
    high, low = high_low(extra[...])
    for step, target in enumerate((own, message)):
        columns = pl.ds(pl.multiple_of((where[0] ^ step) * chunk, chunk), chunk)
        block = sum(
            lax.dot_general(
                right[pl.ds(i * rows, rows), columns], a[:rows], (((0,), (0,)), ((), ())), preferred_element_type=f32
            )
            for i, a in enumerate(acts)
        )
        if step == 0:
            target[...] = block
        else:
            target[...] = jnp.concatenate([block.astype(bf16), high[:4], low[:4]])


def near(where, right, extra, acts, rows, levels):
    width = acts[0].shape[1]
    chunk = right.shape[1] // levels
    return pl.pallas_call(
        functools.partial(near_kernel, levels, rows),
        out_shape=(shape((chunk, width), f32), shape((chunk + 8, width), bf16)),
        in_specs=[SMEM] + [VMEM] * 6,
        out_specs=(VMEM, VMEM),
        compiler_params=params(LARGE),
        cost_estimate=cost(16 * rows * chunk * width, 16 * rows * width),
    )(where, right, extra, *acts)


def add_kernel(kept, extra, got, out):
    chunk = kept.shape[0]
    more = got[...].astype(f32)
    high, low = high_low(extra[0:4] + (more[chunk : chunk + 4] + more[chunk + 4 :]))
    out[...] = jnp.concatenate([(kept[...] + more[:chunk]).astype(bf16), high, low])


def add(kept, extra, got):
    return pl.pallas_call(
        add_kernel,
        out_shape=shape(got.shape, bf16),
        in_specs=[VMEM] * 3,
        out_specs=VMEM,
        compiler_params=params(SMALL),
        cost_estimate=cost(kept.size, 8 * kept.size),
    )(kept, extra, got)


def middle_kernel(levels, where, own, own_extra, *refs):
    count = len(refs) - levels - 6
    messages, bases, outs = refs[:count], refs[count : count + 4], refs[count + 4 : -2]
    basis, turned = refs[-2:]
    chunk, width = own.shape
    cols = chunk * levels
    part = bases[0].shape[1]
    for i, b in enumerate(bases):
        basis[:, pl.ds(i * part, part)] = b[...]
    total = own[...]
    extra = own_extra[...]
    for message in messages:
        part_sum = message[...].astype(f32)
        total = total + part_sum[:chunk]
        more = part_sum[chunk:]
        extra = extra + jnp.concatenate([more[0:4] + more[4:8], jnp.zeros_like(more[:4])])
    count = extra[2:3]
    extra = extra / count
    lam_a = extra[1:2]
    turned[...] = jnp.transpose(extra[:, :cols])
    lam_g = turned[pl.ds(pl.multiple_of(where[0] * chunk, chunk), chunk)][:, 0:1]
    both = jnp.dot(jnp.concatenate(high_low(total)), basis[...], preferred_element_type=f32)
    rotated = (both[:chunk] + both[chunk:]) / count
    scaled = (rotated / (lam_g * lam_a + damping)).astype(bf16)
    height = width // levels
    for step, out in enumerate(outs):
        rows = pl.ds(pl.multiple_of((where[0] ^ step) * height, height), height)
        out[...] = lax.dot_general(
            scaled, basis[rows], (((1,), (1,)), ((), ())), preferred_element_type=f32
        ).astype(bf16)


def middle(where, own, own_extra, messages, bases, levels):
    chunk, width = own.shape
    return pl.pallas_call(
        functools.partial(middle_kernel, levels),
        out_shape=[shape((chunk, width // levels), bf16)] * levels,
        in_specs=[SMEM] + [VMEM] * (len(messages) + 6),
        out_specs=[VMEM] * levels,
        scratch_shapes=[pltpu.VMEM((width, width), bf16), pltpu.VMEM((chunk * levels, 8), f32)],
        compiler_params=params(SMALL),
        cost_estimate=cost(6 * chunk * width * width, 2 * width * width),
    )(where, own, own_extra, *messages, *bases)


def result_kernel(levels, where, *refs):
    slots = refs[:levels]
    one, two, sent, kept, mid, whole, sems = refs[levels:]
    chunk, height = slots[0].shape
    wide, part = one.shape
    copies = []
    for step, slot in enumerate(slots):
        row = pl.multiple_of((where[0] ^ step) * chunk, chunk)
        copy = pltpu.make_async_copy(slot, mid.at[pl.ds(row, chunk)], sems.at[step])
        copy.start()
        copies.append(copy)
    for copy in copies:
        copy.wait()
    quarter = wide // 4
    for j in range(4):
        columns = pl.ds(j * quarter, quarter)
        whole[:, columns] = sum(
            lax.dot_general(
                mid[pl.ds(i * part, part)], b[columns], (((0,), (1,)), ((), ())), preferred_element_type=f32
            )
            for i, b in enumerate((one, two))
        )
    rows = height // 4
    for i, (other, target) in enumerate(((3, sent), (1, sent), (2, kept), (0, kept))):
        block = whole[pl.ds(pl.multiple_of((where[1] ^ other) * rows, rows), rows)]
        target[pl.ds((i % 2) * rows, rows)] = block.astype(target.dtype)


def result(where, slots, bases):
    levels = len(slots)
    chunk, height = slots[0].shape
    wide, part = bases[0].shape
    return pl.pallas_call(
        functools.partial(result_kernel, levels),
        out_shape=(shape((height // 2, wide), f32), shape((height // 2, wide), f32)),
        in_specs=[SMEM] + [ANY] * levels + [VMEM] * 2,
        out_specs=(VMEM, VMEM),
        scratch_shapes=[
            pltpu.VMEM((2 * part, height), bf16),
            pltpu.VMEM((height, wide), f32),
            pltpu.SemaphoreType.DMA((levels,)),
        ],
        compiler_params=params(SMALL),
        cost_estimate=cost(4 * height * part * wide, 4 * wide * part),
    )(where, *slots, *bases)


def gather_levels(unit, level, levels, ready):
    def over(slot):
        return lax.ppermute(slot, "group", SWAP)

    if levels != 4:
        slots = [unit] + [across(unit, step, levels) for step in range(1, levels)]
        return slots, [over(slot) for slot in slots], ready
    middle = (level == 1) | (level == 2)
    together = lax.optimization_barrier
    inner = lax.ppermute(unit, "level", [(1, 2), (2, 1)])
    first, inner, other0, ready = together((across(unit, 1, levels), inner, over(unit), ready))
    held, inner = together((unit, inner))
    outer, other1 = together((lax.ppermute(held, "level", [(0, 3), (3, 0)]), over(first)))
    third = jnp.where(middle, inner, outer)
    second, other3 = together((across(third, 1, levels), over(third)))
    return [unit, first, second, third], [other0, other1, over(second), other3], ready


def body(acts, grads, counts, basis_a, basis_g):
    group, level, chip, core = (lax.axis_index(n) for n in ("group", "level", "chip", "core"))
    levels = lax.axis_size("level")
    rows, width_a = acts.shape
    width_g = grads.shape[1]
    rows_a, rows_g = basis_a.shape[0], basis_g.shape[0]
    part_a, part_g = width_a // 4, width_g // 8
    where = jnp.stack([level, chip * 2 + core]).astype(jnp.int32)

    def columns(y, c):
        return jnp.concatenate(
            [
                cut(basis_g, ((y * 2 + c) * 2 + group) * part_g, part_g, 1),
                cut(basis_a, (c * 2 + group) * part_a, part_a, 1),
            ]
        )

    def diagonal(x):
        return lax.ppermute(x, ("chip", "core"), [(i, 3 - i) for i in range(4)])

    beyond = [lax.ppermute(columns(1 - chip, core), "chip", SWAP), diagonal(columns(1 - chip, 1 - core))]
    beside = lax.ppermute(columns(chip, 1 - core), "core", SWAP)
    blocks = jnp.stack([columns(chip, core), beside] + beyond)
    blocks = [lax.dynamic_index_in_dim(blocks, j ^ (chip * 2 + core), 0, False) for j in range(4)]
    unit = jnp.concatenate([b[:rows_g] for b in blocks] + [b[rows_g:] for b in blocks])
    level_g, level_a = 4 * rows_g, 4 * rows_a

    valid = counts[0]
    keep = jnp.arange(rows, dtype=jnp.int32)[:, None] < valid
    half = split(rows)[0]
    later, _ = lax.optimization_barrier((grads, unit))
    slots, others, late = gather_levels(unit, level, levels, jnp.where(keep[half:], later[half:], 0))
    marks = jnp.stack([valid // 16 * 16, valid % 16]).astype(bf16)
    marks = jnp.broadcast_to(jnp.pad(marks, (0, 14))[:, None], (16, width_a))
    early = jnp.where(keep[:half], grads[:half], 0)
    early = jnp.concatenate([jnp.where(keep, acts, 0), marks, early[:, :width_a], early[:, width_a:]])
    early_out, _ = lax.optimization_barrier((early, beyond[0]))

    def four(mine, out, after):
        far, after = lax.optimization_barrier((lax.ppermute(out, "chip", SWAP), after))
        return [mine, lax.ppermute(mine, "core", SWAP), far, lax.ppermute(far, "core", SWAP)], after

    early, slots[2] = four(early, early_out, slots[2])
    first = turn(where, slots, early, rows, level_g, level_a)
    others[2], first = lax.optimization_barrier((others[2], first))
    second = turn(where, others, early, rows, level_g, level_a)
    late, second = four(late, late, second)
    bases_a, turned_g, bases_g, sums = zip(first, second)
    sums += tuple(lax.ppermute(t, "core", SWAP) for t in sums)
    bases_a += tuple(lax.ppermute(t, "core", SWAP) for t in bases_a)
    if levels == 4:
        message, kept, own_extra, right = far(where, early, turned_g, bases_g, late, sums, rows, levels)
        message = across(message, 1, levels)
        own, beside = near(where, right, own_extra, early, rows, levels)
        got = [across(add(kept, own_extra, message), 3, levels), across(beside, 1, levels)]
    else:
        own, own_extra, *messages = cross(where, early, turned_g, bases_g, late, sums, rows, levels)
        got = [across(m, step + 1, levels) for step, m in enumerate(messages)]
    mids = middle(where, own, own_extra, got, bases_a, levels)
    mids = [m if step == 0 else across(m, step, levels) for step, m in enumerate(mids)]

    sent, kept = result(where, mids, bases_g)
    sent = lax.ppermute(sent.astype(bf16), "core", SWAP).astype(f32)
    last = lax.ppermute((kept[:rows_a] + sent[:rows_a]).astype(bf16), "chip", SWAP)
    return (kept[rows_a:] + sent[rows_a:] + last.astype(f32)).astype(bf16)


def solution(mesh):
    groups, samples = mesh.shape["groups"], mesh.shape["samples"]
    grid = Mesh(mesh.devices.reshape(groups, samples // 4, 2, 2), ("group", "level", "chip", "core"))
    every = ("group", "level", "chip", "core")
    in_specs = (
        P(every, None),
        P(every, None),
        P(every),
        P(every[1:], None),
        P(every[1:], None),
    )
    return jax.shard_map(body, mesh=grid, in_specs=in_specs, out_specs=P(every, None), check_vma=False)
```

```python
import functools

import jax
import jax.numpy as jnp
from jax import lax
from jax.experimental import pallas as pl
from jax.experimental.pallas import tpu as pltpu
from jax.sharding import Mesh, PartitionSpec as P

damping = 0.01
bf16 = jnp.bfloat16
f32 = jnp.float32
SWAP = [(0, 1), (1, 0)]
ANY = pl.BlockSpec(memory_space=pl.ANY)
VMEM = pl.BlockSpec(memory_space=pltpu.VMEM)
SMEM = pl.BlockSpec(memory_space=pltpu.SMEM)
LARGE = 18 * 2**20
MIDDLE = 16 * 2**20
SMALL = 12 * 2**20


def params(limit):
    return pltpu.CompilerParams(vmem_limit_bytes=limit)


def cost(flops, moved):
    return pl.CostEstimate(flops=flops, bytes_accessed=moved, transcendentals=0)


def shape(dims, dtype):
    return jax.ShapeDtypeStruct(dims, dtype)


def cut(x, first, size, axis=0):
    return lax.dynamic_slice_in_dim(x, first, size, axis)


def across(x, step, levels):
    return lax.ppermute(x, "level", [(i, i ^ step) for i in range(levels)])


def split(rows):
    return rows * 5 // 8, rows - rows * 5 // 8


def turn_kernel(levels, level_g, level_a, rows, where, *refs):
    slots, pieces, later = refs[:levels], refs[levels : levels + 4], refs[levels + 4 : levels + 6]
    basis_a, out_g, basis_g, sums, sems = refs[levels + 6 :]
    (half, late), width = split(rows), basis_a.shape[0]
    part = basis_a.shape[1]
    copies = []
    for i, (first, height, target) in enumerate(((level_g, level_a, basis_a), (0, level_g, basis_g))):
        for step, slot in enumerate(slots):
            row = pl.multiple_of((where[0] ^ step) * height, height)
            copy = pltpu.make_async_copy(
                slot.at[pl.ds(first, height)], target.at[pl.ds(row, height)], sems.at[i * levels + step]
            )
            copy.start()
            copies.append(copy)
    for copy in copies[:levels]:
        copy.wait()
    total_a = jnp.zeros((1, part), f32)
    total_g = jnp.zeros((1, part), f32)
    for piece in pieces:
        block = jnp.dot(piece[:rows], basis_a[...], preferred_element_type=f32).astype(bf16)
        total_a = total_a + jnp.sum(jnp.square(block.astype(f32)), axis=0, keepdims=True)
    for copy in copies[levels:]:
        copy.wait()
    for i, piece in enumerate(pieces):
        turned = sum(
            jnp.dot(
                piece[pl.ds(rows + 16 + j * half, half)],
                basis_g[pl.ds(j * width, width)],
                preferred_element_type=f32,
            )
            for j in range(2)
        ).astype(bf16)
        out_g[pl.ds(i * half, half)] = turned
        total_g = total_g + jnp.sum(jnp.square(turned.astype(f32)), axis=0, keepdims=True)
    for i, piece in enumerate(later):
        turned = jnp.dot(piece[...], basis_g[...], preferred_element_type=f32).astype(bf16)
        out_g[pl.ds(4 * half + i * late, late)] = turned
        total_g = total_g + jnp.sum(jnp.square(turned.astype(f32)), axis=0, keepdims=True)
    marks = sum(piece[rows : rows + 16, :part].astype(f32) for piece in pieces)
    sums[0:1] = total_g
    sums[1:2] = marks[0:1] + marks[1:2]
    sums[2:3] = total_a
    sums[3:8] = jnp.zeros((5, part), f32)


def turn(where, slots, pieces, later, rows, level_g, level_a):
    levels = len(slots)
    width_a, width_g = levels * level_a, levels * level_g
    part = slots[0].shape[1]
    half, late = split(rows)
    return pl.pallas_call(
        functools.partial(turn_kernel, levels, level_g, level_a, rows),
        out_shape=(
            shape((width_a, part), bf16),
            shape((4 * half + 2 * late, part), bf16),
            shape((width_g, part), bf16),
            shape((8, part), f32),
        ),
        in_specs=[SMEM] + [ANY] * levels + [VMEM] * 6,
        out_specs=(VMEM,) * 4,
        scratch_shapes=[pltpu.SemaphoreType.DMA((2 * levels,))],
        compiler_params=params(MIDDLE),
        cost_estimate=cost(8 * rows * part * (width_a + width_g // 2), 8 * rows * (width_a + width_g // 2)),
    )(where, *slots, *pieces, *later)


def high_low(v):
    high = v.astype(bf16)
    return high, (v - high.astype(f32)).astype(bf16)


def turn_late(rows, acts, early, bases, pieces, sums, right, left, basis, held, sems, extra):
    half, late = split(rows)
    part = bases[0].shape[1]
    cols = 2 * part
    count = 0

    def copy(source, target):
        nonlocal count
        made = pltpu.make_async_copy(source, target, sems.at[count])
        made.start()
        count += 1
        return made

    first = [copy(b, basis.at[:, pl.ds(i * part, part)]) for i, b in enumerate(bases)]
    first += [copy(p, held.at[pl.ds(i * late, late)]) for i, p in enumerate(pieces)]
    rest = [copy(a.at[pl.ds(0, rows)], left.at[pl.ds(i * rows, rows)]) for i, a in enumerate(acts)]
    for i in range(2):
        columns = pl.ds(i * part, part)
        for j in range(4):
            rest.append(copy(early[i].at[pl.ds(j * half, half)], right.at[pl.ds(j * rows, half), columns]))
        for j in range(2):
            source = early[i].at[pl.ds(4 * half + j * late, late)]
            rest.append(copy(source, right.at[pl.ds(j * rows + half, late), columns]))
    for made in first:
        made.wait()
    block = jnp.dot(held[...], basis[...], preferred_element_type=f32).astype(bf16)
    right[pl.ds(2 * rows + half, late)] = block[:late]
    right[pl.ds(3 * rows + half, late)] = block[late:]
    total = jnp.concatenate([sums[0][0:1], sums[1][0:1]], axis=1)
    extra[...] = jnp.zeros_like(extra)
    extra[0:1, :cols] = total + jnp.sum(jnp.square(block.astype(f32)), axis=0, keepdims=True)
    for i in range(4):
        extra[1:2, pl.ds(i * part, part)] = sums[i][2:3]
        extra[2:3, pl.ds(i * part, part)] = sums[i][1:2]
    for made in rest:
        made.wait()


def with_sums(block, sums):
    high, low = high_low(sums[0:4])
    return jnp.concatenate([block.astype(bf16), high, low])


def cross_kernel(levels, rows, where, *refs):
    acts, early, bases, pieces, sums = refs[:4], refs[4:6], refs[6:8], refs[8:10], refs[10:14]
    own, extra, messages = refs[14], refs[15], refs[16 : 15 + levels]
    right, left, basis, held, whole, sems = refs[15 + levels :]
    chunk = right.shape[1] // levels
    turn_late(rows, acts, early, bases, pieces, sums, right, left, basis, held, sems, extra)
    whole[...] = lax.dot_general(right[...], left[...], (((0,), (0,)), ((), ())), preferred_element_type=f32)
    own[...] = whole[pl.ds(pl.multiple_of(where[0] * chunk, chunk), chunk)]
    for step in range(1, levels):
        block = whole[pl.ds(pl.multiple_of((where[0] ^ step) * chunk, chunk), chunk)]
        messages[step - 1][...] = with_sums(block, extra)


def scratch(rows, width, width_g, cols):
    return [
        pltpu.VMEM((4 * rows, width), bf16),
        pltpu.VMEM((width_g, cols), bf16),
        pltpu.VMEM((2 * split(rows)[1], width_g), bf16),
    ]


def cross(where, acts, early, bases, pieces, sums, rows, levels):
    width_g, part = bases[0].shape
    width = acts[0].shape[1]
    cols = 2 * part
    chunk = cols // levels
    return pl.pallas_call(
        functools.partial(cross_kernel, levels, rows),
        out_shape=[shape((chunk, width), f32), shape((8, width), f32)]
        + [shape((chunk + 8, width), bf16)] * (levels - 1),
        in_specs=[SMEM] + [ANY] * 10 + [VMEM] * 4,
        out_specs=[VMEM] * (1 + levels),
        scratch_shapes=[pltpu.VMEM((4 * rows, cols), bf16)]
        + scratch(rows, width, width_g, cols)
        + [pltpu.VMEM((cols, width), f32), pltpu.SemaphoreType.DMA((20,))],
        compiler_params=params(LARGE),
        cost_estimate=cost(8 * rows * cols * width, 16 * rows * width),
    )(where, *acts, *early, *bases, *pieces, *sums)


def far_kernel(levels, rows, where, *refs):
    acts, early, bases, pieces, sums = refs[:4], refs[4:6], refs[6:8], refs[8:10], refs[10:14]
    message, extra, right, left, basis, held, sems = refs[14:]
    chunk = right.shape[1] // levels
    turn_late(rows, acts, early, bases, pieces, sums, right, left, basis, held, sems, extra)
    columns = pl.ds(pl.multiple_of((where[0] ^ 2) * chunk, chunk), chunk)
    block = lax.dot_general(right[:, columns], left[...], (((0,), (0,)), ((), ())), preferred_element_type=f32)
    message[...] = with_sums(block, extra)


def far(where, acts, early, bases, pieces, sums, rows, levels):
    width_g, part = bases[0].shape
    width = acts[0].shape[1]
    cols = 2 * part
    chunk = cols // levels
    return pl.pallas_call(
        functools.partial(far_kernel, levels, rows),
        out_shape=(shape((chunk + 8, width), bf16), shape((8, width), f32), shape((4 * rows, cols), bf16)),
        in_specs=[SMEM] + [ANY] * 10 + [VMEM] * 4,
        out_specs=(VMEM,) * 3,
        scratch_shapes=scratch(rows, width, width_g, cols) + [pltpu.SemaphoreType.DMA((20,))],
        compiler_params=params(LARGE),
        cost_estimate=cost(2 * rows * cols * width, 16 * rows * width),
    )(where, *acts, *early, *bases, *pieces, *sums)


def near_kernel(levels, rows, where, right, extra, *refs):
    acts, own, message, kept = refs[:4], refs[4], refs[5], refs[6]
    chunk = right.shape[1] // levels
    for step, target in ((0, own), (1, message), (3, kept)):
        columns = pl.ds(pl.multiple_of((where[0] ^ step) * chunk, chunk), chunk)
        block = sum(
            lax.dot_general(
                right[pl.ds(i * rows, rows), columns], a[:rows], (((0,), (0,)), ((), ())), preferred_element_type=f32
            )
            for i, a in enumerate(acts)
        )
        target[...] = with_sums(block, extra) if step == 1 else block


def near(where, right, extra, acts, rows, levels):
    width = acts[0].shape[1]
    chunk = right.shape[1] // levels
    return pl.pallas_call(
        functools.partial(near_kernel, levels, rows),
        out_shape=(shape((chunk, width), f32), shape((chunk + 8, width), bf16), shape((chunk, width), f32)),
        in_specs=[SMEM] + [VMEM] * 6,
        out_specs=(VMEM,) * 3,
        compiler_params=params(LARGE),
        cost_estimate=cost(24 * rows * chunk * width, 16 * rows * width),
    )(where, right, extra, *acts)


def add_kernel(kept, extra, got, out):
    chunk = kept.shape[0]
    more = got[...].astype(f32)
    high, low = high_low(extra[0:4] + (more[chunk : chunk + 4] + more[chunk + 4 :]))
    out[...] = jnp.concatenate([(kept[...] + more[:chunk]).astype(bf16), high, low])


def add(kept, extra, got):
    return pl.pallas_call(
        add_kernel,
        out_shape=shape(got.shape, bf16),
        in_specs=[VMEM] * 3,
        out_specs=VMEM,
        compiler_params=params(SMALL),
        cost_estimate=cost(kept.size, 8 * kept.size),
    )(kept, extra, got)


def middle_kernel(levels, where, own, own_extra, *refs):
    count = len(refs) - levels - 6
    messages, bases, outs = refs[:count], refs[count : count + 4], refs[count + 4 : -2]
    basis, turned = refs[-2:]
    chunk, width = own.shape
    cols = chunk * levels
    part = bases[0].shape[1]
    for i, b in enumerate(bases):
        basis[:, pl.ds(i * part, part)] = b[...]
    total = own[...]
    extra = own_extra[...]
    for message in messages:
        part_sum = message[...].astype(f32)
        total = total + part_sum[:chunk]
        more = part_sum[chunk:]
        extra = extra + jnp.concatenate([more[0:4] + more[4:8], jnp.zeros_like(more[:4])])
    count = extra[2:3]
    extra = extra / count
    lam_a = extra[1:2]
    turned[...] = jnp.transpose(extra[:, :cols])
    lam_g = turned[pl.ds(pl.multiple_of(where[0] * chunk, chunk), chunk)][:, 0:1]
    both = jnp.dot(jnp.concatenate(high_low(total)), basis[...], preferred_element_type=f32)
    rotated = (both[:chunk] + both[chunk:]) / count
    scaled = (rotated / (lam_g * lam_a + damping)).astype(bf16)
    height = width // levels
    for step, out in enumerate(outs):
        rows = pl.ds(pl.multiple_of((where[0] ^ step) * height, height), height)
        out[...] = lax.dot_general(
            scaled, basis[rows], (((1,), (1,)), ((), ())), preferred_element_type=f32
        ).astype(bf16)


def middle(where, own, own_extra, messages, bases, levels):
    chunk, width = own.shape
    return pl.pallas_call(
        functools.partial(middle_kernel, levels),
        out_shape=[shape((chunk, width // levels), bf16)] * levels,
        in_specs=[SMEM] + [VMEM] * (len(messages) + 6),
        out_specs=[VMEM] * levels,
        scratch_shapes=[pltpu.VMEM((width, width), bf16), pltpu.VMEM((chunk * levels, 8), f32)],
        compiler_params=params(SMALL),
        cost_estimate=cost(6 * chunk * width * width, 2 * width * width),
    )(where, own, own_extra, *messages, *bases)


def result_kernel(levels, where, *refs):
    slots = refs[:levels]
    one, two, sent, kept, mid, whole, sems = refs[levels:]
    chunk, height = slots[0].shape
    wide, part = one.shape
    copies = []
    for step, slot in enumerate(slots):
        row = pl.multiple_of((where[0] ^ step) * chunk, chunk)
        copy = pltpu.make_async_copy(slot, mid.at[pl.ds(row, chunk)], sems.at[step])
        copy.start()
        copies.append(copy)
    for copy in copies:
        copy.wait()
    quarter = wide // 4
    for j in range(4):
        columns = pl.ds(j * quarter, quarter)
        whole[:, columns] = sum(
            lax.dot_general(
                mid[pl.ds(i * part, part)], b[columns], (((0,), (1,)), ((), ())), preferred_element_type=f32
            )
            for i, b in enumerate((one, two))
        )
    rows = height // 4
    for i, (other, target) in enumerate(((3, sent), (1, sent), (2, kept), (0, kept))):
        block = whole[pl.ds(pl.multiple_of((where[1] ^ other) * rows, rows), rows)]
        target[pl.ds((i % 2) * rows, rows)] = block.astype(target.dtype)


def result(where, slots, bases):
    levels = len(slots)
    chunk, height = slots[0].shape
    wide, part = bases[0].shape
    return pl.pallas_call(
        functools.partial(result_kernel, levels),
        out_shape=(shape((height // 2, wide), f32), shape((height // 2, wide), f32)),
        in_specs=[SMEM] + [ANY] * levels + [VMEM] * 2,
        out_specs=(VMEM, VMEM),
        scratch_shapes=[
            pltpu.VMEM((2 * part, height), bf16),
            pltpu.VMEM((height, wide), f32),
            pltpu.SemaphoreType.DMA((levels,)),
        ],
        compiler_params=params(SMALL),
        cost_estimate=cost(4 * height * part * wide, 4 * wide * part),
    )(where, *slots, *bases)


def gather_levels(unit, level, levels, ready):
    def over(slot):
        return lax.ppermute(slot, "group", SWAP)

    if levels != 4:
        slots = [unit] + [across(unit, step, levels) for step in range(1, levels)]
        return slots, [over(slot) for slot in slots], ready
    middle = (level == 1) | (level == 2)
    together = lax.optimization_barrier
    inner = lax.ppermute(unit, "level", [(1, 2), (2, 1)])
    first, inner, other0, ready = together((across(unit, 1, levels), inner, over(unit), ready))
    held, inner = together((unit, inner))
    outer, other1 = together((lax.ppermute(held, "level", [(0, 3), (3, 0)]), over(first)))
    third = jnp.where(middle, inner, outer)
    second, other3 = together((across(third, 1, levels), over(third)))
    return [unit, first, second, third], [other0, other1, over(second), other3], ready


def body(acts, grads, counts, basis_a, basis_g):
    group, level, chip, core = (lax.axis_index(n) for n in ("group", "level", "chip", "core"))
    levels = lax.axis_size("level")
    rows, width_a = acts.shape
    width_g = grads.shape[1]
    rows_a, rows_g = basis_a.shape[0], basis_g.shape[0]
    part_a, part_g = width_a // 4, width_g // 8
    where = jnp.stack([level, chip * 2 + core]).astype(jnp.int32)

    def columns(y, c):
        return jnp.concatenate(
            [
                cut(basis_g, ((y * 2 + c) * 2 + group) * part_g, part_g, 1),
                cut(basis_a, (c * 2 + group) * part_a, part_a, 1),
            ]
        )

    def diagonal(x):
        return lax.ppermute(x, ("chip", "core"), [(i, 3 - i) for i in range(4)])

    beyond = [lax.ppermute(columns(1 - chip, core), "chip", SWAP), diagonal(columns(1 - chip, 1 - core))]
    beside = lax.ppermute(columns(chip, 1 - core), "core", SWAP)
    blocks = jnp.stack([columns(chip, core), beside] + beyond)
    blocks = [lax.dynamic_index_in_dim(blocks, j ^ (chip * 2 + core), 0, False) for j in range(4)]
    unit = jnp.concatenate([b[:rows_g] for b in blocks] + [b[rows_g:] for b in blocks])
    level_g, level_a = 4 * rows_g, 4 * rows_a

    valid = counts[0]
    keep = jnp.arange(rows, dtype=jnp.int32)[:, None] < valid
    half = split(rows)[0]
    later, _ = lax.optimization_barrier((grads, unit))
    slots, others, late = gather_levels(unit, level, levels, jnp.where(keep[half:], later[half:], 0))
    marks = jnp.stack([valid // 16 * 16, valid % 16]).astype(bf16)
    marks = jnp.broadcast_to(jnp.pad(marks, (0, 14))[:, None], (16, width_a))
    early = jnp.where(keep[:half], grads[:half], 0)
    early = jnp.concatenate([jnp.where(keep, acts, 0), marks, early[:, :width_a], early[:, width_a:]])
    early_out, _ = lax.optimization_barrier((early, beyond[0]))

    together = lax.optimization_barrier
    far_rows, slots[2] = together((lax.ppermute(early_out, "chip", SWAP), slots[2]))
    early = [early, lax.ppermute(early, "core", SWAP), far_rows, lax.ppermute(far_rows, "core", SWAP)]
    later = [late, lax.ppermute(late, "core", SWAP)]
    first = turn(where, slots, early, later, rows, level_g, level_a)
    others[2], first = together((others[2], first))
    second = turn(where, others, early, later, rows, level_g, level_a)
    far_rows, second = together((lax.ppermute(late, "chip", SWAP), second))
    late = [far_rows, lax.ppermute(far_rows, "core", SWAP)]
    bases_a, turned_g, bases_g, sums = zip(first, second)
    sums += tuple(lax.ppermute(t, "core", SWAP) for t in sums)
    bases_a += tuple(lax.ppermute(t, "core", SWAP) for t in bases_a)

    if levels == 4:
        message, own_extra, right = far(where, early, turned_g, bases_g, late, sums, rows, levels)
        message = across(message, 1, levels)
        own, beside, kept = near(where, right, own_extra, early, rows, levels)
        got = [across(add(kept, own_extra, message), 3, levels), across(beside, 1, levels)]
    else:
        own, own_extra, *messages = cross(where, early, turned_g, bases_g, late, sums, rows, levels)
        got = [across(m, step + 1, levels) for step, m in enumerate(messages)]
    mids = middle(where, own, own_extra, got, bases_a, levels)
    mids = [m if step == 0 else across(m, step, levels) for step, m in enumerate(mids)]

    sent, kept = result(where, mids, bases_g)
    sent = lax.ppermute(sent.astype(bf16), "core", SWAP).astype(f32)
    last = lax.ppermute((kept[:rows_a] + sent[:rows_a]).astype(bf16), "chip", SWAP)
    return (kept[rows_a:] + sent[rows_a:] + last.astype(f32)).astype(bf16)


def solution(mesh):
    groups, samples = mesh.shape["groups"], mesh.shape["samples"]
    grid = Mesh(mesh.devices.reshape(groups, samples // 4, 2, 2), ("group", "level", "chip", "core"))
    every = ("group", "level", "chip", "core")
    in_specs = (
        P(every, None),
        P(every, None),
        P(every),
        P(every[1:], None),
        P(every[1:], None),
    )
    return jax.shard_map(body, mesh=grid, in_specs=in_specs, out_specs=P(every, None), check_vma=False)
```

```python
import functools

import jax
import jax.numpy as jnp
from jax import lax
from jax.experimental import pallas as pl
from jax.experimental.pallas import tpu as pltpu
from jax.sharding import Mesh, PartitionSpec as P

damping = 0.01
bf16 = jnp.bfloat16
f32 = jnp.float32
SWAP = [(0, 1), (1, 0)]
ANY = pl.BlockSpec(memory_space=pl.ANY)
VMEM = pl.BlockSpec(memory_space=pltpu.VMEM)
SMEM = pl.BlockSpec(memory_space=pltpu.SMEM)
LARGE = 18 * 2**20
MIDDLE = 16 * 2**20
SMALL = 12 * 2**20


def params(limit):
    return pltpu.CompilerParams(vmem_limit_bytes=limit)


def cost(flops, moved):
    return pl.CostEstimate(flops=flops, bytes_accessed=moved, transcendentals=0)


def shape(dims, dtype):
    return jax.ShapeDtypeStruct(dims, dtype)


def cut(x, first, size, axis=0):
    return lax.dynamic_slice_in_dim(x, first, size, axis)


def across(x, step, levels):
    return lax.ppermute(x, "level", [(i, i ^ step) for i in range(levels)])


def split(rows):
    return rows * 5 // 8, rows - rows * 5 // 8


def turn_kernel(levels, level_g, level_a, rows, where, *refs):
    slots, pieces, later = refs[:levels], list(refs[levels : levels + 4]), refs[levels + 4 : levels + 6]
    basis_a, out_g, basis_g, sums, held, held_sem, sems = refs[levels + 6 :]
    (half, late), width = split(rows), basis_a.shape[0]
    part = basis_a.shape[1]
    move = pltpu.make_async_copy(pieces[2], held, held_sem)
    pieces[2] = held
    copies = []
    for i, (first, height, target) in enumerate(((level_g, level_a, basis_a), (0, level_g, basis_g))):
        for step, slot in enumerate(slots):
            row = pl.multiple_of((where[0] ^ step) * height, height)
            copy = pltpu.make_async_copy(
                slot.at[pl.ds(first, height)], target.at[pl.ds(row, height)], sems.at[i * levels + step]
            )
            copy.start()
            copies.append(copy)
    move.start()

    def squares(x):
        return jnp.sum(jnp.square(x.astype(f32)), axis=0, keepdims=True)

    def turn_a(piece):
        return squares(jnp.dot(piece[:rows], basis_a[...], preferred_element_type=f32).astype(bf16))

    def turn_g(i):
        turned = sum(
            jnp.dot(
                pieces[i][pl.ds(rows + 16 + j * half, half)],
                basis_g[pl.ds(j * width, width)],
                preferred_element_type=f32,
            )
            for j in range(2)
        ).astype(bf16)
        out_g[pl.ds(i * half, half)] = turned
        return squares(turned)

    for copy in copies[:levels]:
        copy.wait()
    total_a = sum(turn_a(pieces[i]) for i in (0, 1, 3))
    for copy in copies[levels:]:
        copy.wait()
    total_g = sum(turn_g(i) for i in (0, 1, 3))
    for i, piece in enumerate(later):
        turned = jnp.dot(piece[...], basis_g[...], preferred_element_type=f32).astype(bf16)
        out_g[pl.ds(4 * half + i * late, late)] = turned
        total_g = total_g + squares(turned)
    move.wait()
    marks = sum(piece[rows : rows + 16, :part].astype(f32) for piece in pieces)
    sums[0:1] = total_g + turn_g(2)
    sums[1:2] = marks[0:1] + marks[1:2]
    sums[2:3] = total_a + turn_a(held)
    sums[3:8] = jnp.zeros((5, part), f32)


def turn(where, slots, pieces, later, rows, level_g, level_a):
    levels = len(slots)
    width_a, width_g = levels * level_a, levels * level_g
    part = slots[0].shape[1]
    half, late = split(rows)
    return pl.pallas_call(
        functools.partial(turn_kernel, levels, level_g, level_a, rows),
        out_shape=(
            shape((width_a, part), bf16),
            shape((4 * half + 2 * late, part), bf16),
            shape((width_g, part), bf16),
            shape((8, part), f32),
        ),
        in_specs=[SMEM] + [ANY] * levels + [VMEM] * 2 + [ANY] + [VMEM] * 3,
        out_specs=(VMEM,) * 4,
        scratch_shapes=[
            pltpu.VMEM(pieces[2].shape, bf16),
            pltpu.SemaphoreType.DMA,
            pltpu.SemaphoreType.DMA((2 * levels,)),
        ],
        compiler_params=params(MIDDLE),
        cost_estimate=cost(8 * rows * part * (width_a + width_g // 2), 8 * rows * (width_a + width_g // 2)),
    )(where, *slots, *pieces, *later)


def high_low(v):
    high = v.astype(bf16)
    return high, (v - high.astype(f32)).astype(bf16)


def turn_late(rows, acts, early, bases, pieces, sums, right, left, basis, held, sems, extra):
    half, late = split(rows)
    part = bases[0].shape[1]
    cols = 2 * part
    count = 0

    def copy(source, target):
        nonlocal count
        made = pltpu.make_async_copy(source, target, sems.at[count])
        made.start()
        count += 1
        return made

    first = [copy(b, basis.at[:, pl.ds(i * part, part)]) for i, b in enumerate(bases)]
    first += [copy(p, held.at[pl.ds(i * late, late)]) for i, p in enumerate(pieces)]
    rest = [copy(a.at[pl.ds(0, rows)], left.at[pl.ds(i * rows, rows)]) for i, a in enumerate(acts)]
    for i in range(2):
        columns = pl.ds(i * part, part)
        for j in range(4):
            rest.append(copy(early[i].at[pl.ds(j * half, half)], right.at[pl.ds(j * rows, half), columns]))
        for j in range(2):
            source = early[i].at[pl.ds(4 * half + j * late, late)]
            rest.append(copy(source, right.at[pl.ds(j * rows + half, late), columns]))
    for made in first:
        made.wait()
    block = jnp.dot(held[...], basis[...], preferred_element_type=f32).astype(bf16)
    right[pl.ds(2 * rows + half, late)] = block[:late]
    right[pl.ds(3 * rows + half, late)] = block[late:]
    total = jnp.concatenate([sums[0][0:1], sums[1][0:1]], axis=1)
    extra[...] = jnp.zeros_like(extra)
    extra[0:1, :cols] = total + jnp.sum(jnp.square(block.astype(f32)), axis=0, keepdims=True)
    for i in range(4):
        extra[1:2, pl.ds(i * part, part)] = sums[i][2:3]
        extra[2:3, pl.ds(i * part, part)] = sums[i][1:2]
    for made in rest:
        made.wait()


def with_sums(block, sums):
    high, low = high_low(sums[0:4])
    return jnp.concatenate([block.astype(bf16), high, low])


def cross_kernel(levels, rows, where, *refs):
    acts, early, bases, pieces, sums = refs[:4], refs[4:6], refs[6:8], refs[8:10], refs[10:14]
    own, extra, messages = refs[14], refs[15], refs[16 : 15 + levels]
    right, left, basis, held, whole, sems = refs[15 + levels :]
    chunk = right.shape[1] // levels
    turn_late(rows, acts, early, bases, pieces, sums, right, left, basis, held, sems, extra)
    whole[...] = lax.dot_general(right[...], left[...], (((0,), (0,)), ((), ())), preferred_element_type=f32)
    own[...] = whole[pl.ds(pl.multiple_of(where[0] * chunk, chunk), chunk)]
    for step in range(1, levels):
        block = whole[pl.ds(pl.multiple_of((where[0] ^ step) * chunk, chunk), chunk)]
        messages[step - 1][...] = with_sums(block, extra)


def scratch(rows, width, width_g, cols):
    return [
        pltpu.VMEM((4 * rows, width), bf16),
        pltpu.VMEM((width_g, cols), bf16),
        pltpu.VMEM((2 * split(rows)[1], width_g), bf16),
    ]


def cross(where, acts, early, bases, pieces, sums, rows, levels):
    width_g, part = bases[0].shape
    width = acts[0].shape[1]
    cols = 2 * part
    chunk = cols // levels
    return pl.pallas_call(
        functools.partial(cross_kernel, levels, rows),
        out_shape=[shape((chunk, width), f32), shape((8, width), f32)]
        + [shape((chunk + 8, width), bf16)] * (levels - 1),
        in_specs=[SMEM] + [ANY] * 10 + [VMEM] * 4,
        out_specs=[VMEM] * (1 + levels),
        scratch_shapes=[pltpu.VMEM((4 * rows, cols), bf16)]
        + scratch(rows, width, width_g, cols)
        + [pltpu.VMEM((cols, width), f32), pltpu.SemaphoreType.DMA((20,))],
        compiler_params=params(LARGE),
        cost_estimate=cost(8 * rows * cols * width, 16 * rows * width),
    )(where, *acts, *early, *bases, *pieces, *sums)


def far_kernel(levels, rows, where, *refs):
    acts, early, bases, pieces, sums = refs[:4], refs[4:6], refs[6:8], refs[8:10], refs[10:14]
    message, extra, right, left, basis, held, sems = refs[14:]
    chunk = right.shape[1] // levels
    turn_late(rows, acts, early, bases, pieces, sums, right, left, basis, held, sems, extra)
    columns = pl.ds(pl.multiple_of((where[0] ^ 2) * chunk, chunk), chunk)
    block = lax.dot_general(right[:, columns], left[...], (((0,), (0,)), ((), ())), preferred_element_type=f32)
    message[...] = with_sums(block, extra)


def far(where, acts, early, bases, pieces, sums, rows, levels):
    width_g, part = bases[0].shape
    width = acts[0].shape[1]
    cols = 2 * part
    chunk = cols // levels
    return pl.pallas_call(
        functools.partial(far_kernel, levels, rows),
        out_shape=(shape((chunk + 8, width), bf16), shape((8, width), f32), shape((4 * rows, cols), bf16)),
        in_specs=[SMEM] + [ANY] * 10 + [VMEM] * 4,
        out_specs=(VMEM,) * 3,
        scratch_shapes=scratch(rows, width, width_g, cols) + [pltpu.SemaphoreType.DMA((20,))],
        compiler_params=params(LARGE),
        cost_estimate=cost(2 * rows * cols * width, 16 * rows * width),
    )(where, *acts, *early, *bases, *pieces, *sums)


def near_kernel(levels, rows, where, right, extra, *refs):
    acts, own, message, kept = refs[:4], refs[4], refs[5], refs[6]
    chunk = right.shape[1] // levels
    for step, target in ((0, own), (1, message), (3, kept)):
        columns = pl.ds(pl.multiple_of((where[0] ^ step) * chunk, chunk), chunk)
        block = sum(
            lax.dot_general(
                right[pl.ds(i * rows, rows), columns], a[:rows], (((0,), (0,)), ((), ())), preferred_element_type=f32
            )
            for i, a in enumerate(acts)
        )
        target[...] = with_sums(block, extra) if step == 1 else block


def near(where, right, extra, acts, rows, levels):
    width = acts[0].shape[1]
    chunk = right.shape[1] // levels
    return pl.pallas_call(
        functools.partial(near_kernel, levels, rows),
        out_shape=(shape((chunk, width), f32), shape((chunk + 8, width), bf16), shape((chunk, width), f32)),
        in_specs=[SMEM] + [VMEM] * 6,
        out_specs=(VMEM,) * 3,
        compiler_params=params(LARGE),
        cost_estimate=cost(24 * rows * chunk * width, 16 * rows * width),
    )(where, right, extra, *acts)


def add_kernel(kept, extra, got, out):
    chunk = kept.shape[0]
    more = got[...].astype(f32)
    high, low = high_low(extra[0:4] + (more[chunk : chunk + 4] + more[chunk + 4 :]))
    out[...] = jnp.concatenate([(kept[...] + more[:chunk]).astype(bf16), high, low])


def add(kept, extra, got):
    return pl.pallas_call(
        add_kernel,
        out_shape=shape(got.shape, bf16),
        in_specs=[VMEM] * 3,
        out_specs=VMEM,
        compiler_params=params(SMALL),
        cost_estimate=cost(kept.size, 8 * kept.size),
    )(kept, extra, got)


def middle_kernel(levels, where, own, own_extra, *refs):
    count = len(refs) - levels - 6
    messages, bases, outs = refs[:count], refs[count : count + 4], refs[count + 4 : -2]
    basis, turned = refs[-2:]
    chunk, width = own.shape
    cols = chunk * levels
    part = bases[0].shape[1]
    for i, b in enumerate(bases):
        basis[:, pl.ds(i * part, part)] = b[...]
    total = own[...]
    extra = own_extra[...]
    for message in messages:
        part_sum = message[...].astype(f32)
        total = total + part_sum[:chunk]
        more = part_sum[chunk:]
        extra = extra + jnp.concatenate([more[0:4] + more[4:8], jnp.zeros_like(more[:4])])
    count = extra[2:3]
    extra = extra / count
    lam_a = extra[1:2]
    turned[...] = jnp.transpose(extra[:, :cols])
    lam_g = turned[pl.ds(pl.multiple_of(where[0] * chunk, chunk), chunk)][:, 0:1]
    both = jnp.dot(jnp.concatenate(high_low(total)), basis[...], preferred_element_type=f32)
    rotated = (both[:chunk] + both[chunk:]) / count
    scaled = (rotated / (lam_g * lam_a + damping)).astype(bf16)
    height = width // levels
    for step, out in enumerate(outs):
        rows = pl.ds(pl.multiple_of((where[0] ^ step) * height, height), height)
        out[...] = lax.dot_general(
            scaled, basis[rows], (((1,), (1,)), ((), ())), preferred_element_type=f32
        ).astype(bf16)


def middle(where, own, own_extra, messages, bases, levels):
    chunk, width = own.shape
    return pl.pallas_call(
        functools.partial(middle_kernel, levels),
        out_shape=[shape((chunk, width // levels), bf16)] * levels,
        in_specs=[SMEM] + [VMEM] * (len(messages) + 6),
        out_specs=[VMEM] * levels,
        scratch_shapes=[pltpu.VMEM((width, width), bf16), pltpu.VMEM((chunk * levels, 8), f32)],
        compiler_params=params(SMALL),
        cost_estimate=cost(6 * chunk * width * width, 2 * width * width),
    )(where, own, own_extra, *messages, *bases)


def result_kernel(levels, where, *refs):
    slots = refs[:levels]
    one, two, outs, (mid, whole, sems) = refs[levels], refs[levels + 1], refs[levels + 2 : -3], refs[-3:]
    chunk, height = slots[0].shape
    wide, part = one.shape
    copies = []
    for step, slot in enumerate(slots):
        row = pl.multiple_of((where[0] ^ step) * chunk, chunk)
        copy = pltpu.make_async_copy(slot, mid.at[pl.ds(row, chunk)], sems.at[step])
        copy.start()
        copies.append(copy)
    for copy in copies:
        copy.wait()
    quarter = wide // 4
    for j in range(4):
        columns = pl.ds(j * quarter, quarter)
        whole[:, columns] = sum(
            lax.dot_general(
                mid[pl.ds(i * part, part)], b[columns], (((0,), (1,)), ((), ())), preferred_element_type=f32
            )
            for i, b in enumerate((one, two))
        )
    rows = height // 4
    for other, out in zip((3, 1, 2, 0), outs):
        out[...] = whole[pl.ds(pl.multiple_of((where[1] ^ other) * rows, rows), rows)].astype(out.dtype)


def result(where, slots, bases):
    levels = len(slots)
    chunk, height = slots[0].shape
    wide, part = bases[0].shape
    return pl.pallas_call(
        functools.partial(result_kernel, levels),
        out_shape=[shape((height // 4, wide), t) for t in (bf16, bf16, f32, f32)],
        in_specs=[SMEM] + [ANY] * levels + [VMEM] * 2,
        out_specs=[VMEM] * 4,
        scratch_shapes=[
            pltpu.VMEM((2 * part, height), bf16),
            pltpu.VMEM((height, wide), f32),
            pltpu.SemaphoreType.DMA((levels,)),
        ],
        compiler_params=params(SMALL),
        cost_estimate=cost(4 * height * part * wide, 4 * wide * part),
    )(where, *slots, *bases)


def gather_levels(unit, level, levels, ready):
    def over(slot):
        return lax.ppermute(slot, "group", SWAP)

    if levels != 4:
        slots = [unit] + [across(unit, step, levels) for step in range(1, levels)]
        return slots, [over(slot) for slot in slots], ready
    middle = (level == 1) | (level == 2)
    together = lax.optimization_barrier
    inner = lax.ppermute(unit, "level", [(1, 2), (2, 1)])
    first, inner, other0, ready = together((across(unit, 1, levels), inner, over(unit), ready))
    held, inner = together((unit, inner))
    outer, other1 = together((lax.ppermute(held, "level", [(0, 3), (3, 0)]), over(first)))
    third = jnp.where(middle, inner, outer)
    second, other3 = together((across(third, 1, levels), over(third)))
    return [unit, first, second, third], [other0, other1, over(second), other3], ready


def body(acts, grads, counts, basis_a, basis_g):
    group, level, chip, core = (lax.axis_index(n) for n in ("group", "level", "chip", "core"))
    levels = lax.axis_size("level")
    rows, width_a = acts.shape
    width_g = grads.shape[1]
    rows_a, rows_g = basis_a.shape[0], basis_g.shape[0]
    part_a, part_g = width_a // 4, width_g // 8
    where = jnp.stack([level, chip * 2 + core]).astype(jnp.int32)

    def columns(y, c):
        return jnp.concatenate(
            [
                cut(basis_g, ((y * 2 + c) * 2 + group) * part_g, part_g, 1),
                cut(basis_a, (c * 2 + group) * part_a, part_a, 1),
            ]
        )

    def diagonal(x):
        return lax.ppermute(x, ("chip", "core"), [(i, 3 - i) for i in range(4)])

    beyond = [lax.ppermute(columns(1 - chip, core), "chip", SWAP), diagonal(columns(1 - chip, 1 - core))]
    beside = lax.ppermute(columns(chip, 1 - core), "core", SWAP)
    blocks = jnp.stack([columns(chip, core), beside] + beyond)
    blocks = [lax.dynamic_index_in_dim(blocks, j ^ (chip * 2 + core), 0, False) for j in range(4)]
    unit = jnp.concatenate([b[:rows_g] for b in blocks] + [b[rows_g:] for b in blocks])
    level_g, level_a = 4 * rows_g, 4 * rows_a

    valid = counts[0]
    keep = jnp.arange(rows, dtype=jnp.int32)[:, None] < valid
    half = split(rows)[0]
    later, _ = lax.optimization_barrier((grads, unit))
    slots, others, late = gather_levels(unit, level, levels, jnp.where(keep[half:], later[half:], 0))
    marks = jnp.stack([valid // 16 * 16, valid % 16]).astype(bf16)
    marks = jnp.broadcast_to(jnp.pad(marks, (0, 14))[:, None], (16, width_a))
    early = jnp.where(keep[:half], grads[:half], 0)
    early = jnp.concatenate([jnp.where(keep, acts, 0), marks, early[:, :width_a], early[:, width_a:]])
    early_out, _ = lax.optimization_barrier((early, beyond[0]))

    together = lax.optimization_barrier
    far_rows, slots[2] = together((lax.ppermute(early_out, "chip", SWAP), slots[2]))
    early = [early, lax.ppermute(early, "core", SWAP), far_rows, lax.ppermute(far_rows, "core", SWAP)]
    later = [late, lax.ppermute(late, "core", SWAP)]
    first = turn(where, slots, early, later, rows, level_g, level_a)
    others[2], first = together((others[2], first))
    second = turn(where, others, early, later, rows, level_g, level_a)
    far_rows, second = together((lax.ppermute(late, "chip", SWAP), second))
    late = [far_rows, lax.ppermute(far_rows, "core", SWAP)]
    bases_a, turned_g, bases_g, sums = zip(first, second)
    sums += tuple(lax.ppermute(t, "core", SWAP) for t in sums)
    bases_a += tuple(lax.ppermute(t, "core", SWAP) for t in bases_a)

    if levels == 4:
        message, own_extra, right = far(where, early, turned_g, bases_g, late, sums, rows, levels)
        message = across(message, 1, levels)
        own, beside, kept = near(where, right, own_extra, early, rows, levels)
        got = [across(add(kept, own_extra, message), 3, levels), across(beside, 1, levels)]
    else:
        own, own_extra, *messages = cross(where, early, turned_g, bases_g, late, sums, rows, levels)
        got = [across(m, step + 1, levels) for step, m in enumerate(messages)]
    mids = middle(where, own, own_extra, got, bases_a, levels)
    mids = [m if step == 0 else across(m, step, levels) for step, m in enumerate(mids)]

    *sent, far_kept, near_kept = result(where, mids, bases_g)
    far_sent, near_sent = (lax.ppermute(x, "core", SWAP).astype(f32) for x in sent)
    last = lax.ppermute((far_kept + far_sent).astype(bf16), "chip", SWAP)
    return (near_kept + near_sent + last.astype(f32)).astype(bf16)


def solution(mesh):
    groups, samples = mesh.shape["groups"], mesh.shape["samples"]
    grid = Mesh(mesh.devices.reshape(groups, samples // 4, 2, 2), ("group", "level", "chip", "core"))
    every = ("group", "level", "chip", "core")
    in_specs = (
        P(every, None),
        P(every, None),
        P(every),
        P(every[1:], None),
        P(every[1:], None),
    )
    return jax.shard_map(body, mesh=grid, in_specs=in_specs, out_specs=P(every, None), check_vma=False)
```

```python
import functools

import jax
import jax.numpy as jnp
from jax import lax
from jax.experimental import pallas as pl
from jax.experimental.pallas import tpu as pltpu
from jax.sharding import Mesh, PartitionSpec as P

damping = 0.01
bf16 = jnp.bfloat16
f32 = jnp.float32
SWAP = [(0, 1), (1, 0)]
ANY = pl.BlockSpec(memory_space=pl.ANY)
VMEM = pl.BlockSpec(memory_space=pltpu.VMEM)
SMEM = pl.BlockSpec(memory_space=pltpu.SMEM)
LARGE = 18 * 2**20
MIDDLE = 16 * 2**20
SMALL = 12 * 2**20


def params(limit):
    return pltpu.CompilerParams(vmem_limit_bytes=limit)


def cost(flops, moved):
    return pl.CostEstimate(flops=flops, bytes_accessed=moved, transcendentals=0)


def shape(dims, dtype):
    return jax.ShapeDtypeStruct(dims, dtype)


def cut(x, first, size, axis=0):
    return lax.dynamic_slice_in_dim(x, first, size, axis)


def across(x, step, levels):
    return lax.ppermute(x, "level", [(i, i ^ step) for i in range(levels)])


def split(rows):
    return rows * 5 // 8, rows - rows * 5 // 8


def turn_kernel(levels, level_g, level_a, rows, where, *refs):
    slots, pieces, later = refs[:levels], list(refs[levels : levels + 4]), refs[levels + 4 : levels + 6]
    basis_a, out_g, basis_g, sums, held, held_sem, sems = refs[levels + 6 :]
    (half, late), width = split(rows), basis_a.shape[0]
    part = basis_a.shape[1]
    move = pltpu.make_async_copy(pieces[2], held, held_sem)
    pieces[2] = held
    copies = []
    for i, (first, height, target) in enumerate(((level_g, level_a, basis_a), (0, level_g, basis_g))):
        for step, slot in enumerate(slots):
            row = pl.multiple_of((where[0] ^ step) * height, height)
            copy = pltpu.make_async_copy(
                slot.at[pl.ds(first, height)], target.at[pl.ds(row, height)], sems.at[i * levels + step]
            )
            copy.start()
            copies.append(copy)
    move.start()

    def squares(x):
        return jnp.sum(jnp.square(x.astype(f32)), axis=0, keepdims=True)

    def turn_a(piece):
        return squares(jnp.dot(piece[:rows], basis_a[...], preferred_element_type=f32).astype(bf16))

    def turn_g(i):
        turned = sum(
            jnp.dot(
                pieces[i][pl.ds(rows + 16 + j * half, half)],
                basis_g[pl.ds(j * width, width)],
                preferred_element_type=f32,
            )
            for j in range(2)
        ).astype(bf16)
        out_g[pl.ds(i * half, half)] = turned
        return squares(turned)

    for copy in copies[:levels]:
        copy.wait()
    total_a = sum(turn_a(pieces[i]) for i in (0, 1, 3))
    for copy in copies[levels:]:
        copy.wait()
    total_g = sum(turn_g(i) for i in (0, 1, 3))
    for i, piece in enumerate(later):
        turned = jnp.dot(piece[...], basis_g[...], preferred_element_type=f32).astype(bf16)
        out_g[pl.ds(4 * half + i * late, late)] = turned
        total_g = total_g + squares(turned)
    move.wait()
    marks = sum(piece[rows : rows + 16, :part].astype(f32) for piece in pieces)
    sums[0:1] = total_g + turn_g(2)
    sums[1:2] = marks[0:1] + marks[1:2]
    sums[2:3] = total_a + turn_a(held)
    sums[3:8] = jnp.zeros((5, part), f32)


def turn(where, slots, pieces, later, rows, level_g, level_a):
    levels = len(slots)
    width_a, width_g = levels * level_a, levels * level_g
    part = slots[0].shape[1]
    half, late = split(rows)
    return pl.pallas_call(
        functools.partial(turn_kernel, levels, level_g, level_a, rows),
        out_shape=(
            shape((width_a, part), bf16),
            shape((4 * half + 2 * late, part), bf16),
            shape((width_g, part), bf16),
            shape((8, part), f32),
        ),
        in_specs=[SMEM] + [ANY] * levels + [VMEM] * 2 + [ANY] + [VMEM] * 3,
        out_specs=(VMEM,) * 4,
        scratch_shapes=[
            pltpu.VMEM(pieces[2].shape, bf16),
            pltpu.SemaphoreType.DMA,
            pltpu.SemaphoreType.DMA((2 * levels,)),
        ],
        compiler_params=params(MIDDLE),
        cost_estimate=cost(8 * rows * part * (width_a + width_g // 2), 8 * rows * (width_a + width_g // 2)),
    )(where, *slots, *pieces, *later)


def high_low(v):
    high = v.astype(bf16)
    return high, (v - high.astype(f32)).astype(bf16)


def turn_late(rows, acts, early, bases, pieces, sums, right, moved, held, sems, extra):
    half, late = split(rows)
    part = bases[0].shape[1]
    count = 0

    def copy(source, target):
        nonlocal count
        made = pltpu.make_async_copy(source, target, sems.at[count])
        made.start()
        count += 1
        return made

    first = [copy(p, held.at[pl.ds(i * late, late)]) for i, p in enumerate(pieces)]
    rest = [copy(acts[2].at[pl.ds(0, rows)], moved)]
    for i in range(2):
        columns = pl.ds(i * part, part)
        for j in range(4):
            rest.append(copy(early[i].at[pl.ds(j * half, half)], right.at[pl.ds(j * rows, half), columns]))
        for j in range(2):
            source = early[i].at[pl.ds(4 * half + j * late, late)]
            rest.append(copy(source, right.at[pl.ds(j * rows + half, late), columns]))
    extra[...] = jnp.zeros_like(extra)
    for i in range(4):
        extra[1:2, pl.ds(i * part, part)] = sums[i][2:3]
        extra[2:3, pl.ds(i * part, part)] = sums[i][1:2]
    for made in first:
        made.wait()
    for i, basis in enumerate(bases):
        columns = pl.ds(i * part, part)
        block = jnp.dot(held[...], basis[...], preferred_element_type=f32).astype(bf16)
        right[pl.ds(2 * rows + half, late), columns] = block[:late]
        right[pl.ds(3 * rows + half, late), columns] = block[late:]
        extra[0:1, columns] = sums[i][0:1] + jnp.sum(jnp.square(block.astype(f32)), axis=0, keepdims=True)
    for made in rest:
        made.wait()
    return acts[0], acts[1], moved, acts[3]


def chunk_of(right, columns, acts, rows):
    return sum(
        lax.dot_general(
            right[pl.ds(i * rows, rows), columns], a[:rows], (((0,), (0,)), ((), ())), preferred_element_type=f32
        )
        for i, a in enumerate(acts)
    )


def with_sums(block, sums):
    high, low = high_low(sums[0:4])
    return jnp.concatenate([block.astype(bf16), high, low])


def cross_kernel(levels, rows, where, *refs):
    acts, early, bases, pieces, sums = refs[:4], refs[4:6], refs[6:8], refs[8:10], refs[10:14]
    own, extra, messages = refs[14], refs[15], refs[16 : 15 + levels]
    right, moved, held, whole, sems = refs[15 + levels :]
    chunk = right.shape[1] // levels
    acts = turn_late(rows, acts, early, bases, pieces, sums, right, moved, held, sems, extra)
    whole[...] = chunk_of(right, slice(None), acts, rows)
    own[...] = whole[pl.ds(pl.multiple_of(where[0] * chunk, chunk), chunk)]
    for step in range(1, levels):
        block = whole[pl.ds(pl.multiple_of((where[0] ^ step) * chunk, chunk), chunk)]
        messages[step - 1][...] = with_sums(block, extra)


GIVEN = [SMEM] + [VMEM] * 2 + [ANY] + [VMEM] + [ANY] * 2 + [VMEM] * 2 + [ANY] * 2 + [VMEM] * 4


def scratch(rows, width, width_g):
    return [pltpu.VMEM((rows, width), bf16), pltpu.VMEM((2 * split(rows)[1], width_g), bf16)]


def cross(where, acts, early, bases, pieces, sums, rows, levels):
    width_g, part = bases[0].shape
    width = acts[0].shape[1]
    cols = 2 * part
    chunk = cols // levels
    return pl.pallas_call(
        functools.partial(cross_kernel, levels, rows),
        out_shape=[shape((chunk, width), f32), shape((8, width), f32)]
        + [shape((chunk + 8, width), bf16)] * (levels - 1),
        in_specs=GIVEN,
        out_specs=[VMEM] * (1 + levels),
        scratch_shapes=[pltpu.VMEM((4 * rows, cols), bf16)]
        + scratch(rows, width, width_g)
        + [pltpu.VMEM((cols, width), f32), pltpu.SemaphoreType.DMA((15,))],
        compiler_params=params(LARGE),
        cost_estimate=cost(8 * rows * cols * width, 16 * rows * width),
    )(where, *acts, *early, *bases, *pieces, *sums)


def far_kernel(levels, rows, where, *refs):
    acts, early, bases, pieces, sums = refs[:4], refs[4:6], refs[6:8], refs[8:10], refs[10:14]
    message, extra, right, moved, held, sems = refs[14:]
    chunk = right.shape[1] // levels
    acts = turn_late(rows, acts, early, bases, pieces, sums, right, moved, held, sems, extra)
    columns = pl.ds(pl.multiple_of((where[0] ^ 2) * chunk, chunk), chunk)
    message[...] = with_sums(chunk_of(right, columns, acts, rows), extra)


def far(where, acts, early, bases, pieces, sums, rows, levels):
    width_g, part = bases[0].shape
    width = acts[0].shape[1]
    cols = 2 * part
    chunk = cols // levels
    return pl.pallas_call(
        functools.partial(far_kernel, levels, rows),
        out_shape=(shape((chunk + 8, width), bf16), shape((8, width), f32), shape((4 * rows, cols), bf16)),
        in_specs=GIVEN,
        out_specs=(VMEM,) * 3,
        scratch_shapes=scratch(rows, width, width_g) + [pltpu.SemaphoreType.DMA((15,))],
        compiler_params=params(LARGE),
        cost_estimate=cost(2 * rows * cols * width, 16 * rows * width),
    )(where, *acts, *early, *bases, *pieces, *sums)


def near_kernel(levels, rows, where, right, extra, *refs):
    acts, own, message, kept = refs[:4], refs[4], refs[5], refs[6]
    chunk = right.shape[1] // levels
    for step, target in ((0, own), (1, message), (3, kept)):
        columns = pl.ds(pl.multiple_of((where[0] ^ step) * chunk, chunk), chunk)
        block = chunk_of(right, columns, acts, rows)
        target[...] = with_sums(block, extra) if step == 1 else block


def near(where, right, extra, acts, rows, levels):
    width = acts[0].shape[1]
    chunk = right.shape[1] // levels
    return pl.pallas_call(
        functools.partial(near_kernel, levels, rows),
        out_shape=(shape((chunk, width), f32), shape((chunk + 8, width), bf16), shape((chunk, width), f32)),
        in_specs=[SMEM] + [VMEM] * 6,
        out_specs=(VMEM,) * 3,
        compiler_params=params(LARGE),
        cost_estimate=cost(24 * rows * chunk * width, 16 * rows * width),
    )(where, right, extra, *acts)


def add_kernel(kept, extra, got, out):
    chunk = kept.shape[0]
    more = got[...].astype(f32)
    high, low = high_low(extra[0:4] + (more[chunk : chunk + 4] + more[chunk + 4 :]))
    out[...] = jnp.concatenate([(kept[...] + more[:chunk]).astype(bf16), high, low])


def add(kept, extra, got):
    return pl.pallas_call(
        add_kernel,
        out_shape=shape(got.shape, bf16),
        in_specs=[VMEM] * 3,
        out_specs=VMEM,
        compiler_params=params(SMALL),
        cost_estimate=cost(kept.size, 8 * kept.size),
    )(kept, extra, got)


def middle_kernel(levels, where, own, own_extra, *refs):
    count = len(refs) - levels - 6
    messages, bases, outs = refs[:count], refs[count : count + 4], refs[count + 4 : -2]
    basis, turned = refs[-2:]
    chunk, width = own.shape
    cols = chunk * levels
    part = bases[0].shape[1]
    for i, b in enumerate(bases):
        basis[:, pl.ds(i * part, part)] = b[...]
    total = own[...]
    extra = own_extra[...]
    for message in messages:
        part_sum = message[...].astype(f32)
        total = total + part_sum[:chunk]
        more = part_sum[chunk:]
        extra = extra + jnp.concatenate([more[0:4] + more[4:8], jnp.zeros_like(more[:4])])
    count = extra[2:3]
    extra = extra / count
    lam_a = extra[1:2]
    turned[...] = jnp.transpose(extra[:, :cols])
    lam_g = turned[pl.ds(pl.multiple_of(where[0] * chunk, chunk), chunk)][:, 0:1]
    both = jnp.dot(jnp.concatenate(high_low(total)), basis[...], preferred_element_type=f32)
    rotated = (both[:chunk] + both[chunk:]) / count
    scaled = (rotated / (lam_g * lam_a + damping)).astype(bf16)
    height = width // levels
    for step, out in enumerate(outs):
        rows = pl.ds(pl.multiple_of((where[0] ^ step) * height, height), height)
        out[...] = lax.dot_general(
            scaled, basis[rows], (((1,), (1,)), ((), ())), preferred_element_type=f32
        ).astype(bf16)


def middle(where, own, own_extra, messages, bases, levels):
    chunk, width = own.shape
    return pl.pallas_call(
        functools.partial(middle_kernel, levels),
        out_shape=[shape((chunk, width // levels), bf16)] * levels,
        in_specs=[SMEM] + [VMEM] * (len(messages) + 6),
        out_specs=[VMEM] * levels,
        scratch_shapes=[pltpu.VMEM((width, width), bf16), pltpu.VMEM((chunk * levels, 8), f32)],
        compiler_params=params(SMALL),
        cost_estimate=cost(6 * chunk * width * width, 2 * width * width),
    )(where, own, own_extra, *messages, *bases)


def result_kernel(levels, where, *refs):
    slots = refs[:levels]
    one, two, outs, (mid, whole) = refs[levels], refs[levels + 1], refs[levels + 2 : -2], refs[-2:]
    chunk, height = slots[0].shape
    wide, part = one.shape
    for step, slot in enumerate(slots):
        mid[pl.ds(pl.multiple_of((where[0] ^ step) * chunk, chunk), chunk)] = slot[...]
    quarter = wide // 4
    for j in range(4):
        columns = pl.ds(j * quarter, quarter)
        whole[:, columns] = sum(
            lax.dot_general(
                mid[pl.ds(i * part, part)], b[columns], (((0,), (1,)), ((), ())), preferred_element_type=f32
            )
            for i, b in enumerate((one, two))
        )
    rows = height // 4
    for other, out in zip((3, 1, 2, 0), outs):
        out[...] = whole[pl.ds(pl.multiple_of((where[1] ^ other) * rows, rows), rows)].astype(out.dtype)


def result(where, slots, bases):
    levels = len(slots)
    chunk, height = slots[0].shape
    wide, part = bases[0].shape
    return pl.pallas_call(
        functools.partial(result_kernel, levels),
        out_shape=[shape((height // 4, wide), t) for t in (bf16, bf16, f32, f32)],
        in_specs=[SMEM] + [VMEM] * (levels + 2),
        out_specs=[VMEM] * 4,
        scratch_shapes=[
            pltpu.VMEM((2 * part, height), bf16),
            pltpu.VMEM((height, wide), f32),
        ],
        compiler_params=params(SMALL),
        cost_estimate=cost(4 * height * part * wide, 4 * wide * part),
    )(where, *slots, *bases)


def gather_levels(unit, level, levels, ready):
    def over(slot):
        return lax.ppermute(slot, "group", SWAP)

    if levels != 4:
        slots = [unit] + [across(unit, step, levels) for step in range(1, levels)]
        return slots, [over(slot) for slot in slots], ready
    middle = (level == 1) | (level == 2)
    together = lax.optimization_barrier
    inner = lax.ppermute(unit, "level", [(1, 2), (2, 1)])
    first, inner, other0, ready = together((across(unit, 1, levels), inner, over(unit), ready))
    held, inner = together((unit, inner))
    outer, other1 = together((lax.ppermute(held, "level", [(0, 3), (3, 0)]), over(first)))
    third = jnp.where(middle, inner, outer)
    second, other3 = together((across(third, 1, levels), over(third)))
    return [unit, first, second, third], [other0, other1, over(second), other3], ready


def body(acts, grads, counts, basis_a, basis_g):
    group, level, chip, core = (lax.axis_index(n) for n in ("group", "level", "chip", "core"))
    levels = lax.axis_size("level")
    rows, width_a = acts.shape
    width_g = grads.shape[1]
    rows_a, rows_g = basis_a.shape[0], basis_g.shape[0]
    part_a, part_g = width_a // 4, width_g // 8
    where = jnp.stack([level, chip * 2 + core]).astype(jnp.int32)

    def columns(y, c):
        return jnp.concatenate(
            [
                cut(basis_g, ((y * 2 + c) * 2 + group) * part_g, part_g, 1),
                cut(basis_a, (c * 2 + group) * part_a, part_a, 1),
            ]
        )

    def diagonal(x):
        return lax.ppermute(x, ("chip", "core"), [(i, 3 - i) for i in range(4)])

    beyond = [lax.ppermute(columns(1 - chip, core), "chip", SWAP), diagonal(columns(1 - chip, 1 - core))]
    beside = lax.ppermute(columns(chip, 1 - core), "core", SWAP)
    blocks = jnp.stack([columns(chip, core), beside] + beyond)
    blocks = [lax.dynamic_index_in_dim(blocks, j ^ (chip * 2 + core), 0, False) for j in range(4)]
    unit = jnp.concatenate([b[:rows_g] for b in blocks] + [b[rows_g:] for b in blocks])
    level_g, level_a = 4 * rows_g, 4 * rows_a

    valid = counts[0]
    keep = jnp.arange(rows, dtype=jnp.int32)[:, None] < valid
    half = split(rows)[0]
    later, _ = lax.optimization_barrier((grads, unit))
    slots, others, late = gather_levels(unit, level, levels, jnp.where(keep[half:], later[half:], 0))
    marks = jnp.stack([valid // 16 * 16, valid % 16]).astype(bf16)
    marks = jnp.broadcast_to(jnp.pad(marks, (0, 14))[:, None], (16, width_a))
    early = jnp.where(keep[:half], grads[:half], 0)
    early = jnp.concatenate([jnp.where(keep, acts, 0), marks, early[:, :width_a], early[:, width_a:]])
    early_out, _ = lax.optimization_barrier((early, beyond[0]))

    together = lax.optimization_barrier
    far_rows, slots[2] = together((lax.ppermute(early_out, "chip", SWAP), slots[2]))
    early = [early, lax.ppermute(early, "core", SWAP), far_rows, lax.ppermute(far_rows, "core", SWAP)]
    later = [late, lax.ppermute(late, "core", SWAP)]
    first = turn(where, slots, early, later, rows, level_g, level_a)
    others[2], first = together((others[2], first))
    second = turn(where, others, early, later, rows, level_g, level_a)
    far_rows, second = together((lax.ppermute(late, "chip", SWAP), second))
    late = [far_rows, lax.ppermute(far_rows, "core", SWAP)]
    bases_a, turned_g, bases_g, sums = zip(first, second)
    sums += tuple(lax.ppermute(t, "core", SWAP) for t in sums)
    bases_a += tuple(lax.ppermute(t, "core", SWAP) for t in bases_a)

    if levels == 4:
        message, own_extra, right = far(where, early, turned_g, bases_g, late, sums, rows, levels)
        message = across(message, 1, levels)
        own, beside, kept = near(where, right, own_extra, early, rows, levels)
        got = [across(add(kept, own_extra, message), 3, levels), across(beside, 1, levels)]
    else:
        own, own_extra, *messages = cross(where, early, turned_g, bases_g, late, sums, rows, levels)
        got = [across(m, step + 1, levels) for step, m in enumerate(messages)]
    mids = middle(where, own, own_extra, got, bases_a, levels)
    mids = [m if step == 0 else across(m, step, levels) for step, m in enumerate(mids)]

    *sent, far_kept, near_kept = result(where, mids, bases_g)
    far_sent, near_sent = (lax.ppermute(x, "core", SWAP).astype(f32) for x in sent)
    last = lax.ppermute((far_kept + far_sent).astype(bf16), "chip", SWAP)
    return (near_kept + near_sent + last.astype(f32)).astype(bf16)


def solution(mesh):
    groups, samples = mesh.shape["groups"], mesh.shape["samples"]
    grid = Mesh(mesh.devices.reshape(groups, samples // 4, 2, 2), ("group", "level", "chip", "core"))
    every = ("group", "level", "chip", "core")
    in_specs = (
        P(every, None),
        P(every, None),
        P(every),
        P(every[1:], None),
        P(every[1:], None),
    )
    return jax.shard_map(body, mesh=grid, in_specs=in_specs, out_specs=P(every, None), check_vma=False)
```

```python
import functools

import jax
import jax.numpy as jnp
from jax import lax
from jax.experimental import pallas as pl
from jax.experimental.pallas import tpu as pltpu
from jax.sharding import Mesh, PartitionSpec as P

damping = 0.01
bf16 = jnp.bfloat16
f32 = jnp.float32
SWAP = [(0, 1), (1, 0)]
ANY = pl.BlockSpec(memory_space=pl.ANY)
VMEM = pl.BlockSpec(memory_space=pltpu.VMEM)
SMEM = pl.BlockSpec(memory_space=pltpu.SMEM)
LARGE = 18 * 2**20
MIDDLE = 16 * 2**20
SMALL = 12 * 2**20


def params(limit):
    return pltpu.CompilerParams(vmem_limit_bytes=limit)


def cost(flops, moved):
    return pl.CostEstimate(flops=flops, bytes_accessed=moved, transcendentals=0)


def shape(dims, dtype):
    return jax.ShapeDtypeStruct(dims, dtype)


def cut(x, first, size, axis=0):
    return lax.dynamic_slice_in_dim(x, first, size, axis)


def across(x, step, levels):
    return lax.ppermute(x, "level", [(i, i ^ step) for i in range(levels)])


def split(rows):
    return rows * 5 // 8, rows - rows * 5 // 8


def turn_kernel(levels, level_g, level_a, rows, where, *refs):
    slots, pieces, later = refs[:levels], list(refs[levels : levels + 4]), refs[levels + 4 : levels + 6]
    basis_a, out_g, basis_g, sums, held, held_sem, sems = refs[levels + 6 :]
    (half, late), width = split(rows), basis_a.shape[0]
    part = basis_a.shape[1]
    move = pltpu.make_async_copy(pieces[2], held, held_sem)
    pieces[2] = held
    copies = []
    for i, (first, height, target) in enumerate(((level_g, level_a, basis_a), (0, level_g, basis_g))):
        for step, slot in enumerate(slots):
            row = pl.multiple_of((where[0] ^ step) * height, height)
            copy = pltpu.make_async_copy(
                slot.at[pl.ds(first, height)], target.at[pl.ds(row, height)], sems.at[i * levels + step]
            )
            copy.start()
            copies.append(copy)
    move.start()

    def squares(x):
        return jnp.sum(jnp.square(x.astype(f32)), axis=0, keepdims=True)

    def turn_a(piece):
        return squares(jnp.dot(piece[:rows], basis_a[...], preferred_element_type=f32).astype(bf16))

    def turn_g(i):
        turned = sum(
            jnp.dot(
                pieces[i][pl.ds(rows + 16 + j * half, half)],
                basis_g[pl.ds(j * width, width)],
                preferred_element_type=f32,
            )
            for j in range(2)
        ).astype(bf16)
        out_g[pl.ds(i * half, half)] = turned
        return squares(turned)

    for copy in copies[:levels]:
        copy.wait()
    total_a = sum(turn_a(pieces[i]) for i in (0, 1, 3))
    for copy in copies[levels:]:
        copy.wait()
    total_g = sum(turn_g(i) for i in (0, 1, 3))
    for i, piece in enumerate(later):
        turned = jnp.dot(piece[...], basis_g[...], preferred_element_type=f32).astype(bf16)
        out_g[pl.ds(4 * half + i * late, late)] = turned
        total_g = total_g + squares(turned)
    move.wait()
    marks = sum(piece[rows : rows + 16, :part].astype(f32) for piece in pieces)
    sums[0:1] = total_g + turn_g(2)
    sums[1:2] = marks[0:1] + marks[1:2]
    sums[2:3] = total_a + turn_a(held)
    sums[3:8] = jnp.zeros((5, part), f32)


def turn(where, slots, pieces, later, rows, level_g, level_a):
    levels = len(slots)
    width_a, width_g = levels * level_a, levels * level_g
    part = slots[0].shape[1]
    half, late = split(rows)
    return pl.pallas_call(
        functools.partial(turn_kernel, levels, level_g, level_a, rows),
        out_shape=(
            shape((width_a, part), bf16),
            shape((4 * half + 2 * late, part), bf16),
            shape((width_g, part), bf16),
            shape((8, part), f32),
        ),
        in_specs=[SMEM] + [ANY] * levels + [VMEM] * 2 + [ANY] + [VMEM] * 3,
        out_specs=(VMEM,) * 4,
        scratch_shapes=[
            pltpu.VMEM(pieces[2].shape, bf16),
            pltpu.SemaphoreType.DMA,
            pltpu.SemaphoreType.DMA((2 * levels,)),
        ],
        compiler_params=params(MIDDLE),
        cost_estimate=cost(8 * rows * part * (width_a + width_g // 2), 8 * rows * (width_a + width_g // 2)),
    )(where, *slots, *pieces, *later)


def high_low(v):
    high = v.astype(bf16)
    return high, (v - high.astype(f32)).astype(bf16)


def turn_other_kernel(rows, one, two, out, sums):
    part = one.shape[1]
    sums[...] = jnp.zeros_like(sums)
    for i, basis in enumerate((one, two)):
        columns = pl.ds(i * part, part)
        turned = jnp.dot(rows[...], basis[...], preferred_element_type=f32).astype(bf16)
        out[:, columns] = turned
        sums[0:1, columns] = jnp.sum(jnp.square(turned.astype(f32)), axis=0, keepdims=True)


def turn_other(rows, bases):
    height, width = rows.shape
    part = bases[0].shape[1]
    return pl.pallas_call(
        turn_other_kernel,
        out_shape=(shape((height, 2 * part), bf16), shape((8, 2 * part), f32)),
        in_specs=[VMEM] * 3,
        out_specs=(VMEM, VMEM),
        compiler_params=params(SMALL),
        cost_estimate=cost(4 * height * part * width, 2 * height * width),
    )(rows, *bases)


def turn_late(rows, acts, early, bases, pieces, sums, right, moved, sems, extra):
    half, late = split(rows)
    part = bases[0].shape[1]
    count = 0

    def copy(source, target):
        nonlocal count
        made = pltpu.make_async_copy(source, target, sems.at[count])
        made.start()
        count += 1
        return made

    last, other, other_sums = pieces
    rest = [copy(acts[2].at[pl.ds(0, rows)], moved), copy(other, right.at[pl.ds(2 * rows + half, late)])]
    for i in range(2):
        columns = pl.ds(i * part, part)
        for j in range(4):
            rest.append(copy(early[i].at[pl.ds(j * half, half)], right.at[pl.ds(j * rows, half), columns]))
        for j in range(2):
            source = early[i].at[pl.ds(4 * half + j * late, late)]
            rest.append(copy(source, right.at[pl.ds(j * rows + half, late), columns]))
    extra[...] = jnp.zeros_like(extra)
    for i in range(4):
        extra[1:2, pl.ds(i * part, part)] = sums[i][2:3]
        extra[2:3, pl.ds(i * part, part)] = sums[i][1:2]
    for i, basis in enumerate(bases):
        columns = pl.ds(i * part, part)
        block = jnp.dot(last[...], basis[...], preferred_element_type=f32).astype(bf16)
        right[pl.ds(3 * rows + half, late), columns] = block
        total = sums[i][0:1] + other_sums[0:1, columns]
        extra[0:1, columns] = total + jnp.sum(jnp.square(block.astype(f32)), axis=0, keepdims=True)
    for made in rest:
        made.wait()
    return acts[0], acts[1], moved, acts[3]


def chunk_of(right, columns, acts, rows):
    return sum(
        lax.dot_general(
            right[pl.ds(i * rows, rows), columns], a[:rows], (((0,), (0,)), ((), ())), preferred_element_type=f32
        )
        for i, a in enumerate(acts)
    )


def with_sums(block, sums):
    high, low = high_low(sums[0:4])
    return jnp.concatenate([block.astype(bf16), high, low])


def cross_kernel(levels, rows, where, *refs):
    acts, early, bases, pieces, sums = refs[:4], refs[4:6], refs[6:8], refs[8:11], refs[11:15]
    own, extra, messages = refs[15], refs[16], refs[17 : 16 + levels]
    right, moved, whole, sems = refs[16 + levels :]
    chunk = right.shape[1] // levels
    acts = turn_late(rows, acts, early, bases, pieces, sums, right, moved, sems, extra)
    whole[...] = chunk_of(right, slice(None), acts, rows)
    own[...] = whole[pl.ds(pl.multiple_of(where[0] * chunk, chunk), chunk)]
    for step in range(1, levels):
        block = whole[pl.ds(pl.multiple_of((where[0] ^ step) * chunk, chunk), chunk)]
        messages[step - 1][...] = with_sums(block, extra)


GIVEN = [SMEM] + [VMEM] * 2 + [ANY] + [VMEM] + [ANY] * 2 + [VMEM] * 3 + [ANY] + [VMEM] * 5


def cross(where, acts, early, bases, pieces, sums, rows, levels):
    part = bases[0].shape[1]
    width = acts[0].shape[1]
    cols = 2 * part
    chunk = cols // levels
    return pl.pallas_call(
        functools.partial(cross_kernel, levels, rows),
        out_shape=[shape((chunk, width), f32), shape((8, width), f32)]
        + [shape((chunk + 8, width), bf16)] * (levels - 1),
        in_specs=GIVEN,
        out_specs=[VMEM] * (1 + levels),
        scratch_shapes=[
            pltpu.VMEM((4 * rows, cols), bf16),
            pltpu.VMEM((rows, width), bf16),
            pltpu.VMEM((cols, width), f32),
            pltpu.SemaphoreType.DMA((14,)),
        ],
        compiler_params=params(LARGE),
        cost_estimate=cost(8 * rows * cols * width, 16 * rows * width),
    )(where, *acts, *early, *bases, *pieces, *sums)


def far_kernel(levels, rows, where, *refs):
    acts, early, bases, pieces, sums = refs[:4], refs[4:6], refs[6:8], refs[8:11], refs[11:15]
    message, extra, right, moved, sems = refs[15:]
    chunk = right.shape[1] // levels
    acts = turn_late(rows, acts, early, bases, pieces, sums, right, moved, sems, extra)
    columns = pl.ds(pl.multiple_of((where[0] ^ 2) * chunk, chunk), chunk)
    message[...] = with_sums(chunk_of(right, columns, acts, rows), extra)


def far(where, acts, early, bases, pieces, sums, rows, levels):
    part = bases[0].shape[1]
    width = acts[0].shape[1]
    cols = 2 * part
    chunk = cols // levels
    return pl.pallas_call(
        functools.partial(far_kernel, levels, rows),
        out_shape=(shape((chunk + 8, width), bf16), shape((8, width), f32), shape((4 * rows, cols), bf16)),
        in_specs=GIVEN,
        out_specs=(VMEM,) * 3,
        scratch_shapes=[pltpu.VMEM((rows, width), bf16), pltpu.SemaphoreType.DMA((14,))],
        compiler_params=params(LARGE),
        cost_estimate=cost(2 * rows * cols * width, 16 * rows * width),
    )(where, *acts, *early, *bases, *pieces, *sums)


def near_kernel(levels, rows, where, right, extra, *refs):
    acts, own, message, kept = refs[:4], refs[4], refs[5], refs[6]
    chunk = right.shape[1] // levels
    for step, target in ((0, own), (1, message), (3, kept)):
        columns = pl.ds(pl.multiple_of((where[0] ^ step) * chunk, chunk), chunk)
        block = chunk_of(right, columns, acts, rows)
        target[...] = with_sums(block, extra) if step == 1 else block


def near(where, right, extra, acts, rows, levels):
    width = acts[0].shape[1]
    chunk = right.shape[1] // levels
    return pl.pallas_call(
        functools.partial(near_kernel, levels, rows),
        out_shape=(shape((chunk, width), f32), shape((chunk + 8, width), bf16), shape((chunk, width), f32)),
        in_specs=[SMEM] + [VMEM] * 6,
        out_specs=(VMEM,) * 3,
        compiler_params=params(LARGE),
        cost_estimate=cost(24 * rows * chunk * width, 16 * rows * width),
    )(where, right, extra, *acts)


def add_kernel(kept, extra, got, out):
    chunk = kept.shape[0]
    more = got[...].astype(f32)
    high, low = high_low(extra[0:4] + (more[chunk : chunk + 4] + more[chunk + 4 :]))
    out[...] = jnp.concatenate([(kept[...] + more[:chunk]).astype(bf16), high, low])


def add(kept, extra, got):
    return pl.pallas_call(
        add_kernel,
        out_shape=shape(got.shape, bf16),
        in_specs=[VMEM] * 3,
        out_specs=VMEM,
        compiler_params=params(SMALL),
        cost_estimate=cost(kept.size, 8 * kept.size),
    )(kept, extra, got)


def middle_kernel(levels, where, own, own_extra, *refs):
    count = len(refs) - levels - 6
    messages, bases, outs = refs[:count], refs[count : count + 4], refs[count + 4 : -2]
    basis, turned = refs[-2:]
    chunk, width = own.shape
    cols = chunk * levels
    part = bases[0].shape[1]
    for i, b in enumerate(bases):
        basis[:, pl.ds(i * part, part)] = b[...]
    total = own[...]
    extra = own_extra[...]
    for message in messages:
        part_sum = message[...].astype(f32)
        total = total + part_sum[:chunk]
        more = part_sum[chunk:]
        extra = extra + jnp.concatenate([more[0:4] + more[4:8], jnp.zeros_like(more[:4])])
    count = extra[2:3]
    extra = extra / count
    lam_a = extra[1:2]
    turned[...] = jnp.transpose(extra[:, :cols])
    lam_g = turned[pl.ds(pl.multiple_of(where[0] * chunk, chunk), chunk)][:, 0:1]
    both = jnp.dot(jnp.concatenate(high_low(total)), basis[...], preferred_element_type=f32)
    rotated = (both[:chunk] + both[chunk:]) / count
    scaled = (rotated / (lam_g * lam_a + damping)).astype(bf16)
    height = width // levels
    for step, out in enumerate(outs):
        rows = pl.ds(pl.multiple_of((where[0] ^ step) * height, height), height)
        out[...] = lax.dot_general(
            scaled, basis[rows], (((1,), (1,)), ((), ())), preferred_element_type=f32
        ).astype(bf16)


def middle(where, own, own_extra, messages, bases, levels):
    chunk, width = own.shape
    return pl.pallas_call(
        functools.partial(middle_kernel, levels),
        out_shape=[shape((chunk, width // levels), bf16)] * levels,
        in_specs=[SMEM] + [VMEM] * (len(messages) + 6),
        out_specs=[VMEM] * levels,
        scratch_shapes=[pltpu.VMEM((width, width), bf16), pltpu.VMEM((chunk * levels, 8), f32)],
        compiler_params=params(SMALL),
        cost_estimate=cost(6 * chunk * width * width, 2 * width * width),
    )(where, own, own_extra, *messages, *bases)


def result_kernel(levels, where, *refs):
    slots = refs[:levels]
    one, two, outs, (mid, whole) = refs[levels], refs[levels + 1], refs[levels + 2 : -2], refs[-2:]
    chunk, height = slots[0].shape
    wide, part = one.shape
    for step, slot in enumerate(slots):
        mid[pl.ds(pl.multiple_of((where[0] ^ step) * chunk, chunk), chunk)] = slot[...]
    quarter = wide // 4
    for j in range(4):
        columns = pl.ds(j * quarter, quarter)
        whole[:, columns] = sum(
            lax.dot_general(
                mid[pl.ds(i * part, part)], b[columns], (((0,), (1,)), ((), ())), preferred_element_type=f32
            )
            for i, b in enumerate((one, two))
        )
    rows = height // 4
    for other, out in zip((3, 1, 2, 0), outs):
        out[...] = whole[pl.ds(pl.multiple_of((where[1] ^ other) * rows, rows), rows)].astype(out.dtype)


def result(where, slots, bases):
    levels = len(slots)
    chunk, height = slots[0].shape
    wide, part = bases[0].shape
    return pl.pallas_call(
        functools.partial(result_kernel, levels),
        out_shape=[shape((height // 4, wide), t) for t in (bf16, bf16, f32, f32)],
        in_specs=[SMEM] + [VMEM] * (levels + 2),
        out_specs=[VMEM] * 4,
        scratch_shapes=[
            pltpu.VMEM((2 * part, height), bf16),
            pltpu.VMEM((height, wide), f32),
        ],
        compiler_params=params(SMALL),
        cost_estimate=cost(4 * height * part * wide, 4 * wide * part),
    )(where, *slots, *bases)


def gather_levels(unit, level, levels, ready):
    def over(slot):
        return lax.ppermute(slot, "group", SWAP)

    if levels != 4:
        slots = [unit] + [across(unit, step, levels) for step in range(1, levels)]
        return slots, [over(slot) for slot in slots], ready
    middle = (level == 1) | (level == 2)
    together = lax.optimization_barrier
    inner = lax.ppermute(unit, "level", [(1, 2), (2, 1)])
    first, inner, other0, ready = together((across(unit, 1, levels), inner, over(unit), ready))
    held, inner = together((unit, inner))
    outer, other1 = together((lax.ppermute(held, "level", [(0, 3), (3, 0)]), over(first)))
    third = jnp.where(middle, inner, outer)
    second, other3 = together((across(third, 1, levels), over(third)))
    return [unit, first, second, third], [other0, other1, over(second), other3], ready


def body(acts, grads, counts, basis_a, basis_g):
    group, level, chip, core = (lax.axis_index(n) for n in ("group", "level", "chip", "core"))
    levels = lax.axis_size("level")
    rows, width_a = acts.shape
    width_g = grads.shape[1]
    rows_a, rows_g = basis_a.shape[0], basis_g.shape[0]
    part_a, part_g = width_a // 4, width_g // 8
    where = jnp.stack([level, chip * 2 + core]).astype(jnp.int32)

    def columns(y, c):
        return jnp.concatenate(
            [
                cut(basis_g, ((y * 2 + c) * 2 + group) * part_g, part_g, 1),
                cut(basis_a, (c * 2 + group) * part_a, part_a, 1),
            ]
        )

    def diagonal(x):
        return lax.ppermute(x, ("chip", "core"), [(i, 3 - i) for i in range(4)])

    beyond = [lax.ppermute(columns(1 - chip, core), "chip", SWAP), diagonal(columns(1 - chip, 1 - core))]
    beside = lax.ppermute(columns(chip, 1 - core), "core", SWAP)
    blocks = jnp.stack([columns(chip, core), beside] + beyond)
    blocks = [lax.dynamic_index_in_dim(blocks, j ^ (chip * 2 + core), 0, False) for j in range(4)]
    unit = jnp.concatenate([b[:rows_g] for b in blocks] + [b[rows_g:] for b in blocks])
    level_g, level_a = 4 * rows_g, 4 * rows_a

    valid = counts[0]
    keep = jnp.arange(rows, dtype=jnp.int32)[:, None] < valid
    half = split(rows)[0]
    later, _ = lax.optimization_barrier((grads, unit))
    slots, others, late = gather_levels(unit, level, levels, jnp.where(keep[half:], later[half:], 0))
    marks = jnp.stack([valid // 16 * 16, valid % 16]).astype(bf16)
    marks = jnp.broadcast_to(jnp.pad(marks, (0, 14))[:, None], (16, width_a))
    early = jnp.where(keep[:half], grads[:half], 0)
    early = jnp.concatenate([jnp.where(keep, acts, 0), marks, early[:, :width_a], early[:, width_a:]])
    early_out, _ = lax.optimization_barrier((early, beyond[0]))

    together = lax.optimization_barrier
    far_rows, slots[2] = together((lax.ppermute(early_out, "chip", SWAP), slots[2]))
    early = [early, lax.ppermute(early, "core", SWAP), far_rows, lax.ppermute(far_rows, "core", SWAP)]
    later = [late, lax.ppermute(late, "core", SWAP)]
    first = turn(where, slots, early, later, rows, level_g, level_a)
    first_sums = lax.ppermute(first[3], "core", SWAP)
    others[2], first, first_sums = together((others[2], first, first_sums))
    second = turn(where, others, early, later, rows, level_g, level_a)
    far_rows, second = together((lax.ppermute(late, "chip", SWAP), second))
    bases_a, turned_g, bases_g, sums = zip(first, second)
    late = [lax.ppermute(far_rows, "core", SWAP), *turn_other(far_rows, bases_g)]
    sums += (first_sums, lax.ppermute(sums[1], "core", SWAP))
    bases_a += tuple(lax.ppermute(t, "core", SWAP) for t in bases_a)

    if levels == 4:
        message, own_extra, right = far(where, early, turned_g, bases_g, late, sums, rows, levels)
        message = across(message, 1, levels)
        own, beside, kept = near(where, right, own_extra, early, rows, levels)
        got = [across(add(kept, own_extra, message), 3, levels), across(beside, 1, levels)]
    else:
        own, own_extra, *messages = cross(where, early, turned_g, bases_g, late, sums, rows, levels)
        got = [across(m, step + 1, levels) for step, m in enumerate(messages)]
    mids = middle(where, own, own_extra, got, bases_a, levels)
    mids = [m if step == 0 else across(m, step, levels) for step, m in enumerate(mids)]

    *sent, far_kept, near_kept = result(where, mids, bases_g)
    far_sent, near_sent = (lax.ppermute(x, "core", SWAP).astype(f32) for x in sent)
    last = lax.ppermute((far_kept + far_sent).astype(bf16), "chip", SWAP)
    return (near_kept + near_sent + last.astype(f32)).astype(bf16)


def solution(mesh):
    groups, samples = mesh.shape["groups"], mesh.shape["samples"]
    grid = Mesh(mesh.devices.reshape(groups, samples // 4, 2, 2), ("group", "level", "chip", "core"))
    every = ("group", "level", "chip", "core")
    in_specs = (
        P(every, None),
        P(every, None),
        P(every),
        P(every[1:], None),
        P(every[1:], None),
    )
    return jax.shard_map(body, mesh=grid, in_specs=in_specs, out_specs=P(every, None), check_vma=False)
```

```python
import functools

import jax
import jax.numpy as jnp
from jax import lax
from jax.experimental import pallas as pl
from jax.experimental.pallas import tpu as pltpu
from jax.sharding import Mesh, PartitionSpec as P

damping = 0.01
bf16 = jnp.bfloat16
f32 = jnp.float32
SWAP = [(0, 1), (1, 0)]
ANY = pl.BlockSpec(memory_space=pl.ANY)
VMEM = pl.BlockSpec(memory_space=pltpu.VMEM)
SMEM = pl.BlockSpec(memory_space=pltpu.SMEM)
LARGE = 18 * 2**20
MIDDLE = 16 * 2**20
SMALL = 12 * 2**20


def params(limit):
    return pltpu.CompilerParams(vmem_limit_bytes=limit)


def cost(flops, moved):
    return pl.CostEstimate(flops=flops, bytes_accessed=moved, transcendentals=0)


def shape(dims, dtype):
    return jax.ShapeDtypeStruct(dims, dtype)


def cut(x, first, size, axis=0):
    return lax.dynamic_slice_in_dim(x, first, size, axis)


def across(x, step, levels):
    return lax.ppermute(x, "level", [(i, i ^ step) for i in range(levels)])


def split(rows):
    return rows * 5 // 8, rows - rows * 5 // 8


def turn_kernel(levels, level_g, level_a, rows, where, *refs):
    slots, pieces, later = refs[:levels], list(refs[levels : levels + 4]), refs[levels + 4 : levels + 6]
    basis_a, out_g, basis_g, sums, held, held_sem, sems = refs[levels + 6 :]
    (half, late), width = split(rows), basis_a.shape[0]
    part = basis_a.shape[1]
    move = pltpu.make_async_copy(pieces[2], held, held_sem)
    pieces[2] = held
    copies = []
    for i, (first, height, target) in enumerate(((level_g, level_a, basis_a), (0, level_g, basis_g))):
        for step, slot in enumerate(slots):
            row = pl.multiple_of((where[0] ^ step) * height, height)
            copy = pltpu.make_async_copy(
                slot.at[pl.ds(first, height)], target.at[pl.ds(row, height)], sems.at[i * levels + step]
            )
            copy.start()
            copies.append(copy)
    move.start()

    def squares(x):
        return jnp.sum(jnp.square(x.astype(f32)), axis=0, keepdims=True)

    def turn_a(piece):
        return squares(jnp.dot(piece[:rows], basis_a[...], preferred_element_type=f32).astype(bf16))

    def turn_g(i):
        turned = sum(
            jnp.dot(
                pieces[i][pl.ds(rows + 16 + j * half, half)],
                basis_g[pl.ds(j * width, width)],
                preferred_element_type=f32,
            )
            for j in range(2)
        ).astype(bf16)
        out_g[pl.ds(i * half, half)] = turned
        return squares(turned)

    for copy in copies[:levels]:
        copy.wait()
    total_a = sum(turn_a(pieces[i]) for i in (0, 1, 3))
    for copy in copies[levels:]:
        copy.wait()
    total_g = sum(turn_g(i) for i in (0, 1, 3))
    for i, piece in enumerate(later):
        turned = jnp.dot(piece[...], basis_g[...], preferred_element_type=f32).astype(bf16)
        out_g[pl.ds(4 * half + i * late, late)] = turned
        total_g = total_g + squares(turned)
    move.wait()
    marks = sum(piece[rows : rows + 16, :part].astype(f32) for piece in pieces)
    sums[0:1] = total_g + turn_g(2)
    sums[1:2] = marks[0:1] + marks[1:2]
    sums[2:3] = total_a + turn_a(held)
    sums[3:8] = jnp.zeros((5, part), f32)


def turn(where, slots, pieces, later, rows, level_g, level_a):
    levels = len(slots)
    width_a, width_g = levels * level_a, levels * level_g
    part = slots[0].shape[1]
    half, late = split(rows)
    return pl.pallas_call(
        functools.partial(turn_kernel, levels, level_g, level_a, rows),
        out_shape=(
            shape((width_a, part), bf16),
            shape((4 * half + 2 * late, part), bf16),
            shape((width_g, part), bf16),
            shape((8, part), f32),
        ),
        in_specs=[SMEM] + [ANY] * levels + [VMEM] * 2 + [ANY] + [VMEM] * 3,
        out_specs=(VMEM,) * 4,
        scratch_shapes=[
            pltpu.VMEM(pieces[2].shape, bf16),
            pltpu.SemaphoreType.DMA,
            pltpu.SemaphoreType.DMA((2 * levels,)),
        ],
        compiler_params=params(MIDDLE),
        cost_estimate=cost(8 * rows * part * (width_a + width_g // 2), 8 * rows * (width_a + width_g // 2)),
    )(where, *slots, *pieces, *later)


def high_low(v):
    high = v.astype(bf16)
    return high, (v - high.astype(f32)).astype(bf16)


def turn_other_kernel(rows, one, two, out, sums):
    part = one.shape[1]
    sums[...] = jnp.zeros_like(sums)
    for i, basis in enumerate((one, two)):
        columns = pl.ds(i * part, part)
        turned = jnp.dot(rows[...], basis[...], preferred_element_type=f32).astype(bf16)
        out[:, columns] = turned
        sums[0:1, columns] = jnp.sum(jnp.square(turned.astype(f32)), axis=0, keepdims=True)


def turn_other(rows, bases):
    height, width = rows.shape
    part = bases[0].shape[1]
    return pl.pallas_call(
        turn_other_kernel,
        out_shape=(shape((height, 2 * part), bf16), shape((8, 2 * part), f32)),
        in_specs=[VMEM] * 3,
        out_specs=(VMEM, VMEM),
        compiler_params=params(SMALL),
        cost_estimate=cost(4 * height * part * width, 2 * height * width),
    )(rows, *bases)


def turn_late(rows, acts, early, bases, pieces, sums, right, moved, sems, extra):
    half, late = split(rows)
    part = bases[0].shape[1]
    count = 0

    def copy(source, target):
        nonlocal count
        made = pltpu.make_async_copy(source, target, sems.at[count])
        made.start()
        count += 1
        return made

    last, other, other_sums = pieces
    rest = [copy(acts[2].at[pl.ds(0, rows)], moved), copy(other, right.at[pl.ds(2 * rows + half, late)])]
    for i in range(2):
        columns = pl.ds(i * part, part)
        for j in range(4):
            rest.append(copy(early[i].at[pl.ds(j * half, half)], right.at[pl.ds(j * rows, half), columns]))
        for j in range(2):
            source = early[i].at[pl.ds(4 * half + j * late, late)]
            rest.append(copy(source, right.at[pl.ds(j * rows + half, late), columns]))
    extra[...] = jnp.zeros_like(extra)
    for i in range(4):
        extra[1:2, pl.ds(i * part, part)] = sums[i][2:3]
        extra[2:3, pl.ds(i * part, part)] = sums[i][1:2]
    for i, basis in enumerate(bases):
        columns = pl.ds(i * part, part)
        block = jnp.dot(last[...], basis[...], preferred_element_type=f32).astype(bf16)
        right[pl.ds(3 * rows + half, late), columns] = block
        total = sums[i][0:1] + other_sums[0:1, columns]
        extra[0:1, columns] = total + jnp.sum(jnp.square(block.astype(f32)), axis=0, keepdims=True)
    for made in rest:
        made.wait()
    return acts[0], acts[1], moved, acts[3]


def chunk_of(right, columns, acts, rows):
    return sum(
        lax.dot_general(
            right[pl.ds(i * rows, rows), columns], a[:rows], (((0,), (0,)), ((), ())), preferred_element_type=f32
        )
        for i, a in enumerate(acts)
    )


def with_sums(block, sums):
    high, low = high_low(sums[0:4])
    return jnp.concatenate([block.astype(bf16), high, low])


def cross_kernel(levels, rows, where, *refs):
    acts, early, bases, pieces, sums = refs[:4], refs[4:6], refs[6:8], refs[8:11], refs[11:15]
    own, extra, messages = refs[15], refs[16], refs[17 : 16 + levels]
    right, moved, whole, sems = refs[16 + levels :]
    chunk = right.shape[1] // levels
    acts = turn_late(rows, acts, early, bases, pieces, sums, right, moved, sems, extra)
    whole[...] = chunk_of(right, slice(None), acts, rows)
    own[...] = whole[pl.ds(pl.multiple_of(where[0] * chunk, chunk), chunk)]
    for step in range(1, levels):
        block = whole[pl.ds(pl.multiple_of((where[0] ^ step) * chunk, chunk), chunk)]
        messages[step - 1][...] = with_sums(block, extra)


GIVEN = [SMEM] + [VMEM] * 2 + [ANY] + [VMEM] + [ANY] * 2 + [VMEM] * 3 + [ANY] + [VMEM] * 5


def cross(where, acts, early, bases, pieces, sums, rows, levels):
    part = bases[0].shape[1]
    width = acts[0].shape[1]
    cols = 2 * part
    chunk = cols // levels
    return pl.pallas_call(
        functools.partial(cross_kernel, levels, rows),
        out_shape=[shape((chunk, width), f32), shape((8, width), f32)]
        + [shape((chunk + 8, width), bf16)] * (levels - 1),
        in_specs=GIVEN,
        out_specs=[VMEM] * (1 + levels),
        scratch_shapes=[
            pltpu.VMEM((4 * rows, cols), bf16),
            pltpu.VMEM((rows, width), bf16),
            pltpu.VMEM((cols, width), f32),
            pltpu.SemaphoreType.DMA((14,)),
        ],
        compiler_params=params(LARGE),
        cost_estimate=cost(8 * rows * cols * width, 16 * rows * width),
    )(where, *acts, *early, *bases, *pieces, *sums)


def ready_kernel(levels, rows, where, *refs):
    acts, early, bases, other = refs[:4], refs[4:6], refs[6:8], refs[8]
    right, partial, sums, moved, sems = refs[9:]
    half, late = split(rows)
    part = bases[0].shape[1]
    chunk = right.shape[1] // levels
    pairs = [(acts[2].at[pl.ds(0, rows)], moved)]
    for i in range(2):
        columns = pl.ds(i * part, part)
        for j in range(4):
            pairs.append((early[i].at[pl.ds(j * half, half)], right.at[pl.ds(j * rows, half), columns]))
        for j in range(2):
            source = early[i].at[pl.ds(4 * half + j * late, late)]
            pairs.append((source, right.at[pl.ds(j * rows + half, late), columns]))
    copies = [pltpu.make_async_copy(a, b, sems.at[n]) for n, (a, b) in enumerate(pairs)]
    for copy in copies:
        copy.start()
    sums[...] = jnp.zeros_like(sums)
    right[pl.ds(3 * rows + half, late)] = jnp.zeros((late, 2 * part), bf16)
    for i, basis in enumerate(bases):
        columns = pl.ds(i * part, part)
        turned = jnp.dot(other[...], basis[...], preferred_element_type=f32).astype(bf16)
        right[pl.ds(2 * rows + half, late), columns] = turned
        sums[0:1, columns] = jnp.sum(jnp.square(turned.astype(f32)), axis=0, keepdims=True)
    for copy in copies:
        copy.wait()
    columns = pl.ds(pl.multiple_of((where[0] ^ 2) * chunk, chunk), chunk)
    partial[...] = chunk_of(right, columns, (acts[0], acts[1], moved, acts[3]), rows)


def ready(where, acts, early, bases, other, rows, levels):
    part = bases[0].shape[1]
    width = acts[0].shape[1]
    cols = 2 * part
    return pl.pallas_call(
        functools.partial(ready_kernel, levels, rows),
        out_shape=(
            shape((4 * rows, cols), bf16),
            shape((cols // levels, width), f32),
            shape((8, cols), f32),
        ),
        in_specs=[SMEM] + [VMEM] * 2 + [ANY] + [VMEM] + [ANY] * 2 + [VMEM] * 3,
        out_specs=(VMEM,) * 3,
        scratch_shapes=[pltpu.VMEM((rows, width), bf16), pltpu.SemaphoreType.DMA((13,))],
        compiler_params=params(LARGE),
        cost_estimate=cost(2 * rows * cols * width, 16 * rows * width),
    )(where, *acts, *early, *bases, other)


def last_chunk(block, columns, piece, rows):
    half, late = split(rows)
    return lax.dot_general(
        block[:, columns], piece[pl.ds(half, late)], (((0,), (0,)), ((), ())), preferred_element_type=f32
    )


def far_kernel(levels, rows, where, *refs):
    piece, last, bases, partial, other_sums, sums = refs[0], refs[1], refs[2:4], refs[4], refs[5], refs[6:10]
    message, extra, block = refs[10:]
    part = bases[0].shape[1]
    chunk = 2 * part // levels
    extra[...] = jnp.zeros_like(extra)
    for i in range(4):
        extra[1:2, pl.ds(i * part, part)] = sums[i][2:3]
        extra[2:3, pl.ds(i * part, part)] = sums[i][1:2]
    for i, basis in enumerate(bases):
        columns = pl.ds(i * part, part)
        turned = jnp.dot(last[...], basis[...], preferred_element_type=f32).astype(bf16)
        block[:, columns] = turned
        total = sums[i][0:1] + other_sums[0:1, columns]
        extra[0:1, columns] = total + jnp.sum(jnp.square(turned.astype(f32)), axis=0, keepdims=True)
    columns = pl.ds(pl.multiple_of((where[0] ^ 2) * chunk, chunk), chunk)
    message[...] = with_sums(partial[...] + last_chunk(block, columns, piece, rows), extra)


def far(where, piece, last, bases, partial, other_sums, sums, rows, levels):
    part = bases[0].shape[1]
    width = piece.shape[1]
    chunk = 2 * part // levels
    return pl.pallas_call(
        functools.partial(far_kernel, levels, rows),
        out_shape=(shape((chunk + 8, width), bf16), shape((8, width), f32), shape((last.shape[0], 2 * part), bf16)),
        in_specs=[SMEM] + [VMEM] * 10,
        out_specs=(VMEM,) * 3,
        compiler_params=params(LARGE),
        cost_estimate=cost(rows * part * width, 4 * rows * width),
    )(where, piece, last, *bases, partial, other_sums, *sums)


def near_kernel(levels, rows, where, right, block, extra, *refs):
    acts, own, message, kept = refs[:4], refs[4], refs[5], refs[6]
    chunk = right.shape[1] // levels
    for step, target in ((0, own), (1, message), (3, kept)):
        columns = pl.ds(pl.multiple_of((where[0] ^ step) * chunk, chunk), chunk)
        total = chunk_of(right, columns, acts, rows) + last_chunk(block, columns, acts[3], rows)
        target[...] = with_sums(total, extra) if step == 1 else total


def near(where, right, block, extra, acts, rows, levels):
    width = acts[0].shape[1]
    chunk = right.shape[1] // levels
    return pl.pallas_call(
        functools.partial(near_kernel, levels, rows),
        out_shape=(shape((chunk, width), f32), shape((chunk + 8, width), bf16), shape((chunk, width), f32)),
        in_specs=[SMEM] + [VMEM] * 7,
        out_specs=(VMEM,) * 3,
        compiler_params=params(LARGE),
        cost_estimate=cost(24 * rows * chunk * width, 16 * rows * width),
    )(where, right, block, extra, *acts)


def add_kernel(kept, extra, got, out):
    chunk = kept.shape[0]
    more = got[...].astype(f32)
    high, low = high_low(extra[0:4] + (more[chunk : chunk + 4] + more[chunk + 4 :]))
    out[...] = jnp.concatenate([(kept[...] + more[:chunk]).astype(bf16), high, low])


def add(kept, extra, got):
    return pl.pallas_call(
        add_kernel,
        out_shape=shape(got.shape, bf16),
        in_specs=[VMEM] * 3,
        out_specs=VMEM,
        compiler_params=params(SMALL),
        cost_estimate=cost(kept.size, 8 * kept.size),
    )(kept, extra, got)


def middle_kernel(levels, where, own, own_extra, *refs):
    count = len(refs) - levels - 6
    messages, bases, outs = refs[:count], refs[count : count + 4], refs[count + 4 : -2]
    basis, turned = refs[-2:]
    chunk, width = own.shape
    cols = chunk * levels
    part = bases[0].shape[1]
    for i, b in enumerate(bases):
        basis[:, pl.ds(i * part, part)] = b[...]
    total = own[...]
    extra = own_extra[...]
    for message in messages:
        part_sum = message[...].astype(f32)
        total = total + part_sum[:chunk]
        more = part_sum[chunk:]
        extra = extra + jnp.concatenate([more[0:4] + more[4:8], jnp.zeros_like(more[:4])])
    count = extra[2:3]
    extra = extra / count
    lam_a = extra[1:2]
    turned[...] = jnp.transpose(extra[:, :cols])
    lam_g = turned[pl.ds(pl.multiple_of(where[0] * chunk, chunk), chunk)][:, 0:1]
    both = jnp.dot(jnp.concatenate(high_low(total)), basis[...], preferred_element_type=f32)
    rotated = (both[:chunk] + both[chunk:]) / count
    scaled = (rotated / (lam_g * lam_a + damping)).astype(bf16)
    height = width // levels
    for step, out in enumerate(outs):
        rows = pl.ds(pl.multiple_of((where[0] ^ step) * height, height), height)
        out[...] = lax.dot_general(
            scaled, basis[rows], (((1,), (1,)), ((), ())), preferred_element_type=f32
        ).astype(bf16)


def middle(where, own, own_extra, messages, bases, levels):
    chunk, width = own.shape
    return pl.pallas_call(
        functools.partial(middle_kernel, levels),
        out_shape=[shape((chunk, width // levels), bf16)] * levels,
        in_specs=[SMEM] + [VMEM] * (len(messages) + 6),
        out_specs=[VMEM] * levels,
        scratch_shapes=[pltpu.VMEM((width, width), bf16), pltpu.VMEM((chunk * levels, 8), f32)],
        compiler_params=params(SMALL),
        cost_estimate=cost(6 * chunk * width * width, 2 * width * width),
    )(where, own, own_extra, *messages, *bases)


def result_kernel(levels, where, *refs):
    slots = refs[:levels]
    one, two, outs, (mid, whole) = refs[levels], refs[levels + 1], refs[levels + 2 : -2], refs[-2:]
    chunk, height = slots[0].shape
    wide, part = one.shape
    for step, slot in enumerate(slots):
        mid[pl.ds(pl.multiple_of((where[0] ^ step) * chunk, chunk), chunk)] = slot[...]
    quarter = wide // 4
    for j in range(4):
        columns = pl.ds(j * quarter, quarter)
        whole[:, columns] = sum(
            lax.dot_general(
                mid[pl.ds(i * part, part)], b[columns], (((0,), (1,)), ((), ())), preferred_element_type=f32
            )
            for i, b in enumerate((one, two))
        )
    rows = height // 4
    for other, out in zip((3, 1, 2, 0), outs):
        out[...] = whole[pl.ds(pl.multiple_of((where[1] ^ other) * rows, rows), rows)].astype(out.dtype)


def result(where, slots, bases):
    levels = len(slots)
    chunk, height = slots[0].shape
    wide, part = bases[0].shape
    return pl.pallas_call(
        functools.partial(result_kernel, levels),
        out_shape=[shape((height // 4, wide), t) for t in (bf16, bf16, f32, f32)],
        in_specs=[SMEM] + [VMEM] * (levels + 2),
        out_specs=[VMEM] * 4,
        scratch_shapes=[
            pltpu.VMEM((2 * part, height), bf16),
            pltpu.VMEM((height, wide), f32),
        ],
        compiler_params=params(SMALL),
        cost_estimate=cost(4 * height * part * wide, 4 * wide * part),
    )(where, *slots, *bases)


def gather_levels(unit, level, levels, ready):
    def over(slot):
        return lax.ppermute(slot, "group", SWAP)

    if levels != 4:
        slots = [unit] + [across(unit, step, levels) for step in range(1, levels)]
        return slots, [over(slot) for slot in slots], ready
    middle = (level == 1) | (level == 2)
    together = lax.optimization_barrier
    inner = lax.ppermute(unit, "level", [(1, 2), (2, 1)])
    first, inner, other0, ready = together((across(unit, 1, levels), inner, over(unit), ready))
    held, inner = together((unit, inner))
    outer, other1 = together((lax.ppermute(held, "level", [(0, 3), (3, 0)]), over(first)))
    third = jnp.where(middle, inner, outer)
    second, other3 = together((across(third, 1, levels), over(third)))
    return [unit, first, second, third], [other0, other1, over(second), other3], ready


def body(acts, grads, counts, basis_a, basis_g):
    group, level, chip, core = (lax.axis_index(n) for n in ("group", "level", "chip", "core"))
    levels = lax.axis_size("level")
    rows, width_a = acts.shape
    width_g = grads.shape[1]
    rows_a, rows_g = basis_a.shape[0], basis_g.shape[0]
    part_a, part_g = width_a // 4, width_g // 8
    where = jnp.stack([level, chip * 2 + core]).astype(jnp.int32)

    def columns(y, c):
        return jnp.concatenate(
            [
                cut(basis_g, ((y * 2 + c) * 2 + group) * part_g, part_g, 1),
                cut(basis_a, (c * 2 + group) * part_a, part_a, 1),
            ]
        )

    def diagonal(x):
        return lax.ppermute(x, ("chip", "core"), [(i, 3 - i) for i in range(4)])

    beyond = [lax.ppermute(columns(1 - chip, core), "chip", SWAP), diagonal(columns(1 - chip, 1 - core))]
    beside = lax.ppermute(columns(chip, 1 - core), "core", SWAP)
    blocks = jnp.stack([columns(chip, core), beside] + beyond)
    blocks = [lax.dynamic_index_in_dim(blocks, j ^ (chip * 2 + core), 0, False) for j in range(4)]
    unit = jnp.concatenate([b[:rows_g] for b in blocks] + [b[rows_g:] for b in blocks])
    level_g, level_a = 4 * rows_g, 4 * rows_a

    valid = counts[0]
    keep = jnp.arange(rows, dtype=jnp.int32)[:, None] < valid
    half = split(rows)[0]
    later, _ = lax.optimization_barrier((grads, unit))
    slots, others, late = gather_levels(unit, level, levels, jnp.where(keep[half:], later[half:], 0))
    marks = jnp.stack([valid // 16 * 16, valid % 16]).astype(bf16)
    marks = jnp.broadcast_to(jnp.pad(marks, (0, 14))[:, None], (16, width_a))
    early = jnp.where(keep[:half], grads[:half], 0)
    early = jnp.concatenate([jnp.where(keep, acts, 0), marks, early[:, :width_a], early[:, width_a:]])
    early_out, _ = lax.optimization_barrier((early, beyond[0]))

    together = lax.optimization_barrier
    far_rows, slots[2] = together((lax.ppermute(early_out, "chip", SWAP), slots[2]))
    early = [early, lax.ppermute(early, "core", SWAP), far_rows, lax.ppermute(far_rows, "core", SWAP)]
    later = [late, lax.ppermute(late, "core", SWAP)]
    first = turn(where, slots, early, later, rows, level_g, level_a)
    first_sums = lax.ppermute(first[3], "core", SWAP)
    others[2], first, first_sums = together((others[2], first, first_sums))
    second = turn(where, others, early, later, rows, level_g, level_a)
    far_rows, second = together((lax.ppermute(late, "chip", SWAP), second))
    bases_a, turned_g, bases_g, sums = zip(first, second)
    last = lax.ppermute(far_rows, "core", SWAP)
    sums += (first_sums, lax.ppermute(sums[1], "core", SWAP))
    bases_a += tuple(lax.ppermute(t, "core", SWAP) for t in bases_a)

    if levels == 4:
        right, partial, other_sums = ready(where, early, turned_g, bases_g, far_rows, rows, levels)
        message, own_extra, block = far(where, early[3], last, bases_g, partial, other_sums, sums, rows, levels)
        message = across(message, 1, levels)
        own, beside, kept = near(where, right, block, own_extra, early, rows, levels)
        got = [across(add(kept, own_extra, message), 3, levels), across(beside, 1, levels)]
    else:
        late = [last, *turn_other(far_rows, bases_g)]
        own, own_extra, *messages = cross(where, early, turned_g, bases_g, late, sums, rows, levels)
        got = [across(m, step + 1, levels) for step, m in enumerate(messages)]
    mids = middle(where, own, own_extra, got, bases_a, levels)
    mids = [m if step == 0 else across(m, step, levels) for step, m in enumerate(mids)]

    *sent, far_kept, near_kept = result(where, mids, bases_g)
    far_sent, near_sent = (lax.ppermute(x, "core", SWAP).astype(f32) for x in sent)
    last = lax.ppermute((far_kept + far_sent).astype(bf16), "chip", SWAP)
    return (near_kept + near_sent + last.astype(f32)).astype(bf16)


def solution(mesh):
    groups, samples = mesh.shape["groups"], mesh.shape["samples"]
    grid = Mesh(mesh.devices.reshape(groups, samples // 4, 2, 2), ("group", "level", "chip", "core"))
    every = ("group", "level", "chip", "core")
    in_specs = (
        P(every, None),
        P(every, None),
        P(every),
        P(every[1:], None),
        P(every[1:], None),
    )
    return jax.shard_map(body, mesh=grid, in_specs=in_specs, out_specs=P(every, None), check_vma=False)
```

```python
import functools

import jax
import jax.numpy as jnp
from jax import lax
from jax.experimental import pallas as pl
from jax.experimental.pallas import tpu as pltpu
from jax.sharding import Mesh, PartitionSpec as P

damping = 0.01
bf16 = jnp.bfloat16
f32 = jnp.float32
SWAP = [(0, 1), (1, 0)]
ANY = pl.BlockSpec(memory_space=pl.ANY)
VMEM = pl.BlockSpec(memory_space=pltpu.VMEM)
SMEM = pl.BlockSpec(memory_space=pltpu.SMEM)
LARGE = 18 * 2**20
MIDDLE = 16 * 2**20
SMALL = 12 * 2**20


def params(limit):
    return pltpu.CompilerParams(vmem_limit_bytes=limit)


def cost(flops, moved):
    return pl.CostEstimate(flops=flops, bytes_accessed=moved, transcendentals=0)


def shape(dims, dtype):
    return jax.ShapeDtypeStruct(dims, dtype)


def cut(x, first, size, axis=0):
    return lax.dynamic_slice_in_dim(x, first, size, axis)


def across(x, step, levels):
    return lax.ppermute(x, "level", [(i, i ^ step) for i in range(levels)])


def split(rows):
    return rows * 5 // 8, rows - rows * 5 // 8


def turn_kernel(levels, level_g, level_a, rows, where, *refs):
    slots, pieces, later = refs[:levels], list(refs[levels : levels + 4]), refs[levels + 4 : levels + 6]
    basis_a, out_g, basis_g, sums, held, held_sem, sems = refs[levels + 6 :]
    (half, late), width = split(rows), basis_a.shape[0]
    part = basis_a.shape[1]
    move = pltpu.make_async_copy(pieces[2], held, held_sem)
    pieces[2] = held
    copies = []
    for i, (first, height, target) in enumerate(((level_g, level_a, basis_a), (0, level_g, basis_g))):
        for step, slot in enumerate(slots):
            row = pl.multiple_of((where[0] ^ step) * height, height)
            copy = pltpu.make_async_copy(
                slot.at[pl.ds(first, height)], target.at[pl.ds(row, height)], sems.at[i * levels + step]
            )
            copy.start()
            copies.append(copy)
    move.start()

    def squares(x):
        return jnp.sum(jnp.square(x.astype(f32)), axis=0, keepdims=True)

    def turn_a(piece):
        return squares(jnp.dot(piece[:rows], basis_a[...], preferred_element_type=f32).astype(bf16))

    def turn_g(i):
        turned = sum(
            jnp.dot(
                pieces[i][pl.ds(rows + 16 + j * half, half)],
                basis_g[pl.ds(j * width, width)],
                preferred_element_type=f32,
            )
            for j in range(2)
        ).astype(bf16)
        out_g[pl.ds(i * half, half)] = turned
        return squares(turned)

    for copy in copies[:levels]:
        copy.wait()
    total_a = sum(turn_a(pieces[i]) for i in (0, 1, 3))
    for copy in copies[levels:]:
        copy.wait()
    total_g = sum(turn_g(i) for i in (0, 1, 3))
    for i, piece in enumerate(later):
        turned = jnp.dot(piece[...], basis_g[...], preferred_element_type=f32).astype(bf16)
        out_g[pl.ds(4 * half + i * late, late)] = turned
        total_g = total_g + squares(turned)
    move.wait()
    marks = sum(piece[rows : rows + 16, :part].astype(f32) for piece in pieces)
    sums[0:1] = total_g + turn_g(2)
    sums[1:2] = marks[0:1] + marks[1:2]
    sums[2:3] = total_a + turn_a(held)
    sums[3:8] = jnp.zeros((5, part), f32)


def turn(where, slots, pieces, later, rows, level_g, level_a):
    levels = len(slots)
    width_a, width_g = levels * level_a, levels * level_g
    part = slots[0].shape[1]
    half, late = split(rows)
    return pl.pallas_call(
        functools.partial(turn_kernel, levels, level_g, level_a, rows),
        out_shape=(
            shape((width_a, part), bf16),
            shape((4 * half + 2 * late, part), bf16),
            shape((width_g, part), bf16),
            shape((8, part), f32),
        ),
        in_specs=[SMEM] + [ANY] * levels + [VMEM] * 2 + [ANY] + [VMEM] * 3,
        out_specs=(VMEM,) * 4,
        scratch_shapes=[
            pltpu.VMEM(pieces[2].shape, bf16),
            pltpu.SemaphoreType.DMA,
            pltpu.SemaphoreType.DMA((2 * levels,)),
        ],
        compiler_params=params(MIDDLE),
        cost_estimate=cost(8 * rows * part * (width_a + width_g // 2), 8 * rows * (width_a + width_g // 2)),
    )(where, *slots, *pieces, *later)


def high_low(v):
    high = v.astype(bf16)
    return high, (v - high.astype(f32)).astype(bf16)


def turn_other_kernel(rows, one, two, out, sums):
    part = one.shape[1]
    sums[...] = jnp.zeros_like(sums)
    for i, basis in enumerate((one, two)):
        columns = pl.ds(i * part, part)
        turned = jnp.dot(rows[...], basis[...], preferred_element_type=f32).astype(bf16)
        out[:, columns] = turned
        sums[0:1, columns] = jnp.sum(jnp.square(turned.astype(f32)), axis=0, keepdims=True)


def turn_other(rows, bases):
    height, width = rows.shape
    part = bases[0].shape[1]
    return pl.pallas_call(
        turn_other_kernel,
        out_shape=(shape((height, 2 * part), bf16), shape((8, 2 * part), f32)),
        in_specs=[VMEM] * 3,
        out_specs=(VMEM, VMEM),
        compiler_params=params(SMALL),
        cost_estimate=cost(4 * height * part * width, 2 * height * width),
    )(rows, *bases)


def turn_late(rows, acts, early, bases, pieces, sums, right, moved, sems, extra):
    half, late = split(rows)
    part = bases[0].shape[1]
    count = 0

    def copy(source, target):
        nonlocal count
        made = pltpu.make_async_copy(source, target, sems.at[count])
        made.start()
        count += 1
        return made

    last, other, other_sums = pieces
    rest = [copy(acts[2].at[pl.ds(0, rows)], moved), copy(other, right.at[pl.ds(2 * rows + half, late)])]
    for i in range(2):
        columns = pl.ds(i * part, part)
        for j in range(4):
            rest.append(copy(early[i].at[pl.ds(j * half, half)], right.at[pl.ds(j * rows, half), columns]))
        for j in range(2):
            source = early[i].at[pl.ds(4 * half + j * late, late)]
            rest.append(copy(source, right.at[pl.ds(j * rows + half, late), columns]))
    extra[...] = jnp.zeros_like(extra)
    for i in range(4):
        extra[1:2, pl.ds(i * part, part)] = sums[i][2:3]
        extra[2:3, pl.ds(i * part, part)] = sums[i][1:2]
    for i, basis in enumerate(bases):
        columns = pl.ds(i * part, part)
        block = jnp.dot(last[...], basis[...], preferred_element_type=f32).astype(bf16)
        right[pl.ds(3 * rows + half, late), columns] = block
        total = sums[i][0:1] + other_sums[0:1, columns]
        extra[0:1, columns] = total + jnp.sum(jnp.square(block.astype(f32)), axis=0, keepdims=True)
    for made in rest:
        made.wait()
    return acts[0], acts[1], moved, acts[3]


def chunk_of(right, columns, acts, rows):
    return sum(
        lax.dot_general(
            right[pl.ds(i * rows, rows), columns], a[:rows], (((0,), (0,)), ((), ())), preferred_element_type=f32
        )
        for i, a in enumerate(acts)
    )


def with_sums(block, sums):
    high, low = high_low(sums[0:4])
    return jnp.concatenate([block.astype(bf16), high, low])


def cross_kernel(levels, rows, where, *refs):
    acts, early, bases, pieces, sums = refs[:4], refs[4:6], refs[6:8], refs[8:11], refs[11:15]
    own, extra, messages = refs[15], refs[16], refs[17 : 16 + levels]
    right, moved, whole, sems = refs[16 + levels :]
    chunk = right.shape[1] // levels
    acts = turn_late(rows, acts, early, bases, pieces, sums, right, moved, sems, extra)
    whole[...] = chunk_of(right, slice(None), acts, rows)
    own[...] = whole[pl.ds(pl.multiple_of(where[0] * chunk, chunk), chunk)]
    for step in range(1, levels):
        block = whole[pl.ds(pl.multiple_of((where[0] ^ step) * chunk, chunk), chunk)]
        messages[step - 1][...] = with_sums(block, extra)


GIVEN = [SMEM] + [VMEM] * 2 + [ANY] + [VMEM] + [ANY] * 2 + [VMEM] * 3 + [ANY] + [VMEM] * 5


def cross(where, acts, early, bases, pieces, sums, rows, levels):
    part = bases[0].shape[1]
    width = acts[0].shape[1]
    cols = 2 * part
    chunk = cols // levels
    return pl.pallas_call(
        functools.partial(cross_kernel, levels, rows),
        out_shape=[shape((chunk, width), f32), shape((8, width), f32)]
        + [shape((chunk + 8, width), bf16)] * (levels - 1),
        in_specs=GIVEN,
        out_specs=[VMEM] * (1 + levels),
        scratch_shapes=[
            pltpu.VMEM((4 * rows, cols), bf16),
            pltpu.VMEM((rows, width), bf16),
            pltpu.VMEM((cols, width), f32),
            pltpu.SemaphoreType.DMA((14,)),
        ],
        compiler_params=params(LARGE),
        cost_estimate=cost(8 * rows * cols * width, 16 * rows * width),
    )(where, *acts, *early, *bases, *pieces, *sums)


def ready_kernel(levels, rows, where, *refs):
    acts, early, bases, other = refs[:4], refs[4:6], refs[6:8], refs[8]
    right, partial, sums, moved, sems = refs[9:]
    half, late = split(rows)
    part = bases[0].shape[1]
    chunk = right.shape[1] // levels
    pairs = [(acts[2].at[pl.ds(0, rows)], moved)]
    for i in range(2):
        columns = pl.ds(i * part, part)
        for j in range(4):
            pairs.append((early[i].at[pl.ds(j * half, half)], right.at[pl.ds(j * rows, half), columns]))
        for j in range(2):
            source = early[i].at[pl.ds(4 * half + j * late, late)]
            pairs.append((source, right.at[pl.ds(j * rows + half, late), columns]))
    copies = [pltpu.make_async_copy(a, b, sems.at[n]) for n, (a, b) in enumerate(pairs)]
    for copy in copies:
        copy.start()
    sums[...] = jnp.zeros_like(sums)
    right[pl.ds(3 * rows + half, late)] = jnp.zeros((late, 2 * part), bf16)
    for i, basis in enumerate(bases):
        columns = pl.ds(i * part, part)
        turned = jnp.dot(other[...], basis[...], preferred_element_type=f32).astype(bf16)
        right[pl.ds(2 * rows + half, late), columns] = turned
        sums[0:1, columns] = jnp.sum(jnp.square(turned.astype(f32)), axis=0, keepdims=True)
    for copy in copies[1:]:
        copy.wait()
    columns = pl.ds(pl.multiple_of((where[0] ^ 2) * chunk, chunk), chunk)
    total = chunk_of(right, columns, acts[:2], rows)
    copies[0].wait()
    partial[...] = total + chunk_of(right.at[pl.ds(2 * rows, 2 * rows)], columns, (moved, acts[3]), rows)


def ready(where, acts, early, bases, other, rows, levels):
    part = bases[0].shape[1]
    width = acts[0].shape[1]
    cols = 2 * part
    return pl.pallas_call(
        functools.partial(ready_kernel, levels, rows),
        out_shape=(
            shape((4 * rows, cols), bf16),
            shape((cols // levels, width), f32),
            shape((8, cols), f32),
        ),
        in_specs=[SMEM] + [VMEM] * 2 + [ANY] + [VMEM] + [ANY] * 2 + [VMEM] * 3,
        out_specs=(VMEM,) * 3,
        scratch_shapes=[pltpu.VMEM((rows, width), bf16), pltpu.SemaphoreType.DMA((13,))],
        compiler_params=params(LARGE),
        cost_estimate=cost(2 * rows * cols * width, 16 * rows * width),
    )(where, *acts, *early, *bases, other)


def last_chunk(block, columns, piece, rows):
    half, late = split(rows)
    return lax.dot_general(
        block[:, columns], piece[pl.ds(half, late)], (((0,), (0,)), ((), ())), preferred_element_type=f32
    )


def far_kernel(levels, rows, where, *refs):
    piece, last, bases, partial, other_sums, sums = refs[0], refs[1], refs[2:4], refs[4], refs[5], refs[6:10]
    message, extra, block = refs[10:]
    part = bases[0].shape[1]
    chunk = 2 * part // levels
    extra[...] = jnp.zeros_like(extra)
    for i in range(4):
        extra[1:2, pl.ds(i * part, part)] = sums[i][2:3]
        extra[2:3, pl.ds(i * part, part)] = sums[i][1:2]
    for i, basis in enumerate(bases):
        columns = pl.ds(i * part, part)
        turned = jnp.dot(last[...], basis[...], preferred_element_type=f32).astype(bf16)
        block[:, columns] = turned
        total = sums[i][0:1] + other_sums[0:1, columns]
        extra[0:1, columns] = total + jnp.sum(jnp.square(turned.astype(f32)), axis=0, keepdims=True)
    columns = pl.ds(pl.multiple_of((where[0] ^ 2) * chunk, chunk), chunk)
    message[...] = with_sums(partial[...] + last_chunk(block, columns, piece, rows), extra)


def far(where, piece, last, bases, partial, other_sums, sums, rows, levels):
    part = bases[0].shape[1]
    width = piece.shape[1]
    chunk = 2 * part // levels
    return pl.pallas_call(
        functools.partial(far_kernel, levels, rows),
        out_shape=(shape((chunk + 8, width), bf16), shape((8, width), f32), shape((last.shape[0], 2 * part), bf16)),
        in_specs=[SMEM] + [VMEM] * 10,
        out_specs=(VMEM,) * 3,
        compiler_params=params(LARGE),
        cost_estimate=cost(rows * part * width, 4 * rows * width),
    )(where, piece, last, *bases, partial, other_sums, *sums)


def near_kernel(levels, rows, where, right, block, extra, *refs):
    acts, own, message, kept = refs[:4], refs[4], refs[5], refs[6]
    chunk = right.shape[1] // levels
    for step, target in ((0, own), (1, message), (3, kept)):
        columns = pl.ds(pl.multiple_of((where[0] ^ step) * chunk, chunk), chunk)
        total = chunk_of(right, columns, acts, rows) + last_chunk(block, columns, acts[3], rows)
        target[...] = with_sums(total, extra) if step == 1 else total


def near(where, right, block, extra, acts, rows, levels):
    width = acts[0].shape[1]
    chunk = right.shape[1] // levels
    return pl.pallas_call(
        functools.partial(near_kernel, levels, rows),
        out_shape=(shape((chunk, width), f32), shape((chunk + 8, width), bf16), shape((chunk, width), f32)),
        in_specs=[SMEM] + [VMEM] * 7,
        out_specs=(VMEM,) * 3,
        compiler_params=params(LARGE),
        cost_estimate=cost(24 * rows * chunk * width, 16 * rows * width),
    )(where, right, block, extra, *acts)


def add_kernel(kept, extra, got, out):
    chunk = kept.shape[0]
    more = got[...].astype(f32)
    high, low = high_low(extra[0:4] + (more[chunk : chunk + 4] + more[chunk + 4 :]))
    out[...] = jnp.concatenate([(kept[...] + more[:chunk]).astype(bf16), high, low])


def add(kept, extra, got):
    return pl.pallas_call(
        add_kernel,
        out_shape=shape(got.shape, bf16),
        in_specs=[VMEM] * 3,
        out_specs=VMEM,
        compiler_params=params(SMALL),
        cost_estimate=cost(kept.size, 8 * kept.size),
    )(kept, extra, got)


def middle_kernel(levels, where, own, own_extra, *refs):
    count = len(refs) - levels - 6
    messages, bases, outs = refs[:count], refs[count : count + 4], refs[count + 4 : -2]
    basis, turned = refs[-2:]
    chunk, width = own.shape
    cols = chunk * levels
    part = bases[0].shape[1]
    for i, b in enumerate(bases):
        basis[:, pl.ds(i * part, part)] = b[...]
    total = own[...]
    extra = own_extra[...]
    for message in messages:
        part_sum = message[...].astype(f32)
        total = total + part_sum[:chunk]
        more = part_sum[chunk:]
        extra = extra + jnp.concatenate([more[0:4] + more[4:8], jnp.zeros_like(more[:4])])
    count = extra[2:3]
    extra = extra / count
    lam_a = extra[1:2]
    turned[...] = jnp.transpose(extra[:, :cols])
    lam_g = turned[pl.ds(pl.multiple_of(where[0] * chunk, chunk), chunk)][:, 0:1]
    both = jnp.dot(jnp.concatenate(high_low(total)), basis[...], preferred_element_type=f32)
    rotated = (both[:chunk] + both[chunk:]) / count
    scaled = (rotated / (lam_g * lam_a + damping)).astype(bf16)
    height = width // levels
    for step, out in enumerate(outs):
        rows = pl.ds(pl.multiple_of((where[0] ^ step) * height, height), height)
        out[...] = lax.dot_general(
            scaled, basis[rows], (((1,), (1,)), ((), ())), preferred_element_type=f32
        ).astype(bf16)


def middle(where, own, own_extra, messages, bases, levels):
    chunk, width = own.shape
    return pl.pallas_call(
        functools.partial(middle_kernel, levels),
        out_shape=[shape((chunk, width // levels), bf16)] * levels,
        in_specs=[SMEM] + [VMEM] * (len(messages) + 6),
        out_specs=[VMEM] * levels,
        scratch_shapes=[pltpu.VMEM((width, width), bf16), pltpu.VMEM((chunk * levels, 8), f32)],
        compiler_params=params(SMALL),
        cost_estimate=cost(6 * chunk * width * width, 2 * width * width),
    )(where, own, own_extra, *messages, *bases)


def result_kernel(levels, where, *refs):
    slots = refs[:levels]
    one, two, outs, (mid, whole) = refs[levels], refs[levels + 1], refs[levels + 2 : -2], refs[-2:]
    chunk, height = slots[0].shape
    wide, part = one.shape
    for step, slot in enumerate(slots):
        mid[pl.ds(pl.multiple_of((where[0] ^ step) * chunk, chunk), chunk)] = slot[...]
    quarter = wide // 4
    for j in range(4):
        columns = pl.ds(j * quarter, quarter)
        whole[:, columns] = sum(
            lax.dot_general(
                mid[pl.ds(i * part, part)], b[columns], (((0,), (1,)), ((), ())), preferred_element_type=f32
            )
            for i, b in enumerate((one, two))
        )
    rows = height // 4
    for other, out in zip((3, 1, 2, 0), outs):
        out[...] = whole[pl.ds(pl.multiple_of((where[1] ^ other) * rows, rows), rows)].astype(out.dtype)


def result(where, slots, bases):
    levels = len(slots)
    chunk, height = slots[0].shape
    wide, part = bases[0].shape
    return pl.pallas_call(
        functools.partial(result_kernel, levels),
        out_shape=[shape((height // 4, wide), t) for t in (bf16, bf16, f32, f32)],
        in_specs=[SMEM] + [VMEM] * (levels + 2),
        out_specs=[VMEM] * 4,
        scratch_shapes=[
            pltpu.VMEM((2 * part, height), bf16),
            pltpu.VMEM((height, wide), f32),
        ],
        compiler_params=params(SMALL),
        cost_estimate=cost(4 * height * part * wide, 4 * wide * part),
    )(where, *slots, *bases)


def gather_levels(unit, level, levels, ready):
    def over(slot):
        return lax.ppermute(slot, "group", SWAP)

    if levels != 4:
        slots = [unit] + [across(unit, step, levels) for step in range(1, levels)]
        return slots, [over(slot) for slot in slots], ready
    middle = (level == 1) | (level == 2)
    together = lax.optimization_barrier
    inner = lax.ppermute(unit, "level", [(1, 2), (2, 1)])
    first, inner, other0, ready = together((across(unit, 1, levels), inner, over(unit), ready))
    held, inner = together((unit, inner))
    outer, other1 = together((lax.ppermute(held, "level", [(0, 3), (3, 0)]), over(first)))
    third = jnp.where(middle, inner, outer)
    second, other3 = together((across(third, 1, levels), over(third)))
    return [unit, first, second, third], [other0, other1, over(second), other3], ready


def body(acts, grads, counts, basis_a, basis_g):
    group, level, chip, core = (lax.axis_index(n) for n in ("group", "level", "chip", "core"))
    levels = lax.axis_size("level")
    rows, width_a = acts.shape
    width_g = grads.shape[1]
    rows_a, rows_g = basis_a.shape[0], basis_g.shape[0]
    part_a, part_g = width_a // 4, width_g // 8
    where = jnp.stack([level, chip * 2 + core]).astype(jnp.int32)

    def columns(y, c):
        return jnp.concatenate(
            [
                cut(basis_g, ((y * 2 + c) * 2 + group) * part_g, part_g, 1),
                cut(basis_a, (c * 2 + group) * part_a, part_a, 1),
            ]
        )

    def diagonal(x):
        return lax.ppermute(x, ("chip", "core"), [(i, 3 - i) for i in range(4)])

    beyond = [lax.ppermute(columns(1 - chip, core), "chip", SWAP), diagonal(columns(1 - chip, 1 - core))]
    beside = lax.ppermute(columns(chip, 1 - core), "core", SWAP)
    blocks = jnp.stack([columns(chip, core), beside] + beyond)
    blocks = [lax.dynamic_index_in_dim(blocks, j ^ (chip * 2 + core), 0, False) for j in range(4)]
    unit = jnp.concatenate([b[:rows_g] for b in blocks] + [b[rows_g:] for b in blocks])
    level_g, level_a = 4 * rows_g, 4 * rows_a

    valid = counts[0]
    keep = jnp.arange(rows, dtype=jnp.int32)[:, None] < valid
    half = split(rows)[0]
    later, _ = lax.optimization_barrier((grads, unit))
    slots, others, late = gather_levels(unit, level, levels, jnp.where(keep[half:], later[half:], 0))
    marks = jnp.stack([valid // 16 * 16, valid % 16]).astype(bf16)
    marks = jnp.broadcast_to(jnp.pad(marks, (0, 14))[:, None], (16, width_a))
    early = jnp.where(keep[:half], grads[:half], 0)
    early = jnp.concatenate([jnp.where(keep, acts, 0), marks, early[:, :width_a], early[:, width_a:]])
    early_out, _ = lax.optimization_barrier((early, beyond[0]))

    together = lax.optimization_barrier
    far_rows, slots[2] = together((lax.ppermute(early_out, "chip", SWAP), slots[2]))
    early = [early, lax.ppermute(early, "core", SWAP), far_rows, lax.ppermute(far_rows, "core", SWAP)]
    later = [late, lax.ppermute(late, "core", SWAP)]
    first = turn(where, slots, early, later, rows, level_g, level_a)
    first_sums = lax.ppermute(first[3], "core", SWAP)
    others[2], first, first_sums = together((others[2], first, first_sums))
    second = turn(where, others, early, later, rows, level_g, level_a)
    far_rows, second = together((lax.ppermute(late, "chip", SWAP), second))
    bases_a, turned_g, bases_g, sums = zip(first, second)
    last = lax.ppermute(far_rows, "core", SWAP)
    sums += (first_sums, lax.ppermute(sums[1], "core", SWAP))
    bases_a += tuple(lax.ppermute(t, "core", SWAP) for t in bases_a)

    if levels == 4:
        right, partial, other_sums = ready(where, early, turned_g, bases_g, far_rows, rows, levels)
        message, own_extra, block = far(where, early[3], last, bases_g, partial, other_sums, sums, rows, levels)
        message = across(message, 1, levels)
        own, beside, kept = near(where, right, block, own_extra, early, rows, levels)
        got = [across(add(kept, own_extra, message), 3, levels), across(beside, 1, levels)]
    else:
        late = [last, *turn_other(far_rows, bases_g)]
        own, own_extra, *messages = cross(where, early, turned_g, bases_g, late, sums, rows, levels)
        got = [across(m, step + 1, levels) for step, m in enumerate(messages)]
    mids = middle(where, own, own_extra, got, bases_a, levels)
    mids = [m if step == 0 else across(m, step, levels) for step, m in enumerate(mids)]

    *sent, far_kept, near_kept = result(where, mids, bases_g)
    far_sent, near_sent = (lax.ppermute(x, "core", SWAP).astype(f32) for x in sent)
    last = lax.ppermute((far_kept + far_sent).astype(bf16), "chip", SWAP)
    return (near_kept + near_sent + last.astype(f32)).astype(bf16)


def solution(mesh):
    groups, samples = mesh.shape["groups"], mesh.shape["samples"]
    grid = Mesh(mesh.devices.reshape(groups, samples // 4, 2, 2), ("group", "level", "chip", "core"))
    every = ("group", "level", "chip", "core")
    in_specs = (
        P(every, None),
        P(every, None),
        P(every),
        P(every[1:], None),
        P(every[1:], None),
    )
    return jax.shard_map(body, mesh=grid, in_specs=in_specs, out_specs=P(every, None), check_vma=False)
```
